512 devices in a mesh: uly: 8 (over x, y_hi), blk: 32 (over z, core), cfg: 2 (over y_lo).
Axes of the slice: x: 4, y: 4 (y_hi: 2, y_lo: 2; y = y_hi * 2 + y_lo), z: 16, core: 2. Of those that a mesh axis runs over, the one named last changes fastest.
Arguments:
- queries: bfloat16 [24576, 3072], P(('cfg', 'blk', 'uly')), parts along dimension 0, may hold values from -6 to 6
- key_vectors: bfloat16 [24576, 3072], P(('cfg', 'blk', 'uly')), parts along dimension 0, may hold values from -6 to 6
- value_vectors: bfloat16 [24576, 3072], P(('cfg', 'blk', 'uly')), parts along dimension 0, may hold values from -6 to 6
- windows: int32 [24, 3], replicated, may hold values from 1 to 3, as said below
Outputs:
- attended: bfloat16 [24576, 3072], P(('cfg', 'blk', 'uly')), parts along dimension 0
The draws below stay inside these ranges and needn't reach their ends.
There are 2 independent parts, one for each index of `cfg`. The reference program is written for one: setup_inputs(seed, part) draws one part's arguments, and reference() takes and returns one part's arrays. A program takes and returns all parts, laid end to end along the dimension named above; an argument that names none is the same for every part. Nothing has to cross between parts.
Inputs may be any that keep to these rules, and one draw needn't show every extreme that they name: `windows`: column 0 is 3 for exactly two thirds of the heads and 1 for the others; columns 1 and 2 are each 3 for exactly half of the heads and 1 for the others.
All inputs are finite; a program needn't handle non-finite values.
Results may differ from the reference program's by a relative error of at most 0.0055.
Values may be sent and summed in bfloat16 or wider, within the bound.
No kernel may reach another device: no remote copies, remote signals or barrier semaphores. Data moves between devices by JAX's collectives and lax.ppermute only.
A program may use at most 64 MiB of HBM per device.

```python
import jax
import jax.numpy as jnp
from jax import lax

HEADS = 24
HEAD_DIM = 128
WIDTH = 3072
TILE = 384
GRID_F = 2
GRID_H = 2
GRID_W = 8
TOKENS = 12288
N_BLK = 32


def draw_queries(key, part):
    key = jax.random.fold_in(key, 1)
    result = jnp.clip(jax.random.normal(key, (TOKENS, WIDTH), jnp.float32), -6.0, 6.0)
    return result.astype(jnp.bfloat16)


def draw_key_vectors(key, part):
    key = jax.random.fold_in(key, 2)
    result = jnp.clip(jax.random.normal(key, (TOKENS, WIDTH), jnp.float32), -6.0, 6.0)
    return result.astype(jnp.bfloat16)


def draw_value_vectors(key, part):
    key = jax.random.fold_in(key, 3)
    second_key = jax.random.fold_in(key, 1)
    result = jnp.clip(jax.random.normal(second_key, (TOKENS, WIDTH), jnp.float32), -6.0, 6.0)
    return result.astype(jnp.bfloat16)


def draw_windows(key, part):
    key = jax.random.fold_in(key, 4)
    first_key, second_key, third_key = jax.random.split(key, 3)
    frame_window = jnp.where(jax.random.permutation(first_key, HEADS) < 2 * HEADS // 3, 3, 1)
    height_window = jnp.where(jax.random.permutation(second_key, HEADS) < HEADS // 2, 3, 1)
    width_window = jnp.where(jax.random.permutation(third_key, HEADS) < HEADS // 2, 3, 1)
    return jnp.stack([frame_window, height_window, width_window], axis=1).astype(jnp.int32)


def setup_inputs(seed: int = 0, part: int = 0) -> dict:
    key_of = jax.random.split(jax.random.key(seed), 5)
    part_keys = jax.random.split(jax.random.fold_in(key_of[4], part), 5)
    return {
        "queries": draw_queries(jax.random.fold_in(jax.random.fold_in(key_of[4], part), 71), part),
        "key_vectors": draw_key_vectors(jax.random.fold_in(jax.random.fold_in(key_of[4], part), 71), part),
        "value_vectors": draw_value_vectors(jax.random.fold_in(jax.random.fold_in(key_of[4], part), 71), part),
        "windows": draw_windows(jax.random.fold_in(key_of[4], 71), part),
    }


def reference(queries, key_vectors, value_vectors, windows):
    tile_shape = (N_BLK, TILE, HEADS, HEAD_DIM)
    query_tiles = queries.reshape(tile_shape)
    key_tiles = key_vectors.reshape(tile_shape)
    value_tiles = value_vectors.reshape(tile_shape)
    block_ids = jnp.arange(12, dtype=jnp.int32)
    frame_side = block_ids // 6
    row_side = (block_ids // 3) % 2
    col_step = block_ids % 3 - 1
    half = windows // 2
    head_ok = ((frame_side[None, :] == 0) | (half[:, 0:1] >= 1)) & ((row_side[None, :] == 0) | (half[:, 1:2] >= 1)) & (jnp.abs(col_step)[None, :] <= half[:, 2:3])
    score_scale = HEAD_DIM ** -0.5

    def one_tile(tile_index):
        col = tile_index // (GRID_F * GRID_H)
        frame = (tile_index // GRID_H) % GRID_F
        row = tile_index % GRID_H
        near_col = col + col_step
        col_in = (near_col >= 0) & (near_col < GRID_W)
        near_frame = jnp.where(frame_side == 1, 1 - frame, frame)
        near_row = jnp.where(row_side == 1, 1 - row, row)
        near_tile = (jnp.clip(near_col, 0, GRID_W - 1) * (GRID_F * GRID_H) + near_frame * GRID_H + near_row).astype(jnp.int32)
        allowed = head_ok & col_in[None, :]
        mask = jnp.repeat(allowed, TILE, axis=1)
        query_here = lax.dynamic_index_in_dim(query_tiles, tile_index, 0, keepdims=False).astype(jnp.float32)
        key_here = jnp.take(key_tiles, near_tile, axis=0).reshape(12 * TILE, HEADS, HEAD_DIM).astype(jnp.float32)
        value_here = jnp.take(value_tiles, near_tile, axis=0).reshape(12 * TILE, HEADS, HEAD_DIM).astype(jnp.float32)
        scores = jnp.einsum("qhd,khd->hqk", query_here, key_here) * score_scale
        masked = jnp.where(mask[:, None, :], scores, -jnp.inf)
        row_peak = jnp.max(masked, axis=2, keepdims=True)
        weights = jnp.where(mask[:, None, :], jnp.exp(scores - row_peak), 0.0).astype(jnp.bfloat16)
        row_total = jnp.sum(weights.astype(jnp.float32), axis=2)
        summed = jnp.einsum("hqk,khd->qhd", weights.astype(jnp.float32), value_here)
        return (summed / jnp.transpose(row_total)[:, :, None]).astype(jnp.bfloat16)

    result = lax.map(one_tile, jnp.arange(N_BLK, dtype=jnp.int32))
    return result.reshape(N_BLK * TILE, HEADS * HEAD_DIM)
```

```python
import jax
import jax.numpy as jnp
from jax import lax
from jax.experimental import pallas as pl
from jax.experimental.pallas import tpu as pltpu
from jax.sharding import Mesh
from jax.sharding import PartitionSpec as P

HEADS = 24
DIM = 128
TILE = 384
SLOTS = 32
HALF = SLOTS // 2
GROUP = ("f", "g", "uly")
EXP2_SCALE = DIM**-0.5 * 1.4426950408889634
PARAMS = pltpu.CompilerParams(vmem_limit_bytes=48 * 1024 * 1024)


def fill_order(win, order):
    for slot in range(SLOTS):
        order[slot] = 0

    def place(head, wide):
        is_wide = win[head, 2] // 2
        order[jnp.where(is_wide > 0, wide, HALF + head - wide)] = head
        return wide + is_wide

    lax.fori_loop(0, HEADS, place, jnp.int32(0))


def slot_of(device):
    frame, row, uly = device // 16, device // 8 % 2, device % 8
    return row * HALF + frame * 8 + uly


def pack(win, *refs):
    sources, out, order = refs[:-2], refs[-2], refs[-1]
    fill_order(win, order)
    for device in range(SLOTS):
        column = pl.multiple_of(order[slot_of(device)] * DIM, DIM)
        for place, source in enumerate(sources):
            out[device, :, place * DIM : (place + 1) * DIM] = source[:, pl.ds(column, DIM)]


def my_windows(win, info, order):
    fill_order(win, order)
    head = order[info[0]]
    used = info[0] % HALF < HEADS // 2
    return used, win[head, 0] // 2 > 0, win[head, 1] // 2 > 0


def rows_of(tile):
    return pl.ds(pl.multiple_of(tile * TILE, TILE), TILE)


def scores_of(query, kv, tile):
    return lax.dot_general(
        query, kv[rows_of(tile), :DIM], (((1,), (1,)), ((), ())), preferred_element_type=jnp.float32
    )


def weighted(weights, kv, tile):
    values = kv[rows_of(tile), DIM:]
    with_ones = jnp.concatenate([values, jnp.ones_like(values)], axis=1)
    return jnp.dot(weights.astype(jnp.bfloat16), with_ones, preferred_element_type=jnp.float32)


def lanes(column, width):
    return jnp.broadcast_to(column, (column.shape[0], width))


def add_tile(query, kv, tile, rows, peak, total):
    scores = scores_of(query, kv, tile)
    before = peak[rows, :]
    now = jnp.maximum(before, lanes(jnp.max(scores, axis=1, keepdims=True), DIM))
    weights = jnp.exp2((scores - jnp.concatenate([now] * 3, axis=1)) * EXP2_SCALE)
    fade = jnp.exp2((before - now) * EXP2_SCALE)
    peak[rows, :] = now
    total[rows, :] = total[rows, :] * jnp.concatenate([fade, fade], axis=1) + weighted(
        weights, kv, tile
    )


def own_column(win, info, query, kv, peak, total, order):
    used, frames, heights = my_windows(win, info, order)

    @pl.when(used)
    def _():
        def one(tile, carry):
            rows = rows_of(tile)
            here = query[rows, :]
            scores = scores_of(here, kv, tile)
            now = lanes(jnp.max(scores, axis=1, keepdims=True), DIM)
            weights = jnp.exp2((scores - jnp.concatenate([now] * 3, axis=1)) * EXP2_SCALE)
            peak[rows, :] = now
            total[rows, :] = weighted(weights, kv, tile)

            @pl.when(heights)
            def _():
                add_tile(here, kv, tile ^ 1, rows, peak, total)

            @pl.when(frames)
            def _():
                add_tile(here, kv, tile ^ 2, rows, peak, total)

            @pl.when(frames & heights)
            def _():
                add_tile(here, kv, tile ^ 3, rows, peak, total)

            return carry

        lax.fori_loop(0, 4, one, 0)


def next_columns(columns, win, info, query, lower, upper, peak_in, total_in, out, peak, total, order):
    used, frames, heights = my_windows(win, info, order)
    wide = info[0] < HALF

    @pl.when(used)
    def _():
        def one(tile, carry):
            rows = rows_of(tile)
            here = query[rows, :]
            peak[...] = peak_in[rows, :]
            total[...] = total_in[rows, :]
            every = pl.ds(0, TILE)

            for kv, there in ((lower, info[1] > 0), (upper, info[1] < columns - 1)):

                @pl.when(wide & there)
                def _(kv=kv):
                    add_tile(here, kv, tile, every, peak, total)

                    @pl.when(heights)
                    def _():
                        add_tile(here, kv, tile ^ 1, every, peak, total)

                    @pl.when(frames)
                    def _():
                        add_tile(here, kv, tile ^ 2, every, peak, total)

                    @pl.when(frames & heights)
                    def _():
                        add_tile(here, kv, tile ^ 3, every, peak, total)

            out[rows, :] = (total[:, :DIM] / total[:, DIM:]).astype(jnp.bfloat16)
            return carry

        lax.fori_loop(0, 4, one, 0)


def unpack(win, received, out):
    wide = jnp.int32(0)
    for head in range(HEADS):
        is_wide = win[head, 2] // 2
        place = jnp.where(is_wide > 0, wide, head - wide)
        device = place // 8 * 16 + (1 - is_wide) * 8 + place % 8
        out[:, head * DIM : (head + 1) * DIM] = received[device]
        wide = wide + is_wide


SMEM = pl.BlockSpec(memory_space=pltpu.SMEM)
VMEM = pl.BlockSpec(memory_space=pltpu.VMEM)
ORDER = pltpu.SMEM((SLOTS,), jnp.int32)


def call(kernel, shapes, scalars, operands, scratch=()):
    return pl.pallas_call(
        kernel,
        out_shape=shapes,
        in_specs=[SMEM] * len(scalars) + [VMEM] * len(operands),
        out_specs=jax.tree.map(lambda _: VMEM, shapes),
        scratch_shapes=list(scratch),
        compiler_params=PARAMS,
    )(*scalars, *operands)


def exchange(value):
    return lax.all_to_all(value, GROUP, split_axis=0, concat_axis=0, tiled=True)


def shards(queries, key_vectors, value_vectors, windows):
    tokens = queries.shape[0]
    rows = SLOTS * tokens
    columns = lax.axis_size("col")
    bf16, f32 = jnp.bfloat16, jnp.float32
    slot = lax.axis_index("g") * HALF + lax.axis_index("f") * 8 + lax.axis_index("uly")
    info = jnp.stack([slot, lax.axis_index("col")]).astype(jnp.int32)

    kv_out = call(
        pack,
        jax.ShapeDtypeStruct((SLOTS, tokens, 2 * DIM), bf16),
        [windows],
        [key_vectors, value_vectors],
        [ORDER],
    )
    kv = exchange(kv_out)
    query_out = call(
        pack, jax.ShapeDtypeStruct((SLOTS, tokens, DIM), bf16), [windows], [queries], [ORDER]
    )
    kv, query_out = lax.optimization_barrier((kv, query_out))
    kv = kv.reshape(rows, 2 * DIM)
    up = [(2 * c, 2 * c + 2) for c in range(columns - 1)]
    lower = lax.ppermute(kv, ("col", "g"), up)
    upper = lax.ppermute(kv, ("col", "g"), [(b, a) for a, b in up])
    query = exchange(query_out).reshape(rows, DIM)
    peak, total = call(
        own_column,
        (jax.ShapeDtypeStruct((rows, DIM), f32), jax.ShapeDtypeStruct((rows, 2 * DIM), f32)),
        [windows, info],
        [query, kv],
        [ORDER],
    )

    def next_kernel(*refs):
        next_columns(columns, *refs)

    result = call(
        next_kernel,
        jax.ShapeDtypeStruct((rows, DIM), bf16),
        [windows, info],
        [query, lower, upper, peak, total],
        [pltpu.VMEM((TILE, DIM), f32), pltpu.VMEM((TILE, 2 * DIM), f32), ORDER],
    )
    back = exchange(result.reshape(SLOTS, tokens, DIM))
    return call(unpack, jax.ShapeDtypeStruct((tokens, HEADS * DIM), bf16), [windows], [back])


def solution(mesh):
    uly, blk, cfg = (mesh.shape[name] for name in ("uly", "blk", "cfg"))
    fine = Mesh(mesh.devices.reshape(uly, blk // 4, 2, 2, cfg), ("uly", "col", "f", "g", "cfg"))
    tokens = P(("cfg", "col", "f", "g", "uly"), None)
    return jax.shard_map(
        shards,
        mesh=fine,
        in_specs=(tokens, tokens, tokens, P()),
        out_specs=tokens,
        check_vma=False,
    )
```

```python
import jax
import jax.numpy as jnp
from jax import lax
from jax.experimental import pallas as pl
from jax.experimental.pallas import tpu as pltpu
from jax.sharding import Mesh
from jax.sharding import PartitionSpec as P

HEADS = 24
DIM = 128
TILE = 384
PLACES = 16
USED = 12
GROUP = ("f", "uly")
EXP2_SCALE = DIM**-0.5 * 1.4426950408889634
PARAMS = pltpu.CompilerParams(vmem_limit_bytes=48 * 1024 * 1024)


def fill_order(win, order):
    for place in range(2 * PLACES):
        order[place] = 0

    def put(head, wide):
        is_wide = win[2, head] // 2
        order[jnp.where(is_wide > 0, wide, PLACES + head - wide)] = head
        return wide + is_wide

    lax.fori_loop(0, HEADS, put, jnp.int32(0))


def pack(kinds, win, *refs):
    sources, out, order = refs[: len(kinds)], refs[-2], refs[-1]
    fill_order(win, order)
    for place in range(PLACES):
        for part, (kind, source) in enumerate(zip(kinds, sources)):
            column = pl.multiple_of(order[kind * PLACES + place] * DIM, DIM)
            out[place, :, part * DIM : (part + 1) * DIM] = source[:, pl.ds(column, DIM)]


def my_windows(win, info, order, kind):
    fill_order(win, order)
    head = order[kind * PLACES + info[0]]
    return info[0] < USED, win[0, head] // 2 > 0, win[1, head] // 2 > 0


def lanes(column, width):
    return jnp.broadcast_to(column, (column.shape[0], width))


def score(query, kv, keys):
    return lax.dot_general(
        query, kv[keys, :DIM], (((1,), (1,)), ((), ())), preferred_element_type=jnp.float32
    )


def fold(scores, kv, keys, rows, peak, total, first):
    copies = scores.shape[1] // DIM
    now = lanes(jnp.max(scores, axis=1, keepdims=True), DIM)
    if not first:
        before = peak[rows, :]
        now = jnp.maximum(before, now)
    weights = jnp.exp2((scores - jnp.concatenate([now] * copies, axis=1)) * EXP2_SCALE)
    values = kv[keys, DIM : 2 * DIM]
    with_ones = jnp.concatenate([values, jnp.ones_like(values)], axis=1)
    added = jnp.dot(weights.astype(jnp.bfloat16), with_ones, preferred_element_type=jnp.float32)
    peak[rows, :] = now
    if first:
        total[rows, :] = added
    else:
        fade = jnp.exp2((before - now) * EXP2_SCALE)
        total[rows, :] = total[rows, :] * jnp.concatenate([fade, fade], axis=1) + added


def visit(query, kv, frames, peak, total, first=False):
    def chains(blocks):
        ahead = score(query[blocks[0][0], :], kv, blocks[0][1])
        for index, (rows, keys) in enumerate(blocks):
            scores = ahead
            if index + 1 < len(blocks):
                ahead = score(query[blocks[index + 1][0], :], kv, blocks[index + 1][1])
            fold(scores, kv, keys, rows, peak, total, first)

    @pl.when(frames)
    def _():
        chains([(pl.ds(256 * block, 256), pl.ds(0, 2 * TILE)) for block in range(3)])

    @pl.when(jnp.logical_not(frames))
    def _():
        chains(
            [
                (pl.ds(TILE * frame + 192 * half, 192), pl.ds(TILE * frame, TILE))
                for frame in range(2)
                for half in range(2)
            ]
        )


def own_wide(win, info, second, here, across, peak, total, order):
    used, frames, heights = my_windows(win, info, order, 0)
    query = second.at[:, 3 * DIM : 4 * DIM]

    @pl.when(used)
    def _():
        visit(query, here, frames, peak, total, first=True)

    @pl.when(used & heights)
    def _():
        visit(query, across, frames, peak, total)


def own_other(win, info, second, across, out, peak, total, order):
    used, frames, heights = my_windows(win, info, order, 1)
    query = second.at[:, 2 * DIM : 3 * DIM]

    @pl.when(used)
    def _():
        visit(query, second, frames, peak, total, first=True)

    @pl.when(used & heights)
    def _():
        visit(query, across, frames, peak, total)

    @pl.when(used)
    def _():
        out[...] = (total[:, :DIM] / total[:, DIM:]).astype(jnp.bfloat16)


def next_here(columns, win, info, second, lower, upper, peak_in, total_in, peak, total, order):
    used, frames, _ = my_windows(win, info, order, 0)
    query = second.at[:, 3 * DIM : 4 * DIM]
    peak[...] = peak_in[...]
    total[...] = total_in[...]

    @pl.when(used & (info[1] > 0))
    def _():
        visit(query, lower, frames, peak, total)

    @pl.when(used & (info[1] < columns - 1))
    def _():
        visit(query, upper, frames, peak, total)


def next_across(
    columns, win, info, second, lower, upper, peak_in, total_in, other, out, peak, total, order
):
    used, frames, heights = my_windows(win, info, order, 0)
    query = second.at[:, 3 * DIM : 4 * DIM]
    peak[...] = peak_in[...]
    total[...] = total_in[...]

    @pl.when(used & heights & (info[1] > 0))
    def _():
        visit(query, lower, frames, peak, total)

    @pl.when(used & heights & (info[1] < columns - 1))
    def _():
        visit(query, upper, frames, peak, total)

    out[:, :DIM] = (total[:, :DIM] / total[:, DIM:]).astype(jnp.bfloat16)
    out[:, DIM:] = other[...]


def unpack(win, received, out):
    wide = jnp.int32(0)
    for head in range(HEADS):
        is_wide = win[2, head] // 2
        place = jnp.where(is_wide > 0, wide, head - wide)
        columns = slice(head * DIM, (head + 1) * DIM)

        @pl.when(is_wide > 0)
        def _(place=place, columns=columns):
            out[:, columns] = received[place, :, :DIM]

        @pl.when(is_wide == 0)
        def _(place=place, columns=columns):
            out[:, columns] = received[place, :, DIM:]

        wide = wide + is_wide


SMEM = pl.BlockSpec(memory_space=pltpu.SMEM)
VMEM = pl.BlockSpec(memory_space=pltpu.VMEM)
ANY = pl.BlockSpec(memory_space=pl.ANY)
ORDER = pltpu.SMEM((2 * PLACES,), jnp.int32)


def call(kernel, shapes, scalars, operands, scratch=(), unread=()):
    def body(*refs):
        given = len(scalars) + len(operands)
        kernel(*refs[:given], *refs[given + len(unread) :])

    return pl.pallas_call(
        body,
        out_shape=shapes,
        in_specs=[SMEM] * len(scalars) + [VMEM] * len(operands) + [ANY] * len(unread),
        out_specs=jax.tree.map(lambda _: VMEM, shapes),
        scratch_shapes=list(scratch),
        compiler_params=PARAMS,
    )(*scalars, *operands, *unread)


def shards(queries, key_vectors, value_vectors, windows):
    tokens = queries.shape[0]
    rows = PLACES * tokens
    columns = lax.axis_size("col")
    bf16, f32 = jnp.bfloat16, jnp.float32
    place = lax.axis_index("f") * 8 + lax.axis_index("uly")
    info = jnp.stack([place, lax.axis_index("col")]).astype(jnp.int32)
    win = windows.T

    def packed(kinds, sources, unread=()):
        def kernel(*refs):
            pack(kinds, *refs)

        shape = jax.ShapeDtypeStruct((PLACES, tokens, len(kinds) * DIM), bf16)
        return call(kernel, shape, [win], sources, [ORDER], unread)

    def exchange(value):
        return lax.all_to_all(value, GROUP, split_axis=0, concat_axis=0, tiled=True)

    def swap(value):
        return lax.ppermute(value, "g", [(0, 1), (1, 0)])

    here = exchange(packed((0, 0), [key_vectors, value_vectors])).reshape(rows, 2 * DIM)
    up = [(c, c + 1) for c in range(columns - 1)]
    lower = lax.ppermute(here, "col", up)
    upper = lax.ppermute(here, "col", [(b, a) for a, b in up])
    across = swap(here)
    second = exchange(
        packed((1, 1, 1, 0), [key_vectors, value_vectors, queries, queries], [here])
    ).reshape(rows, 4 * DIM)
    other_across = swap(second[:, : 2 * DIM])

    state = (jax.ShapeDtypeStruct((rows, DIM), f32), jax.ShapeDtypeStruct((rows, 2 * DIM), f32))
    held = [pltpu.VMEM((rows, DIM), f32), pltpu.VMEM((rows, 2 * DIM), f32), ORDER]
    peak, total = call(own_wide, state, [win, info], [second, here, across], [ORDER])
    other = call(
        own_other,
        jax.ShapeDtypeStruct((rows, DIM), bf16),
        [win, info],
        [second, other_across],
        held,
    )

    def here_kernel(*refs):
        next_here(columns, *refs)

    def across_kernel(*refs):
        next_across(columns, *refs)

    peak, total = call(
        here_kernel, state, [win, info], [second, lower, upper, peak, total], [ORDER]
    )
    result = call(
        across_kernel,
        jax.ShapeDtypeStruct((rows, 2 * DIM), bf16),
        [win, info],
        [second, swap(lower), swap(upper), peak, total, other],
        held,
    )
    back = exchange(result.reshape(PLACES, tokens, 2 * DIM))
    return call(unpack, jax.ShapeDtypeStruct((tokens, HEADS * DIM), bf16), [win], [back])


def solution(mesh):
    uly, blk, cfg = (mesh.shape[name] for name in ("uly", "blk", "cfg"))
    fine = Mesh(mesh.devices.reshape(uly, blk // 4, 2, 2, cfg), ("uly", "col", "f", "g", "cfg"))
    tokens = P(("cfg", "col", "f", "g", "uly"), None)
    return jax.shard_map(
        shards,
        mesh=fine,
        in_specs=(tokens, tokens, tokens, P()),
        out_specs=tokens,
        check_vma=False,
    )
```

```python
import jax
import jax.numpy as jnp
from jax import lax
from jax.experimental import pallas as pl
from jax.experimental.pallas import tpu as pltpu
from jax.sharding import Mesh
from jax.sharding import PartitionSpec as P

HEADS = 24
DIM = 128
TILE = 384
PLACES = 16
USED = 12
MEMBERS = 2 * PLACES
CHUNK = 16
GROUP = ("f", "g", "uly")
EXP2_SCALE = DIM**-0.5 * 1.4426950408889634
PARAMS = pltpu.CompilerParams(vmem_limit_bytes=48 * 1024 * 1024)


def fill_order(win, order):
    for place in range(MEMBERS):
        order[place] = 0

    def put(head, wide):
        is_wide = win[2, head] // 2
        order[jnp.where(is_wide > 0, wide, PLACES + head - wide)] = head
        return wide + is_wide

    lax.fori_loop(0, HEADS, put, jnp.int32(0))


def pack(count, win_hbm, *refs):
    sources = refs[:count]
    out, win, held, order, win_done, done = refs[-6:]
    first = pltpu.make_async_copy(win_hbm, win, win_done)
    first.start()
    copies = []
    for part, source in enumerate(sources):
        for chunk in range(source.shape[0] // CHUNK):
            rows = pl.ds(chunk * CHUNK, CHUNK)
            copy = pltpu.make_async_copy(
                source.at[rows, :], held.at[part, rows, :], done.at[part, chunk]
            )
            copy.start()
            copies.append(copy)
    first.wait()
    fill_order(win, order)
    for copy in copies:
        copy.wait()
    for member in range(MEMBERS):
        frame, row, uly = member // 16, member // 8 % 2, member % 8
        column = pl.multiple_of(order[row * PLACES + frame * 8 + uly] * DIM, DIM)
        for part in range(count):
            out[member, :, part * DIM : (part + 1) * DIM] = held[part, :, pl.ds(column, DIM)]


def my_windows(win, info, order):
    fill_order(win, order)
    head = order[info[1] * PLACES + info[0]]
    return info[0] < USED, win[0, head] // 2 > 0, win[1, head] // 2 > 0


def lanes(column, width):
    return jnp.broadcast_to(column, (column.shape[0], width))


def side_by_side(parts, axis):
    return parts[0] if len(parts) == 1 else jnp.concatenate(parts, axis=axis)


def score(query, kv, keys):
    parts = [
        lax.dot_general(
            query, kv[some, :DIM], (((1,), (1,)), ((), ())), preferred_element_type=jnp.float32
        )
        for some in keys
    ]
    return side_by_side(parts, 1)


def fold(scores, kv, keys, rows, peak, total, first):
    copies = scores.shape[1] // DIM
    now = lanes(jnp.max(scores, axis=1, keepdims=True), DIM)
    if not first:
        before = peak[rows, :]
        now = jnp.maximum(before, now)
    weights = jnp.exp2((scores - jnp.concatenate([now] * copies, axis=1)) * EXP2_SCALE)
    values = side_by_side([kv[some, DIM:] for some in keys], 0)
    with_ones = jnp.concatenate([values, jnp.ones_like(values)], axis=1)
    added = jnp.dot(weights.astype(jnp.bfloat16), with_ones, preferred_element_type=jnp.float32)
    peak[rows, :] = now
    if first:
        total[rows, :] = added
    else:
        fade = jnp.exp2((before - now) * EXP2_SCALE)
        total[rows, :] = total[rows, :] * jnp.concatenate([fade, fade], axis=1) + added


def visit(query, kv, frames, heights, peak, total, first=False):
    def chains(blocks, keys):
        ahead = score(query[blocks[0], :], kv, keys[0])
        for index, rows in enumerate(blocks):
            scores = ahead
            if index + 1 < len(blocks):
                ahead = score(query[blocks[index + 1], :], kv, keys[index + 1])
            fold(scores, kv, keys[index], rows, peak, total, first)

    def part(start, size, step):
        return pl.ds(pl.multiple_of(start, step), size)

    @pl.when(frames & heights)
    def _():
        def some(index, carry):
            blocks = [part(index * 512 + 256 * half, 256, 256) for half in range(2)]
            chains(blocks, [[pl.ds(0, 4 * TILE)]] * 2)
            return carry

        lax.fori_loop(0, 3, some, 0)

    @pl.when(frames != heights)
    def _():
        def some(index, carry):
            low = jnp.where(heights, 2 * index, index)
            starts = [low * TILE, (low + jnp.where(heights, 1, 2)) * TILE]
            keys = [part(start, TILE, TILE) for start in starts]
            blocks = [part(start + 192 * half, 192, 192) for start in starts for half in range(2)]
            chains(blocks, [keys] * 4)
            return carry

        lax.fori_loop(0, 2, some, 0)

    @pl.when(jnp.logical_not(frames | heights))
    def _():
        def some(index, carry):
            starts = [index * 2 * TILE, index * 2 * TILE + TILE]
            blocks = [part(start + 192 * half, 192, 192) for start in starts for half in range(2)]
            keys = [[part(start, TILE, TILE)] for start in starts for half in range(2)]
            chains(blocks, keys)
            return carry

        lax.fori_loop(0, 2, some, 0)


def own_column(win, info, query, kv, peak, total, order):
    used, frames, heights = my_windows(win, info, order)

    @pl.when(used)
    def _():
        visit(query, kv, frames, heights, peak, total, first=True)


def next_columns(columns, win, info, query, lower, upper, peak_in, total_in, out, peak, total, order):
    used, frames, heights = my_windows(win, info, order)
    wide = info[1] == 0

    @pl.when(used & jnp.logical_not(wide))
    def _():
        out[...] = (total_in[:, :DIM] / total_in[:, DIM:]).astype(jnp.bfloat16)

    @pl.when(used & wide)
    def _():
        peak[...] = peak_in[...]
        total[...] = total_in[...]

    @pl.when(used & wide & (info[2] > 0))
    def _():
        visit(query, lower, frames, heights, peak, total)

    @pl.when(used & wide & (info[2] < columns - 1))
    def _():
        visit(query, upper, frames, heights, peak, total)

    @pl.when(used & wide)
    def _():
        out[...] = (total[:, :DIM] / total[:, DIM:]).astype(jnp.bfloat16)


def unpack(win, received, out):
    wide = jnp.int32(0)
    for head in range(HEADS):
        is_wide = win[2, head] // 2
        place = jnp.where(is_wide > 0, wide, head - wide)
        member = place // 8 * 16 + (1 - is_wide) * 8 + place % 8
        out[:, head * DIM : (head + 1) * DIM] = received[member]
        wide = wide + is_wide


HBM = pl.BlockSpec(memory_space=pltpu.HBM)
SMEM = pl.BlockSpec(memory_space=pltpu.SMEM)
VMEM = pl.BlockSpec(memory_space=pltpu.VMEM)
ORDER = pltpu.SMEM((MEMBERS,), jnp.int32)


def call(kernel, shapes, scalars, operands, scratch=(), unread=(), given=SMEM, held=VMEM):
    def body(*refs):
        count = len(scalars) + len(operands)
        kernel(*refs[:count], *refs[count + len(unread) :])

    return pl.pallas_call(
        body,
        out_shape=shapes,
        in_specs=[given] * len(scalars) + [held] * len(operands) + [HBM] * len(unread),
        out_specs=jax.tree.map(lambda _: VMEM, shapes),
        scratch_shapes=list(scratch),
        compiler_params=PARAMS,
    )(*scalars, *operands, *unread)


def shards(queries, key_vectors, value_vectors, windows):
    tokens, width = queries.shape
    rows = MEMBERS * tokens
    columns = lax.axis_size("col")
    bf16, f32 = jnp.bfloat16, jnp.float32
    place = lax.axis_index("f") * 8 + lax.axis_index("uly")
    info = jnp.stack([place, lax.axis_index("g"), lax.axis_index("col")]).astype(jnp.int32)
    win = windows.T

    def packed(sources, unread=()):
        count = len(sources)

        def kernel(*refs):
            pack(count, *refs)

        scratch = [
            pltpu.SMEM(win.shape, jnp.int32),
            pltpu.VMEM((count, tokens, width), bf16),
            ORDER,
            pltpu.SemaphoreType.DMA,
            pltpu.SemaphoreType.DMA((count, tokens // CHUNK)),
        ]
        shape = jax.ShapeDtypeStruct((MEMBERS, tokens, count * DIM), bf16)
        return call(kernel, shape, [win], sources, scratch, unread, HBM, HBM)

    def exchange(value):
        return lax.all_to_all(value, GROUP, split_axis=0, concat_axis=0, tiled=True)

    kv = exchange(packed([key_vectors, value_vectors])).reshape(rows, 2 * DIM)
    sending = [
        ((uly * columns + col) * 2 + frame) * 2
        for uly in range(8)
        for col in range(columns - 1)
        for frame in range(2)
        if frame * 8 + uly < USED
    ]
    along = ("uly", "col", "f", "g")
    lower = lax.ppermute(kv, along, [(member, member + 4) for member in sending])
    upper = lax.ppermute(kv, along, [(member + 4, member) for member in sending])
    query = exchange(packed([queries], [kv])).reshape(rows, DIM)
    peak, total = call(
        own_column,
        (jax.ShapeDtypeStruct((rows, DIM), f32), jax.ShapeDtypeStruct((rows, 2 * DIM), f32)),
        [win, info],
        [query, kv],
        [ORDER],
    )

    def next_kernel(*refs):
        next_columns(columns, *refs)

    result = call(
        next_kernel,
        jax.ShapeDtypeStruct((rows, DIM), bf16),
        [win, info],
        [query, lower, upper, peak, total],
        [pltpu.VMEM((rows, DIM), f32), pltpu.VMEM((rows, 2 * DIM), f32), ORDER],
    )
    back = exchange(result.reshape(MEMBERS, tokens, DIM))
    return call(unpack, jax.ShapeDtypeStruct((tokens, HEADS * DIM), bf16), [win], [back])


def solution(mesh):
    uly, blk, cfg = (mesh.shape[name] for name in ("uly", "blk", "cfg"))
    fine = Mesh(mesh.devices.reshape(uly, blk // 4, 2, 2, cfg), ("uly", "col", "f", "g", "cfg"))
    tokens = P(("cfg", "col", "f", "g", "uly"), None)
    return jax.shard_map(
        shards,
        mesh=fine,
        in_specs=(tokens, tokens, tokens, P()),
        out_specs=tokens,
        check_vma=False,
    )
```

```python
import jax
import jax.numpy as jnp
from jax import lax
from jax.experimental import pallas as pl
from jax.experimental.pallas import tpu as pltpu
from jax.sharding import Mesh
from jax.sharding import PartitionSpec as P

HEADS = 24
DIM = 128
TILE = 384
PLACES = 16
USED = 12
MEMBERS = 2 * PLACES
CHUNK = 16
GROUP = ("f", "g", "uly")
EXP2_SCALE = DIM**-0.5 * 1.4426950408889634
PARAMS = pltpu.CompilerParams(vmem_limit_bytes=48 * 1024 * 1024)


def fill_order(win, order):
    for place in range(MEMBERS):
        order[place] = 0

    def put(head, wide):
        is_wide = win[2, head] // 2
        order[jnp.where(is_wide > 0, wide, PLACES + head - wide)] = head
        return wide + is_wide

    lax.fori_loop(0, HEADS, put, jnp.int32(0))


def pack(count, win_hbm, *refs):
    sources = refs[:count]
    out, win, held, order, win_done, done = refs[-6:]
    first = pltpu.make_async_copy(win_hbm, win, win_done)
    first.start()
    copies = []
    for part, source in enumerate(sources):
        for chunk in range(source.shape[0] // CHUNK):
            rows = pl.ds(chunk * CHUNK, CHUNK)
            copy = pltpu.make_async_copy(
                source.at[rows, :], held.at[part, rows, :], done.at[part, chunk]
            )
            copy.start()
            copies.append(copy)
    first.wait()
    fill_order(win, order)
    for copy in copies:
        copy.wait()
    for member in range(MEMBERS):
        frame, row, uly = member // 16, member // 8 % 2, member % 8
        column = pl.multiple_of(order[row * PLACES + frame * 8 + uly] * DIM, DIM)
        for part in range(count):
            out[member, :, part * DIM : (part + 1) * DIM] = held[part, :, pl.ds(column, DIM)]


def my_windows(win, info, order):
    fill_order(win, order)
    head = order[info[1] * PLACES + info[0]]
    return info[0] < USED, win[0, head] // 2 > 0, win[1, head] // 2 > 0


def lanes(column, width):
    return jnp.broadcast_to(column, (column.shape[0], width))


def side_by_side(parts, axis):
    return parts[0] if len(parts) == 1 else jnp.concatenate(parts, axis=axis)


def score(query, kv, keys):
    parts = [
        lax.dot_general(
            query, kv[some, :DIM], (((1,), (1,)), ((), ())), preferred_element_type=jnp.float32
        )
        for some in keys
    ]
    return side_by_side(parts, 1)


def fold(scores, kv, keys, rows, peak, total, first):
    copies = scores.shape[1] // DIM
    now = lanes(jnp.max(scores, axis=1, keepdims=True), DIM)
    if not first:
        before = peak[rows, :]
        now = jnp.maximum(before, now)
    weights = jnp.exp2((scores - jnp.concatenate([now] * copies, axis=1)) * EXP2_SCALE)
    values = side_by_side([kv[some, DIM:] for some in keys], 0)
    with_ones = jnp.concatenate([values, jnp.ones_like(values)], axis=1)
    added = jnp.dot(weights.astype(jnp.bfloat16), with_ones, preferred_element_type=jnp.float32)
    peak[rows, :] = now
    if first:
        total[rows, :] = added
    else:
        fade = jnp.exp2((before - now) * EXP2_SCALE)
        total[rows, :] = total[rows, :] * jnp.concatenate([fade, fade], axis=1) + added


def visit(query, kv, frames, heights, peak, total, first=False):
    def chains(blocks, keys):
        ahead = score(query[blocks[0], :], kv, keys[0])
        for index, rows in enumerate(blocks):
            scores = ahead
            if index + 1 < len(blocks):
                ahead = score(query[blocks[index + 1], :], kv, keys[index + 1])
            fold(scores, kv, keys[index], rows, peak, total, first)

    def part(start, size, step):
        return pl.ds(pl.multiple_of(start, step), size)

    @pl.when(frames & heights)
    def _():
        def some(index, carry):
            blocks = [part(index * 512 + 256 * half, 256, 256) for half in range(2)]
            chains(blocks, [[pl.ds(0, 4 * TILE)]] * 2)
            return carry

        lax.fori_loop(0, 3, some, 0)

    @pl.when(frames != heights)
    def _():
        def some(index, carry):
            low = jnp.where(heights, 2 * index, index)
            starts = [low * TILE, (low + jnp.where(heights, 1, 2)) * TILE]
            keys = [part(start, TILE, TILE) for start in starts]
            blocks = [part(start + 192 * half, 192, 192) for start in starts for half in range(2)]
            chains(blocks, [keys] * 4)
            return carry

        lax.fori_loop(0, 2, some, 0)

    @pl.when(jnp.logical_not(frames | heights))
    def _():
        def some(index, carry):
            starts = [index * 2 * TILE, index * 2 * TILE + TILE]
            blocks = [part(start + 192 * half, 192, 192) for start in starts for half in range(2)]
            keys = [[part(start, TILE, TILE)] for start in starts for half in range(2)]
            chains(blocks, keys)
            return carry

        lax.fori_loop(0, 2, some, 0)


def own_column(win, info, query, kv, peak, total, order):
    used, frames, heights = my_windows(win, info, order)

    @pl.when(used)
    def _():
        visit(query, kv, frames, heights, peak, total, first=True)


def next_columns(columns, win, info, query, lower, upper, peak_in, total_in, out, peak, total, order):
    used, frames, heights = my_windows(win, info, order)
    wide = info[1] == 0

    @pl.when(used & jnp.logical_not(wide))
    def _():
        out[...] = (total_in[:, :DIM] / total_in[:, DIM:]).astype(jnp.bfloat16)

    @pl.when(used & wide)
    def _():
        peak[...] = peak_in[...]
        total[...] = total_in[...]

    @pl.when(used & wide & (info[2] > 0))
    def _():
        visit(query, lower, frames, heights, peak, total)

    @pl.when(used & wide & (info[2] < columns - 1))
    def _():
        visit(query, upper, frames, heights, peak, total)

    @pl.when(used & wide)
    def _():
        out[...] = (total[:, :DIM] / total[:, DIM:]).astype(jnp.bfloat16)


def unpack(win, received, out):
    wide = jnp.int32(0)
    for head in range(HEADS):
        is_wide = win[2, head] // 2
        place = jnp.where(is_wide > 0, wide, head - wide)
        member = place // 8 * 16 + (1 - is_wide) * 8 + place % 8
        out[:, head * DIM : (head + 1) * DIM] = received[member]
        wide = wide + is_wide


HBM = pl.BlockSpec(memory_space=pltpu.HBM)
SMEM = pl.BlockSpec(memory_space=pltpu.SMEM)
VMEM = pl.BlockSpec(memory_space=pltpu.VMEM)
ORDER = pltpu.SMEM((MEMBERS,), jnp.int32)


def call(kernel, shapes, scalars, operands, scratch=(), unread=(), given=SMEM, held=VMEM):
    def body(*refs):
        count = len(scalars) + len(operands)
        kernel(*refs[:count], *refs[count + len(unread) :])

    return pl.pallas_call(
        body,
        out_shape=shapes,
        in_specs=[given] * len(scalars) + [held] * len(operands) + [HBM] * len(unread),
        out_specs=jax.tree.map(lambda _: VMEM, shapes),
        scratch_shapes=list(scratch),
        compiler_params=PARAMS,
        cost_estimate=pl.CostEstimate(flops=1000, transcendentals=0, bytes_accessed=1000),
    )(*scalars, *operands, *unread)


def shards(queries, key_vectors, value_vectors, windows):
    tokens, width = queries.shape
    rows = MEMBERS * tokens
    columns = lax.axis_size("col")
    bf16, f32 = jnp.bfloat16, jnp.float32
    place = lax.axis_index("f") * 8 + lax.axis_index("uly")
    info = jnp.stack([place, lax.axis_index("g"), lax.axis_index("col")]).astype(jnp.int32)
    win = windows.T

    def packed(sources, unread=()):
        count = len(sources)

        def kernel(*refs):
            pack(count, *refs)

        scratch = [
            pltpu.SMEM(win.shape, jnp.int32),
            pltpu.VMEM((count, tokens, width), bf16),
            ORDER,
            pltpu.SemaphoreType.DMA,
            pltpu.SemaphoreType.DMA((count, tokens // CHUNK)),
        ]
        shape = jax.ShapeDtypeStruct((MEMBERS, tokens, count * DIM), bf16)
        return call(kernel, shape, [win], sources, scratch, unread, HBM, HBM)

    def exchange(value):
        return lax.all_to_all(value, GROUP, split_axis=0, concat_axis=0, tiled=True)

    kv = exchange(packed([key_vectors, value_vectors])).reshape(rows, 2 * DIM)
    sending = [
        ((uly * columns + col) * 2 + frame) * 2
        for uly in range(8)
        for col in range(columns - 1)
        for frame in range(2)
        if frame * 8 + uly < USED
    ]
    along = ("uly", "col", "f", "g")
    lower = lax.ppermute(kv, along, [(member, member + 4) for member in sending])
    upper = lax.ppermute(kv, along, [(member + 4, member) for member in sending])
    query = exchange(packed([queries], [kv])).reshape(rows, DIM)
    peak, total = call(
        own_column,
        (jax.ShapeDtypeStruct((rows, DIM), f32), jax.ShapeDtypeStruct((rows, 2 * DIM), f32)),
        [win, info],
        [query, kv],
        [ORDER],
    )

    def next_kernel(*refs):
        next_columns(columns, *refs)

    result = call(
        next_kernel,
        jax.ShapeDtypeStruct((rows, DIM), bf16),
        [win, info],
        [query, lower, upper, peak, total],
        [pltpu.VMEM((rows, DIM), f32), pltpu.VMEM((rows, 2 * DIM), f32), ORDER],
    )
    back = exchange(result.reshape(MEMBERS, tokens, DIM))
    return call(unpack, jax.ShapeDtypeStruct((tokens, HEADS * DIM), bf16), [win], [back])


def solution(mesh):
    uly, blk, cfg = (mesh.shape[name] for name in ("uly", "blk", "cfg"))
    fine = Mesh(mesh.devices.reshape(uly, blk // 4, 2, 2, cfg), ("uly", "col", "f", "g", "cfg"))
    tokens = P(("cfg", "col", "f", "g", "uly"), None)
    return jax.shard_map(
        shards,
        mesh=fine,
        in_specs=(tokens, tokens, tokens, P()),
        out_specs=tokens,
        check_vma=False,
    )
```

```python
import jax
import jax.numpy as jnp
from jax import lax
from jax.experimental import pallas as pl
from jax.experimental.pallas import tpu as pltpu
from jax.sharding import Mesh
from jax.sharding import PartitionSpec as P

HEADS = 24
DIM = 128
TILE = 384
PLACES = 16
USED = 12
MEMBERS = 2 * PLACES
CHUNK = 16
GROUP = ("f", "g", "uly")
EXP2_SCALE = DIM**-0.5 * 1.4426950408889634
PARAMS = pltpu.CompilerParams(vmem_limit_bytes=48 * 1024 * 1024)


def fill_order(win, order):
    for place in range(MEMBERS):
        order[place] = 0

    def put(head, wide):
        is_wide = win[2, head] // 2
        order[jnp.where(is_wide > 0, wide, PLACES + head - wide)] = head
        return wide + is_wide

    lax.fori_loop(0, HEADS, put, jnp.int32(0))


def pack(count, win_hbm, *refs):
    sources = refs[:count]
    out, win, held, order, win_done, done = refs[-6:]
    first = pltpu.make_async_copy(win_hbm, win, win_done)
    first.start()
    copies = []
    for part, source in enumerate(sources):
        for chunk in range(source.shape[0] // CHUNK):
            rows = pl.ds(chunk * CHUNK, CHUNK)
            copy = pltpu.make_async_copy(
                source.at[rows, :], held.at[part, rows, :], done.at[part, chunk]
            )
            copy.start()
            copies.append(copy)
    first.wait()
    fill_order(win, order)
    for copy in copies:
        copy.wait()
    for member in range(MEMBERS):
        frame, row, uly = member // 16, member // 8 % 2, member % 8
        column = pl.multiple_of(order[row * PLACES + frame * 8 + uly] * DIM, DIM)
        for part in range(count):
            out[member, :, part * DIM : (part + 1) * DIM] = held[part, :, pl.ds(column, DIM)]


def my_windows(win, info, order):
    fill_order(win, order)
    head = order[info[1] * PLACES + info[0]]
    return info[0] < USED, win[0, head] // 2 > 0, win[1, head] // 2 > 0


def lanes(column, width):
    return jnp.broadcast_to(column, (column.shape[0], width))


def side_by_side(parts, axis):
    return parts[0] if len(parts) == 1 else jnp.concatenate(parts, axis=axis)


def score(query, kv, keys):
    parts = [
        lax.dot_general(
            query, kv[some, :DIM], (((1,), (1,)), ((), ())), preferred_element_type=jnp.float32
        )
        for some in keys
    ]
    return side_by_side(parts, 1)


def fold(scores, kv, keys, rows, peak, total, first):
    copies = scores.shape[1] // DIM
    now = lanes(jnp.max(scores, axis=1, keepdims=True), DIM)
    if not first:
        before = peak[rows, :]
        now = jnp.maximum(before, now)
    weights = jnp.exp2((scores - jnp.concatenate([now] * copies, axis=1)) * EXP2_SCALE)
    values = side_by_side([kv[some, DIM:] for some in keys], 0)
    with_ones = jnp.concatenate([values, jnp.ones_like(values)], axis=1)
    added = jnp.dot(weights.astype(jnp.bfloat16), with_ones, preferred_element_type=jnp.float32)
    peak[rows, :] = now
    if first:
        total[rows, :] = added
    else:
        fade = jnp.exp2((before - now) * EXP2_SCALE)
        total[rows, :] = total[rows, :] * jnp.concatenate([fade, fade], axis=1) + added


def visit(query, kv, frames, heights, peak, total, first=False):
    def chains(blocks, keys):
        ahead = score(query[blocks[0], :], kv, keys[0])
        for index, rows in enumerate(blocks):
            scores = ahead
            if index + 1 < len(blocks):
                ahead = score(query[blocks[index + 1], :], kv, keys[index + 1])
            fold(scores, kv, keys[index], rows, peak, total, first)

    def part(start, size, step):
        return pl.ds(pl.multiple_of(start, step), size)

    @pl.when(frames & heights)
    def _():
        def some(index, carry):
            blocks = [part(index * 512 + 256 * half, 256, 256) for half in range(2)]
            chains(blocks, [[pl.ds(0, 4 * TILE)]] * 2)
            return carry

        lax.fori_loop(0, 3, some, 0)

    @pl.when(frames != heights)
    def _():
        def some(index, carry):
            low = jnp.where(heights, 2 * index, index)
            starts = [low * TILE, (low + jnp.where(heights, 1, 2)) * TILE]
            keys = [part(start, TILE, TILE) for start in starts]
            blocks = [part(start + 192 * half, 192, 192) for start in starts for half in range(2)]
            chains(blocks, [keys] * 4)
            return carry

        lax.fori_loop(0, 2, some, 0)

    @pl.when(jnp.logical_not(frames | heights))
    def _():
        def some(index, carry):
            starts = [index * 2 * TILE, index * 2 * TILE + TILE]
            blocks = [part(start + 192 * half, 192, 192) for start in starts for half in range(2)]
            keys = [[part(start, TILE, TILE)] for start in starts for half in range(2)]
            chains(blocks, keys)
            return carry

        lax.fori_loop(0, 2, some, 0)


def own_column(win, info, query, kv, peak, total, order):
    used, frames, heights = my_windows(win, info, order)

    @pl.when(used)
    def _():
        visit(query, kv, frames, heights, peak, total, first=True)


def next_columns(columns, win, info, query, lower, upper, peak_in, total_in, out, peak, total, order):
    used, frames, heights = my_windows(win, info, order)
    wide = info[1] == 0

    @pl.when(used & jnp.logical_not(wide))
    def _():
        out[...] = (total_in[:, :DIM] / total_in[:, DIM:]).astype(jnp.bfloat16)

    @pl.when(used & wide)
    def _():
        peak[...] = peak_in[...]
        total[...] = total_in[...]

    @pl.when(used & wide & (info[2] > 0))
    def _():
        visit(query, lower, frames, heights, peak, total)

    @pl.when(used & wide & (info[2] < columns - 1))
    def _():
        visit(query, upper, frames, heights, peak, total)

    @pl.when(used & wide)
    def _():
        out[...] = (total[:, :DIM] / total[:, DIM:]).astype(jnp.bfloat16)


def unpack(win, received, out):
    wide = jnp.int32(0)
    for head in range(HEADS):
        is_wide = win[2, head] // 2
        place = jnp.where(is_wide > 0, wide, head - wide)
        member = place // 8 * 16 + (1 - is_wide) * 8 + place % 8
        out[:, head * DIM : (head + 1) * DIM] = received[member]
        wide = wide + is_wide


HBM = pl.BlockSpec(memory_space=pltpu.HBM)
SMEM = pl.BlockSpec(memory_space=pltpu.SMEM)
VMEM = pl.BlockSpec(memory_space=pltpu.VMEM)
ORDER = pltpu.SMEM((MEMBERS,), jnp.int32)


def call(kernel, shapes, scalars, operands, scratch=(), unread=(), given=SMEM, held=VMEM):
    def body(*refs):
        count = len(scalars) + len(operands)
        kernel(*refs[:count], *refs[count + len(unread) :])

    return pl.pallas_call(
        body,
        out_shape=shapes,
        in_specs=[given] * len(scalars) + [held] * len(operands) + [HBM] * len(unread),
        out_specs=jax.tree.map(lambda _: VMEM, shapes),
        scratch_shapes=list(scratch),
        compiler_params=PARAMS,
    )(*scalars, *operands, *unread)


def shards(queries, key_vectors, value_vectors, windows):
    tokens, width = queries.shape
    rows = MEMBERS * tokens
    columns = lax.axis_size("col")
    bf16, f32 = jnp.bfloat16, jnp.float32
    place = lax.axis_index("f") * 8 + lax.axis_index("uly")
    info = jnp.stack([place, lax.axis_index("g"), lax.axis_index("col")]).astype(jnp.int32)
    win = windows.T

    def packed(sources, unread=()):
        count = len(sources)

        def kernel(*refs):
            pack(count, *refs)

        scratch = [
            pltpu.SMEM(win.shape, jnp.int32),
            pltpu.VMEM((count, tokens, width), bf16),
            ORDER,
            pltpu.SemaphoreType.DMA,
            pltpu.SemaphoreType.DMA((count, tokens // CHUNK)),
        ]
        shape = jax.ShapeDtypeStruct((MEMBERS, tokens, count * DIM), bf16)
        return call(kernel, shape, [win], sources, scratch, unread, HBM, HBM)

    def exchange(value):
        return lax.all_to_all(value, GROUP, split_axis=0, concat_axis=0, tiled=True)

    kv = exchange(packed([key_vectors, value_vectors])).reshape(rows, 2 * DIM)
    query_out = packed([queries])
    sending = [
        ((uly * columns + col) * 2 + frame) * 2
        for uly in range(8)
        for col in range(columns - 1)
        for frame in range(2)
        if frame * 8 + uly < USED
    ]
    along = ("uly", "col", "f", "g")
    lower = lax.ppermute(kv, along, [(member, member + 4) for member in sending])
    upper = lax.ppermute(kv, along, [(member + 4, member) for member in sending])
    state = (jax.ShapeDtypeStruct((rows, DIM), f32), jax.ShapeDtypeStruct((rows, 2 * DIM), f32))

    def own(query_out, kv):
        query = exchange(query_out).reshape(rows, DIM)
        return query, *call(own_column, state, [win, info], [query, kv], [ORDER])

    def nothing(query_out, kv):
        return jnp.zeros((rows, DIM), bf16), *(jnp.zeros(each.shape, f32) for each in state)

    query, peak, total = lax.cond(windows[0, 0] > 0, own, nothing, query_out, kv)

    def next_kernel(*refs):
        next_columns(columns, *refs)

    result = call(
        next_kernel,
        jax.ShapeDtypeStruct((rows, DIM), bf16),
        [win, info],
        [query, lower, upper, peak, total],
        [pltpu.VMEM((rows, DIM), f32), pltpu.VMEM((rows, 2 * DIM), f32), ORDER],
    )
    back = exchange(result.reshape(MEMBERS, tokens, DIM))
    return call(unpack, jax.ShapeDtypeStruct((tokens, HEADS * DIM), bf16), [win], [back])


def solution(mesh):
    uly, blk, cfg = (mesh.shape[name] for name in ("uly", "blk", "cfg"))
    fine = Mesh(mesh.devices.reshape(uly, blk // 4, 2, 2, cfg), ("uly", "col", "f", "g", "cfg"))
    tokens = P(("cfg", "col", "f", "g", "uly"), None)
    return jax.shard_map(
        shards,
        mesh=fine,
        in_specs=(tokens, tokens, tokens, P()),
        out_specs=tokens,
        check_vma=False,
    )
```

```python
import jax
import jax.numpy as jnp
from jax import lax
from jax.experimental import pallas as pl
from jax.experimental.pallas import tpu as pltpu
from jax.sharding import Mesh
from jax.sharding import PartitionSpec as P

HEADS = 24
DIM = 128
TILE = 384
PLACES = 16
USED = 12
MEMBERS = 2 * PLACES
CHUNK = 16
BATCH = 4
PACK_VMEM = 62 * 1024 * 1024
GROUP = ("f", "g", "uly")
EXP2_SCALE = DIM**-0.5 * 1.4426950408889634
PARAMS = pltpu.CompilerParams(vmem_limit_bytes=48 * 1024 * 1024)


def fill_order(win, order):
    for place in range(MEMBERS):
        order[place] = 0

    def put(head, wide):
        is_wide = win[2, head] // 2
        order[jnp.where(is_wide > 0, wide, PLACES + head - wide)] = head
        return wide + is_wide

    lax.fori_loop(0, HEADS, put, jnp.int32(0))


def pack(count, win_hbm, *refs):
    sources = refs[:count]
    out, win, held, staged, order, win_done, done, out_done = refs[-8:]
    first = pltpu.make_async_copy(win_hbm, win, win_done)
    first.start()
    copies = []
    for part, source in enumerate(sources):
        for chunk in range(source.shape[0] // CHUNK):
            rows = pl.ds(chunk * CHUNK, CHUNK)
            copy = pltpu.make_async_copy(
                source.at[rows, :], held.at[part, rows, :], done.at[part, chunk]
            )
            copy.start()
            copies.append(copy)
    first.wait()
    fill_order(win, order)
    for copy in copies:
        copy.wait()
    sent = []
    for member in range(MEMBERS):
        frame, row, uly = member // 16, member // 8 % 2, member % 8
        column = pl.multiple_of(order[row * PLACES + frame * 8 + uly] * DIM, DIM)
        for part in range(count):
            staged[member, :, part * DIM : (part + 1) * DIM] = held[part, :, pl.ds(column, DIM)]
        if member % BATCH == BATCH - 1:
            some = pl.ds(member + 1 - BATCH, BATCH)
            copy = pltpu.make_async_copy(
                staged.at[some], out.at[some], out_done.at[member // BATCH]
            )
            copy.start()
            sent.append(copy)
    for copy in sent:
        copy.wait()


def my_windows(win, info, order):
    fill_order(win, order)
    head = order[info[1] * PLACES + info[0]]
    return info[0] < USED, win[0, head] // 2 > 0, win[1, head] // 2 > 0


def lanes(column, width):
    return jnp.broadcast_to(column, (column.shape[0], width))


def side_by_side(parts, axis):
    return parts[0] if len(parts) == 1 else jnp.concatenate(parts, axis=axis)


def score(query, kv, keys):
    parts = [
        lax.dot_general(
            query, kv[some, :DIM], (((1,), (1,)), ((), ())), preferred_element_type=jnp.float32
        )
        for some in keys
    ]
    return side_by_side(parts, 1)


def fold(scores, kv, keys, rows, peak, total, first):
    copies = scores.shape[1] // DIM
    now = lanes(jnp.max(scores, axis=1, keepdims=True), DIM)
    if not first:
        before = peak[rows, :]
        now = jnp.maximum(before, now)
    weights = jnp.exp2((scores - jnp.concatenate([now] * copies, axis=1)) * EXP2_SCALE)
    values = side_by_side([kv[some, DIM : 2 * DIM] for some in keys], 0)
    with_ones = jnp.concatenate([values, jnp.ones_like(values)], axis=1)
    added = jnp.dot(weights.astype(jnp.bfloat16), with_ones, preferred_element_type=jnp.float32)
    peak[rows, :] = now
    if first:
        total[rows, :] = added
    else:
        fade = jnp.exp2((before - now) * EXP2_SCALE)
        total[rows, :] = total[rows, :] * jnp.concatenate([fade, fade], axis=1) + added


def visit(query, kv, keys_at, lo, hi, heights, peak, total, first=False):
    def part(start, size, step):
        return pl.ds(pl.multiple_of(start, step), size)

    def chains(blocks):
        ahead = score(query[blocks[0][0], :], kv, blocks[0][1])
        for index, (rows, keys) in enumerate(blocks):
            scores = ahead
            if index + 1 < len(blocks):
                ahead = score(query[blocks[index + 1][0], :], kv, blocks[index + 1][1])
            fold(scores, kv, keys, rows, peak, total, first)

    @pl.when(heights)
    def _():
        def frame(index, carry):
            keys = [part(keys_at, 2 * TILE, TILE)]
            chains([(part(index * 2 * TILE + 256 * n, 256, 256), keys) for n in range(3)])
            return carry

        lax.fori_loop(lo, hi, frame, 0)

    @pl.when(jnp.logical_not(heights))
    def _():
        def frame(index, carry):
            chains(
                [
                    (
                        part(index * 2 * TILE + row * TILE + 192 * n, 192, 192),
                        [part(keys_at + row * TILE, TILE, TILE)],
                    )
                    for row in range(2)
                    for n in range(2)
                ]
            )
            return carry

        lax.fori_loop(lo, hi, frame, 0)


def own_column(win, info, qkv, peak, total, order):
    used, frames, heights = my_windows(win, info, order)
    query = qkv.at[:, 2 * DIM :]
    for own in range(2):

        @pl.when(used)
        def _(own=own):
            visit(query, qkv, own * 2 * TILE, own, own + 1, heights, peak, total, first=True)

        @pl.when(used & frames)
        def _(own=own):
            visit(query, qkv, (1 - own) * 2 * TILE, own, own + 1, heights, peak, total)


def next_columns(columns, frame, last, win, info, qkv, lower, upper, peak_in, total_in, *refs):
    out, (peak, total, order) = refs[:-3], refs[-3:]
    if not last:
        out, (peak, total), order = (), refs[:2], refs[2]
    used, frames, heights = my_windows(win, info, order)
    wide = info[1] == 0
    query = qkv.at[:, 2 * DIM :]
    lo = jnp.where(frames, 0, frame)
    hi = jnp.where(frames, 2, frame + 1)

    @pl.when(used)
    def _():
        peak[...] = peak_in[...]
        total[...] = total_in[...]

    @pl.when(used & wide & (info[2] > 0))
    def _():
        visit(query, lower, 0, lo, hi, heights, peak, total)

    @pl.when(used & wide & (info[2] < columns - 1))
    def _():
        visit(query, upper, 0, lo, hi, heights, peak, total)

    if last:

        @pl.when(used)
        def _():
            out[0][...] = (total[:, :DIM] / total[:, DIM:]).astype(jnp.bfloat16)


def unpack(win, received, out):
    wide = jnp.int32(0)
    for head in range(HEADS):
        is_wide = win[2, head] // 2
        place = jnp.where(is_wide > 0, wide, head - wide)
        member = place // 8 * 16 + (1 - is_wide) * 8 + place % 8
        out[:, head * DIM : (head + 1) * DIM] = received[member]
        wide = wide + is_wide


HBM = pl.BlockSpec(memory_space=pltpu.HBM)
SMEM = pl.BlockSpec(memory_space=pltpu.SMEM)
VMEM = pl.BlockSpec(memory_space=pltpu.VMEM)
ORDER = pltpu.SMEM((MEMBERS,), jnp.int32)


def call(kernel, shapes, scalars, operands, scratch=()):
    return pl.pallas_call(
        kernel,
        out_shape=shapes,
        in_specs=[SMEM] * len(scalars) + [VMEM] * len(operands),
        out_specs=jax.tree.map(lambda _: VMEM, shapes),
        scratch_shapes=list(scratch),
        compiler_params=PARAMS,
    )(*scalars, *operands)


def shards(queries, key_vectors, value_vectors, windows):
    tokens, width = queries.shape
    rows = MEMBERS * tokens
    half = rows // 2
    columns = lax.axis_size("col")
    bf16, f32 = jnp.bfloat16, jnp.float32
    place = lax.axis_index("f") * 8 + lax.axis_index("uly")
    info = jnp.stack([place, lax.axis_index("g"), lax.axis_index("col")]).astype(jnp.int32)
    win = windows.T
    sources = [key_vectors, value_vectors, queries]
    count = len(sources)

    def pack_kernel(*refs):
        pack(count, *refs)

    def exchange(value):
        return lax.all_to_all(value, GROUP, split_axis=0, concat_axis=0, tiled=True)

    sendable = pl.pallas_call(
        pack_kernel,
        out_shape=jax.ShapeDtypeStruct((MEMBERS, tokens, count * DIM), bf16),
        in_specs=[HBM] * (1 + count),
        out_specs=HBM,
        scratch_shapes=[
            pltpu.SMEM(win.shape, jnp.int32),
            pltpu.VMEM((count, tokens, width), bf16),
            pltpu.VMEM((MEMBERS, tokens, count * DIM), bf16),
            ORDER,
            pltpu.SemaphoreType.DMA,
            pltpu.SemaphoreType.DMA((count, tokens // CHUNK)),
            pltpu.SemaphoreType.DMA((MEMBERS // BATCH,)),
        ],
        compiler_params=pltpu.CompilerParams(vmem_limit_bytes=PACK_VMEM),
    )(win, *sources)
    qkv = exchange(sendable).reshape(rows, count * DIM)

    sending = [
        ((uly * columns + col) * 2 + frame) * 2
        for uly in range(8)
        for col in range(columns - 1)
        for frame in range(2)
        if frame * 8 + uly < USED
    ]
    along = ("uly", "col", "f", "g")
    beside = []
    for frame in range(2):
        kv = qkv[frame * half : (frame + 1) * half, : 2 * DIM]
        lower = lax.ppermute(kv, along, [(member, member + 4) for member in sending])
        upper = lax.ppermute(kv, along, [(member + 4, member) for member in sending])
        beside.append([lower, upper])

    state = (jax.ShapeDtypeStruct((rows, DIM), f32), jax.ShapeDtypeStruct((rows, 2 * DIM), f32))
    peak, total = call(own_column, state, [win, info], [qkv], [ORDER])

    def first_kernel(*refs):
        next_columns(columns, 0, False, *refs)

    def last_kernel(*refs):
        next_columns(columns, 1, True, *refs)

    peak, total = call(first_kernel, state, [win, info], [qkv, *beside[0], peak, total], [ORDER])
    result = call(
        last_kernel,
        jax.ShapeDtypeStruct((rows, DIM), bf16),
        [win, info],
        [qkv, *beside[1], peak, total],
        [pltpu.VMEM((rows, DIM), f32), pltpu.VMEM((rows, 2 * DIM), f32), ORDER],
    )
    back = exchange(result.reshape(MEMBERS, tokens, DIM))
    return call(unpack, jax.ShapeDtypeStruct((tokens, HEADS * DIM), bf16), [win], [back])


def solution(mesh):
    uly, blk, cfg = (mesh.shape[name] for name in ("uly", "blk", "cfg"))
    fine = Mesh(mesh.devices.reshape(uly, blk // 4, 2, 2, cfg), ("uly", "col", "f", "g", "cfg"))
    tokens = P(("cfg", "col", "f", "g", "uly"), None)
    return jax.shard_map(
        shards,
        mesh=fine,
        in_specs=(tokens, tokens, tokens, P()),
        out_specs=tokens,
        check_vma=False,
    )
```

```python
import jax
import jax.numpy as jnp
from jax import lax
from jax.experimental import pallas as pl
from jax.experimental.pallas import tpu as pltpu
from jax.sharding import Mesh
from jax.sharding import PartitionSpec as P

HEADS = 24
DIM = 128
TILE = 384
PLACES = 16
USED = 12
MEMBERS = 2 * PLACES
CHUNK = 16
BATCH = 4
PACK_VMEM = 62 * 1024 * 1024
GROUP = ("f", "g", "uly")
EXP2_SCALE = DIM**-0.5 * 1.4426950408889634
PARAMS = pltpu.CompilerParams(vmem_limit_bytes=32 * 1024 * 1024)


def fill_order(win, order):
    for place in range(MEMBERS):
        order[place] = 0

    def put(head, wide):
        is_wide = win[2, head] // 2
        order[jnp.where(is_wide > 0, wide, PLACES + head - wide)] = head
        return wide + is_wide

    lax.fori_loop(0, HEADS, put, jnp.int32(0))


def pack(count, win_hbm, *refs):
    sources = refs[:count]
    out, win, held, staged, order, win_done, done, out_done = refs[-8:]
    first = pltpu.make_async_copy(win_hbm, win, win_done)
    first.start()
    copies = []
    for part, source in enumerate(sources):
        for chunk in range(source.shape[0] // CHUNK):
            rows = pl.ds(chunk * CHUNK, CHUNK)
            copy = pltpu.make_async_copy(
                source.at[rows, :], held.at[part, rows, :], done.at[part, chunk]
            )
            copy.start()
            copies.append(copy)
    first.wait()
    fill_order(win, order)
    for copy in copies:
        copy.wait()
    sent = []
    for member in range(MEMBERS):
        frame, row, uly = member // 16, member // 8 % 2, member % 8
        column = pl.multiple_of(order[row * PLACES + frame * 8 + uly] * DIM, DIM)
        for part in range(count):
            staged[member, :, part * DIM : (part + 1) * DIM] = held[part, :, pl.ds(column, DIM)]
        if member % BATCH == BATCH - 1:
            some = pl.ds(member + 1 - BATCH, BATCH)
            copy = pltpu.make_async_copy(
                staged.at[some], out.at[some], out_done.at[member // BATCH]
            )
            copy.start()
            sent.append(copy)
    for copy in sent:
        copy.wait()


def my_windows(win, info, order):
    fill_order(win, order)
    head = order[info[1] * PLACES + info[0]]
    return info[0] < USED, win[0, head] // 2 > 0, win[1, head] // 2 > 0


def lanes(column, width):
    return jnp.broadcast_to(column, (column.shape[0], width))


def side_by_side(parts, axis):
    return parts[0] if len(parts) == 1 else jnp.concatenate(parts, axis=axis)


def score(query, kv, keys):
    parts = [
        lax.dot_general(
            query, kv[some, :DIM], (((1,), (1,)), ((), ())), preferred_element_type=jnp.float32
        )
        for some in keys
    ]
    return side_by_side(parts, 1)


def fold(scores, kv, keys, rows, peak, total, first):
    copies = scores.shape[1] // DIM
    now = lanes(jnp.max(scores, axis=1, keepdims=True), DIM)
    if not first:
        before = peak[rows, :]
        now = jnp.maximum(before, now)
    weights = jnp.exp2((scores - jnp.concatenate([now] * copies, axis=1)) * EXP2_SCALE)
    values = side_by_side([kv[some, DIM : 2 * DIM] for some in keys], 0)
    with_ones = jnp.concatenate([values, jnp.ones_like(values)], axis=1)
    added = jnp.dot(weights.astype(jnp.bfloat16), with_ones, preferred_element_type=jnp.float32)
    peak[rows, :] = now
    if first:
        total[rows, :] = added
    else:
        fade = jnp.exp2((before - now) * EXP2_SCALE)
        total[rows, :] = total[rows, :] * jnp.concatenate([fade, fade], axis=1) + added


def visit(query, kv, frames, heights, peak, total, first=False):
    def chains(blocks, keys):
        ahead = score(query[blocks[0], :], kv, keys[0])
        for index, rows in enumerate(blocks):
            scores = ahead
            if index + 1 < len(blocks):
                ahead = score(query[blocks[index + 1], :], kv, keys[index + 1])
            fold(scores, kv, keys[index], rows, peak, total, first)

    def part(start, size, step):
        return pl.ds(pl.multiple_of(start, step), size)

    @pl.when(frames & heights)
    def _():
        def some(index, carry):
            blocks = [part(index * 512 + 256 * half, 256, 256) for half in range(2)]
            chains(blocks, [[pl.ds(0, 4 * TILE)]] * 2)
            return carry

        lax.fori_loop(0, 3, some, 0)

    @pl.when(frames != heights)
    def _():
        def some(index, carry):
            low = jnp.where(heights, 2 * index, index)
            starts = [low * TILE, (low + jnp.where(heights, 1, 2)) * TILE]
            keys = [part(start, TILE, TILE) for start in starts]
            blocks = [part(start + 192 * half, 192, 192) for start in starts for half in range(2)]
            chains(blocks, [keys] * 4)
            return carry

        lax.fori_loop(0, 2, some, 0)

    @pl.when(jnp.logical_not(frames | heights))
    def _():
        def some(index, carry):
            starts = [index * 2 * TILE, index * 2 * TILE + TILE]
            blocks = [part(start + 192 * half, 192, 192) for start in starts for half in range(2)]
            keys = [[part(start, TILE, TILE)] for start in starts for half in range(2)]
            chains(blocks, keys)
            return carry

        lax.fori_loop(0, 2, some, 0)


def own_column(win, info, qkv, peak, total, order):
    used, frames, heights = my_windows(win, info, order)
    query = qkv.at[:, 2 * DIM :]

    @pl.when(used)
    def _():
        visit(query, qkv, frames, heights, peak, total, first=True)


def next_columns(columns, win, info, qkv, lower, upper, peak_in, total_in, out, peak, total, order):
    used, frames, heights = my_windows(win, info, order)
    wide = info[1] == 0
    query = qkv.at[:, 2 * DIM :]

    @pl.when(used & jnp.logical_not(wide))
    def _():
        out[...] = (total_in[:, :DIM] / total_in[:, DIM:]).astype(jnp.bfloat16)

    @pl.when(used & wide)
    def _():
        peak[...] = peak_in[...]
        total[...] = total_in[...]

    @pl.when(used & wide & (info[2] > 0))
    def _():
        visit(query, lower, frames, heights, peak, total)

    @pl.when(used & wide & (info[2] < columns - 1))
    def _():
        visit(query, upper, frames, heights, peak, total)

    @pl.when(used & wide)
    def _():
        out[...] = (total[:, :DIM] / total[:, DIM:]).astype(jnp.bfloat16)


def unpack(win, received, out):
    wide = jnp.int32(0)
    for head in range(HEADS):
        is_wide = win[2, head] // 2
        place = jnp.where(is_wide > 0, wide, head - wide)
        member = place // 8 * 16 + (1 - is_wide) * 8 + place % 8
        out[:, head * DIM : (head + 1) * DIM] = received[member]
        wide = wide + is_wide


HBM = pl.BlockSpec(memory_space=pltpu.HBM)
SMEM = pl.BlockSpec(memory_space=pltpu.SMEM)
VMEM = pl.BlockSpec(memory_space=pltpu.VMEM)
ORDER = pltpu.SMEM((MEMBERS,), jnp.int32)


def call(kernel, shapes, scalars, operands, scratch=()):
    return pl.pallas_call(
        kernel,
        out_shape=shapes,
        in_specs=[SMEM] * len(scalars) + [VMEM] * len(operands),
        out_specs=jax.tree.map(lambda _: VMEM, shapes),
        scratch_shapes=list(scratch),
        compiler_params=PARAMS,
    )(*scalars, *operands)


def shards(queries, key_vectors, value_vectors, windows):
    tokens, width = queries.shape
    rows = MEMBERS * tokens
    columns = lax.axis_size("col")
    bf16, f32 = jnp.bfloat16, jnp.float32
    place = lax.axis_index("f") * 8 + lax.axis_index("uly")
    info = jnp.stack([place, lax.axis_index("g"), lax.axis_index("col")]).astype(jnp.int32)
    win = windows.T
    sources = [key_vectors, value_vectors, queries]
    count = len(sources)

    def pack_kernel(*refs):
        pack(count, *refs)

    def exchange(value):
        return lax.all_to_all(value, GROUP, split_axis=0, concat_axis=0, tiled=True)

    sendable = pl.pallas_call(
        pack_kernel,
        out_shape=jax.ShapeDtypeStruct((MEMBERS, tokens, count * DIM), bf16),
        in_specs=[HBM] * (1 + count),
        out_specs=HBM,
        scratch_shapes=[
            pltpu.SMEM(win.shape, jnp.int32),
            pltpu.VMEM((count, tokens, width), bf16),
            pltpu.VMEM((MEMBERS, tokens, count * DIM), bf16),
            ORDER,
            pltpu.SemaphoreType.DMA,
            pltpu.SemaphoreType.DMA((count, tokens // CHUNK)),
            pltpu.SemaphoreType.DMA((MEMBERS // BATCH,)),
        ],
        compiler_params=pltpu.CompilerParams(vmem_limit_bytes=PACK_VMEM),
    )(win, *sources)
    qkv = exchange(sendable).reshape(rows, count * DIM)

    sending = [
        ((uly * columns + col) * 2 + frame) * 2
        for uly in range(8)
        for col in range(columns - 1)
        for frame in range(2)
        if frame * 8 + uly < USED
    ]
    along = ("uly", "col", "f", "g")
    kv = qkv[:, : 2 * DIM]
    lower = lax.ppermute(kv, along, [(member, member + 4) for member in sending])
    upper = lax.ppermute(kv, along, [(member + 4, member) for member in sending])

    state = (jax.ShapeDtypeStruct((rows, DIM), f32), jax.ShapeDtypeStruct((rows, 2 * DIM), f32))
    peak, total = call(own_column, state, [win, info], [qkv], [ORDER])

    def next_kernel(*refs):
        next_columns(columns, *refs)

    result = call(
        next_kernel,
        jax.ShapeDtypeStruct((rows, DIM), bf16),
        [win, info],
        [qkv, lower, upper, peak, total],
        [pltpu.VMEM((rows, DIM), f32), pltpu.VMEM((rows, 2 * DIM), f32), ORDER],
    )
    back = exchange(result.reshape(MEMBERS, tokens, DIM))
    return call(unpack, jax.ShapeDtypeStruct((tokens, HEADS * DIM), bf16), [win], [back])


def solution(mesh):
    uly, blk, cfg = (mesh.shape[name] for name in ("uly", "blk", "cfg"))
    fine = Mesh(mesh.devices.reshape(uly, blk // 4, 2, 2, cfg), ("uly", "col", "f", "g", "cfg"))
    tokens = P(("cfg", "col", "f", "g", "uly"), None)
    return jax.shard_map(
        shards,
        mesh=fine,
        in_specs=(tokens, tokens, tokens, P()),
        out_specs=tokens,
        check_vma=False,
    )
```

```python
import jax
import jax.numpy as jnp
from jax import lax
from jax.experimental import pallas as pl
from jax.experimental.pallas import tpu as pltpu
from jax.sharding import Mesh
from jax.sharding import PartitionSpec as P

HEADS = 24
DIM = 128
TILE = 384
PLACES = 16
USED = 12
MEMBERS = 2 * PLACES
CHUNK = 16
BATCH = 4
PACK_VMEM = 62 * 1024 * 1024
GROUP = ("f", "g", "uly")
EXP2_SCALE = DIM**-0.5 * 1.4426950408889634
PARAMS = pltpu.CompilerParams(vmem_limit_bytes=32 * 1024 * 1024)


def fill_order(win, order):
    for place in range(MEMBERS):
        order[place] = 0

    def put(head, wide):
        is_wide = win[2, head] // 2
        order[jnp.where(is_wide > 0, wide, PLACES + head - wide)] = head
        return wide + is_wide

    lax.fori_loop(0, HEADS, put, jnp.int32(0))


def home(member):
    return member // 8 % 2, member // 16 * 8 + member % 8


def head_columns(order, row, place):
    return pl.ds(pl.multiple_of(order[row * PLACES + place] * DIM, DIM), DIM)


def pack(count, win_hbm, *refs):
    sources = refs[:count]
    out, win, held, staged, order, win_done, done, out_done = refs[-8:]
    first = pltpu.make_async_copy(win_hbm, win, win_done)
    first.start()
    copies = []
    for part, source in enumerate(sources):
        for chunk in range(source.shape[0] // CHUNK):
            rows = pl.ds(chunk * CHUNK, CHUNK)
            copy = pltpu.make_async_copy(
                source.at[rows, :], held.at[part, rows, :], done.at[part, chunk]
            )
            copy.start()
            copies.append(copy)
    first.wait()
    fill_order(win, order)
    for copy in copies:
        copy.wait()
    sent = []
    for member in range(MEMBERS):
        columns = head_columns(order, *home(member))
        for part in range(count):
            staged[member, :, part * DIM : (part + 1) * DIM] = held[part, :, columns]
        if member % BATCH == BATCH - 1:
            some = pl.ds(member + 1 - BATCH, BATCH)
            copy = pltpu.make_async_copy(
                staged.at[some], out.at[some], out_done.at[member // BATCH]
            )
            copy.start()
            sent.append(copy)
    for copy in sent:
        copy.wait()


def pack_wide(win, values, out, order):
    fill_order(win, order)
    for place in range(USED):
        out[:, place * DIM : (place + 1) * DIM] = values[:, head_columns(order, 0, place)]


def pack_values(win, values, lower, upper, out, order):
    fill_order(win, order)
    for member in range(MEMBERS):
        row, place = home(member)
        own = values[:, head_columns(order, row, place)]
        out[member, :, :DIM] = own
        for part, source in ((1, lower), (2, upper)):
            there = row == 0 and place < USED
            block = source[:, place * DIM : (place + 1) * DIM] if there else own
            out[member, :, part * DIM : (part + 1) * DIM] = block


def my_windows(win, info, order):
    fill_order(win, order)
    head = order[info[1] * PLACES + info[0]]
    return info[0] < USED, win[0, head] // 2 > 0, win[1, head] // 2 > 0


def lanes(column, width):
    return jnp.broadcast_to(column, (column.shape[0], width))


def side_by_side(parts, axis):
    return parts[0] if len(parts) == 1 else jnp.concatenate(parts, axis=axis)


def score(query, key, keys):
    parts = [
        lax.dot_general(
            query, key[some, :], (((1,), (1,)), ((), ())), preferred_element_type=jnp.float32
        )
        for some in keys
    ]
    return side_by_side(parts, 1)


def visit(frames, heights, run):
    def part(start, size, step):
        return pl.ds(pl.multiple_of(start, step), size)

    @pl.when(frames & heights)
    def _():
        def some(index, carry):
            keys = [pl.ds(0, 4 * TILE)]
            run([(part(index * 512 + 256 * half, 256, 256), keys) for half in range(2)])
            return carry

        lax.fori_loop(0, 3, some, 0)

    @pl.when(frames != heights)
    def _():
        def some(index, carry):
            low = jnp.where(heights, 2 * index, index)
            starts = [low * TILE, (low + jnp.where(heights, 1, 2)) * TILE]
            keys = [part(start, TILE, DIM) for start in starts]
            run([(part(at + 192 * half, 192, 192), keys) for at in starts for half in range(2)])
            return carry

        lax.fori_loop(0, 2, some, 0)

    @pl.when(jnp.logical_not(frames | heights))
    def _():
        def some(index, carry):
            starts = [index * 2 * TILE, index * 2 * TILE + TILE]
            run(
                [
                    (part(at + 192 * half, 192, 192), [part(at, TILE, DIM)])
                    for at in starts
                    for half in range(2)
                ]
            )
            return carry

        lax.fori_loop(0, 2, some, 0)


def weigh(query, key, frames, heights, peak, before, weights, fade):
    def run(blocks):
        ahead = score(query[blocks[0][0], :], key, blocks[0][1])
        for index, (rows, keys) in enumerate(blocks):
            scores = ahead
            if index + 1 < len(blocks):
                ahead = score(query[blocks[index + 1][0], :], key, blocks[index + 1][1])
            now = lanes(jnp.max(scores, axis=1, keepdims=True), DIM)
            if before is not None:
                was = before[rows, :]
                now = jnp.maximum(was, now)
                fade[rows, :] = jnp.exp2((was - now) * EXP2_SCALE)
            peak[rows, :] = now
            wide_peak = jnp.concatenate([now] * (scores.shape[1] // DIM), axis=1)
            result = jnp.exp2((scores - wide_peak) * EXP2_SCALE).astype(jnp.bfloat16)
            for number, some in enumerate(keys):
                size = scores.shape[1] // len(keys)
                weights[rows, some] = result[:, number * size : (number + 1) * size]

    visit(frames, heights, run)


def gather(weights, values, column, frames, heights, total, fade):
    def run(blocks):
        for rows, keys in blocks:
            here = side_by_side([weights[rows, some] for some in keys], 1)
            value = side_by_side([values[some, column * DIM : (column + 1) * DIM] for some in keys], 0)
            with_ones = jnp.concatenate([value, jnp.ones_like(value)], axis=1)
            added = jnp.dot(here, with_ones, preferred_element_type=jnp.float32)
            if fade is None:
                total[rows, :] = added
            else:
                scale = fade[rows, :]
                total[rows, :] = total[rows, :] * jnp.concatenate([scale, scale], axis=1) + added

    visit(frames, heights, run)


def own_weights(win, info, qk, weights, peak, order):
    used, frames, heights = my_windows(win, info, order)

    @pl.when(used)
    def _():
        query, key = qk.at[:, DIM:], qk.at[:, :DIM]
        weigh(query, key, frames, heights, peak, None, weights, None)


def sides(columns, info, used):
    wide = used & (info[1] == 0)
    return wide & (info[2] > 0), wide & (info[2] < columns - 1)


def next_weights(columns, win, info, qk, lower, upper, before, *refs):
    low_weights, up_weights, low_fade, up_fade, peak, order = refs
    used, frames, heights = my_windows(win, info, order)
    below, above = sides(columns, info, used)
    query = qk.at[:, DIM:]

    @pl.when(below)
    def _():
        weigh(query, lower, frames, heights, peak, before, low_weights, low_fade)

    @pl.when(jnp.logical_not(below))
    def _():
        peak[...] = before[...]

    @pl.when(above)
    def _():
        weigh(query, upper, frames, heights, peak, peak, up_weights, up_fade)


def attend(columns, win, info, values, weights, low_weights, up_weights, low_fade, up_fade, *refs):
    out, total, order = refs
    used, frames, heights = my_windows(win, info, order)
    below, above = sides(columns, info, used)

    @pl.when(used)
    def _():
        gather(weights, values, 0, frames, heights, total, None)

    @pl.when(below)
    def _():
        gather(low_weights, values, 1, frames, heights, total, low_fade)

    @pl.when(above)
    def _():
        gather(up_weights, values, 2, frames, heights, total, up_fade)

    @pl.when(used)
    def _():
        out[...] = (total[:, :DIM] / total[:, DIM:]).astype(jnp.bfloat16)


def unpack(win, received, out):
    wide = jnp.int32(0)
    for head in range(HEADS):
        is_wide = win[2, head] // 2
        place = jnp.where(is_wide > 0, wide, head - wide)
        member = place // 8 * 16 + (1 - is_wide) * 8 + place % 8
        out[:, head * DIM : (head + 1) * DIM] = received[member]
        wide = wide + is_wide


HBM = pl.BlockSpec(memory_space=pltpu.HBM)
SMEM = pl.BlockSpec(memory_space=pltpu.SMEM)
VMEM = pl.BlockSpec(memory_space=pltpu.VMEM)
ORDER = pltpu.SMEM((MEMBERS,), jnp.int32)


def call(kernel, shapes, scalars, operands, scratch=(), after=()):
    def body(*refs):
        given = len(scalars) + len(operands)
        kernel(*refs[:given], *refs[given + len(after) :])

    return pl.pallas_call(
        body,
        out_shape=shapes,
        in_specs=[SMEM] * len(scalars) + [VMEM] * len(operands) + [HBM] * len(after),
        out_specs=jax.tree.map(lambda _: VMEM, shapes),
        scratch_shapes=list(scratch),
        compiler_params=PARAMS,
    )(*scalars, *operands, *after)


def shards(queries, key_vectors, value_vectors, windows):
    tokens, width = queries.shape
    rows = MEMBERS * tokens
    columns = lax.axis_size("col")
    bf16, f32 = jnp.bfloat16, jnp.float32
    place = lax.axis_index("f") * 8 + lax.axis_index("uly")
    info = jnp.stack([place, lax.axis_index("g"), lax.axis_index("col")]).astype(jnp.int32)
    win = windows.T
    sources = [key_vectors, queries]
    count = len(sources)

    def pack_kernel(*refs):
        pack(count, *refs)

    def exchange(value):
        return lax.all_to_all(value, GROUP, split_axis=0, concat_axis=0, tiled=True)

    def shape(*sizes, dtype=bf16):
        return jax.ShapeDtypeStruct(sizes, dtype)

    sendable = pl.pallas_call(
        pack_kernel,
        out_shape=shape(MEMBERS, tokens, count * DIM),
        in_specs=[HBM] * (1 + count),
        out_specs=HBM,
        scratch_shapes=[
            pltpu.SMEM(win.shape, jnp.int32),
            pltpu.VMEM((count, tokens, width), bf16),
            pltpu.VMEM((MEMBERS, tokens, count * DIM), bf16),
            ORDER,
            pltpu.SemaphoreType.DMA,
            pltpu.SemaphoreType.DMA((count, tokens // CHUNK)),
            pltpu.SemaphoreType.DMA((MEMBERS // BATCH,)),
        ],
        compiler_params=pltpu.CompilerParams(vmem_limit_bytes=PACK_VMEM),
    )(win, *sources)
    qk = exchange(sendable)

    up = [(col, col + 1) for col in range(columns - 1)]
    down = [(after, before) for before, after in up]
    wide_values = call(
        pack_wide, shape(tokens, USED * DIM), [win], [value_vectors], [ORDER], [sendable]
    )
    low_values = lax.ppermute(wide_values, "col", up)
    up_values = lax.ppermute(wide_values, "col", down)
    values_out = call(
        pack_values,
        shape(MEMBERS, tokens, 3 * DIM),
        [win],
        [value_vectors, low_values, up_values],
        [ORDER],
    )
    qk, values_out = lax.optimization_barrier((qk, values_out))
    qk = qk.reshape(rows, count * DIM)
    values = exchange(values_out).reshape(rows, 3 * DIM)

    sending = [
        ((uly * columns + col) * 2 + frame) * 2
        for uly in range(8)
        for col in range(columns - 1)
        for frame in range(2)
        if frame * 8 + uly < USED
    ]
    along = ("uly", "col", "f", "g")
    key = qk[:, :DIM]
    lower = lax.ppermute(key, along, [(member, member + 4) for member in sending])
    upper = lax.ppermute(key, along, [(member + 4, member) for member in sending])

    weight, scale = shape(rows, rows), shape(rows, DIM, dtype=f32)
    weights, peak = call(own_weights, (weight, scale), [win, info], [qk], [ORDER])

    def next_kernel(*refs):
        next_weights(columns, *refs)

    def attend_kernel(*refs):
        attend(columns, *refs)

    beside = call(
        next_kernel,
        (weight, weight, scale, scale),
        [win, info],
        [qk, lower, upper, peak],
        [pltpu.VMEM((rows, DIM), f32), ORDER],
    )
    result = call(
        attend_kernel,
        shape(rows, DIM),
        [win, info],
        [values, weights, *beside],
        [pltpu.VMEM((rows, 2 * DIM), f32), ORDER],
    )
    back = exchange(result.reshape(MEMBERS, tokens, DIM))
    return call(unpack, jax.ShapeDtypeStruct((tokens, HEADS * DIM), bf16), [win], [back])


def solution(mesh):
    uly, blk, cfg = (mesh.shape[name] for name in ("uly", "blk", "cfg"))
    fine = Mesh(mesh.devices.reshape(uly, blk // 4, 2, 2, cfg), ("uly", "col", "f", "g", "cfg"))
    tokens = P(("cfg", "col", "f", "g", "uly"), None)
    return jax.shard_map(
        shards,
        mesh=fine,
        in_specs=(tokens, tokens, tokens, P()),
        out_specs=tokens,
        check_vma=False,
    )
```

```python
import jax
import jax.numpy as jnp
from jax import lax
from jax.experimental import pallas as pl
from jax.experimental.pallas import tpu as pltpu
from jax.sharding import Mesh
from jax.sharding import PartitionSpec as P

HEADS = 24
DIM = 128
TILE = 384
PLACES = 16
USED = 12
MEMBERS = 2 * PLACES
CHUNK = 16
BATCH = 4
PACK_VMEM = 62 * 1024 * 1024
GROUP = ("f", "g", "uly")
EXP2_SCALE = DIM**-0.5 * 1.4426950408889634
PARAMS = pltpu.CompilerParams(vmem_limit_bytes=32 * 1024 * 1024)


def fill_order(win, order):
    for place in range(MEMBERS):
        order[place] = 0

    def put(head, wide):
        is_wide = win[2, head] // 2
        order[jnp.where(is_wide > 0, wide, PLACES + head - wide)] = head
        return wide + is_wide

    lax.fori_loop(0, HEADS, put, jnp.int32(0))


def pack(count, win_hbm, *refs):
    sources = refs[:count]
    out, win, held, staged, order, win_done, done, out_done = refs[-8:]
    first = pltpu.make_async_copy(win_hbm, win, win_done)
    first.start()
    copies = []
    for part, source in enumerate(sources):
        for chunk in range(source.shape[0] // CHUNK):
            rows = pl.ds(chunk * CHUNK, CHUNK)
            copy = pltpu.make_async_copy(
                source.at[rows, :], held.at[part, rows, :], done.at[part, chunk]
            )
            copy.start()
            copies.append(copy)
    first.wait()
    fill_order(win, order)
    for copy in copies:
        copy.wait()
    sent = []
    for member in range(MEMBERS):
        frame, row, uly = member // 16, member // 8 % 2, member % 8
        column = pl.multiple_of(order[row * PLACES + frame * 8 + uly] * DIM, DIM)
        for part in range(count):
            staged[member, :, part * DIM : (part + 1) * DIM] = held[part, :, pl.ds(column, DIM)]
        if member % BATCH == BATCH - 1:
            some = pl.ds(member + 1 - BATCH, BATCH)
            copy = pltpu.make_async_copy(
                staged.at[some], out.at[some], out_done.at[member // BATCH]
            )
            copy.start()
            sent.append(copy)
    for copy in sent:
        copy.wait()


def my_windows(win, info, order):
    fill_order(win, order)
    head = order[info[1] * PLACES + info[0]]
    return info[0] < USED, win[0, head] // 2 > 0, win[1, head] // 2 > 0


def lanes(column, width):
    return jnp.broadcast_to(column, (column.shape[0], width))


def side_by_side(parts, axis):
    return parts[0] if len(parts) == 1 else jnp.concatenate(parts, axis=axis)


def score(query, kv, keys):
    parts = [
        lax.dot_general(
            query, kv[some, :DIM], (((1,), (1,)), ((), ())), preferred_element_type=jnp.float32
        )
        for some in keys
    ]
    return side_by_side(parts, 1)


def fold(scores, kv, keys, rows, peak, total, first):
    copies = scores.shape[1] // DIM
    now = lanes(jnp.max(scores, axis=1, keepdims=True), DIM)
    if not first:
        before = peak[rows, :]
        now = jnp.maximum(before, now)
    weights = jnp.exp2((scores - jnp.concatenate([now] * copies, axis=1)) * EXP2_SCALE)
    values = side_by_side([kv[some, DIM : 2 * DIM] for some in keys], 0)
    with_ones = jnp.concatenate([values, jnp.ones_like(values)], axis=1)
    added = jnp.dot(weights.astype(jnp.bfloat16), with_ones, preferred_element_type=jnp.float32)
    peak[rows, :] = now
    if first:
        total[rows, :] = added
    else:
        fade = jnp.exp2((before - now) * EXP2_SCALE)
        total[rows, :] = total[rows, :] * jnp.concatenate([fade, fade], axis=1) + added


def visit(query, kv, frames, heights, peak, total, first=False):
    def chains(blocks, keys):
        ahead = score(query[blocks[0], :], kv, keys[0])
        for index, rows in enumerate(blocks):
            scores = ahead
            if index + 1 < len(blocks):
                ahead = score(query[blocks[index + 1], :], kv, keys[index + 1])
            fold(scores, kv, keys[index], rows, peak, total, first)

    def part(start, size, step):
        return pl.ds(pl.multiple_of(start, step), size)

    @pl.when(frames & heights)
    def _():
        every = [pl.ds(0, 4 * TILE)]
        chains([pl.ds(512 * block, 512) for block in range(3)], [every] * 3)

    @pl.when(frames != heights)
    def _():
        blocks, keys = [], []
        for index in range(2):
            low = jnp.where(heights, 2 * index, index)
            pair = [low * TILE, (low + jnp.where(heights, 1, 2)) * TILE]
            pair = [part(start, TILE, TILE) for start in pair]
            blocks += pair
            keys += [pair, pair]
        chains(blocks, keys)

    @pl.when(jnp.logical_not(frames | heights))
    def _():
        tiles = [pl.ds(tile * TILE, TILE) for tile in range(4)]
        chains(tiles, [[tile] for tile in tiles])


def own_column(win, info, qkv, peak, total, order):
    used, frames, heights = my_windows(win, info, order)
    query = qkv.at[:, 2 * DIM :]

    @pl.when(used)
    def _():
        visit(query, qkv, frames, heights, peak, total, first=True)


def next_columns(columns, win, info, qkv, lower, upper, peak_in, total_in, out, peak, total, order):
    used, frames, heights = my_windows(win, info, order)
    wide = info[1] == 0
    query = qkv.at[:, 2 * DIM :]

    @pl.when(used & jnp.logical_not(wide))
    def _():
        out[...] = (total_in[:, :DIM] / total_in[:, DIM:]).astype(jnp.bfloat16)

    @pl.when(used & wide)
    def _():
        peak[...] = peak_in[...]
        total[...] = total_in[...]

    @pl.when(used & wide & (info[2] > 0))
    def _():
        visit(query, lower, frames, heights, peak, total)

    @pl.when(used & wide & (info[2] < columns - 1))
    def _():
        visit(query, upper, frames, heights, peak, total)

    @pl.when(used & wide)
    def _():
        out[...] = (total[:, :DIM] / total[:, DIM:]).astype(jnp.bfloat16)


def unpack(win, received, out):
    wide = jnp.int32(0)
    for head in range(HEADS):
        is_wide = win[2, head] // 2
        place = jnp.where(is_wide > 0, wide, head - wide)
        member = place // 8 * 16 + (1 - is_wide) * 8 + place % 8
        out[:, head * DIM : (head + 1) * DIM] = received[member]
        wide = wide + is_wide


HBM = pl.BlockSpec(memory_space=pltpu.HBM)
SMEM = pl.BlockSpec(memory_space=pltpu.SMEM)
VMEM = pl.BlockSpec(memory_space=pltpu.VMEM)
ORDER = pltpu.SMEM((MEMBERS,), jnp.int32)


def call(kernel, shapes, scalars, operands, scratch=()):
    return pl.pallas_call(
        kernel,
        out_shape=shapes,
        in_specs=[SMEM] * len(scalars) + [VMEM] * len(operands),
        out_specs=jax.tree.map(lambda _: VMEM, shapes),
        scratch_shapes=list(scratch),
        compiler_params=PARAMS,
    )(*scalars, *operands)


def shards(queries, key_vectors, value_vectors, windows):
    tokens, width = queries.shape
    rows = MEMBERS * tokens
    columns = lax.axis_size("col")
    bf16, f32 = jnp.bfloat16, jnp.float32
    place = lax.axis_index("f") * 8 + lax.axis_index("uly")
    info = jnp.stack([place, lax.axis_index("g"), lax.axis_index("col")]).astype(jnp.int32)
    win = windows.T
    sources = [key_vectors, value_vectors, queries]
    count = len(sources)

    def pack_kernel(*refs):
        pack(count, *refs)

    def exchange(value):
        return lax.all_to_all(value, GROUP, split_axis=0, concat_axis=0, tiled=True)

    sendable = pl.pallas_call(
        pack_kernel,
        out_shape=jax.ShapeDtypeStruct((MEMBERS, tokens, count * DIM), bf16),
        in_specs=[HBM] * (1 + count),
        out_specs=HBM,
        scratch_shapes=[
            pltpu.SMEM(win.shape, jnp.int32),
            pltpu.VMEM((count, tokens, width), bf16),
            pltpu.VMEM((MEMBERS, tokens, count * DIM), bf16),
            ORDER,
            pltpu.SemaphoreType.DMA,
            pltpu.SemaphoreType.DMA((count, tokens // CHUNK)),
            pltpu.SemaphoreType.DMA((MEMBERS // BATCH,)),
        ],
        compiler_params=pltpu.CompilerParams(vmem_limit_bytes=PACK_VMEM),
    )(win, *sources)
    qkv = exchange(sendable).reshape(rows, count * DIM)

    sending = [
        ((uly * columns + col) * 2 + frame) * 2
        for uly in range(8)
        for col in range(columns - 1)
        for frame in range(2)
        if frame * 8 + uly < USED
    ]
    along = ("uly", "col", "f", "g")
    kv = qkv[:, : 2 * DIM]
    lower = lax.ppermute(kv, along, [(member, member + 4) for member in sending])
    upper = lax.ppermute(kv, along, [(member + 4, member) for member in sending])

    state = (jax.ShapeDtypeStruct((rows, DIM), f32), jax.ShapeDtypeStruct((rows, 2 * DIM), f32))
    peak, total = call(own_column, state, [win, info], [qkv], [ORDER])

    def next_kernel(*refs):
        next_columns(columns, *refs)

    result = call(
        next_kernel,
        jax.ShapeDtypeStruct((rows, DIM), bf16),
        [win, info],
        [qkv, lower, upper, peak, total],
        [pltpu.VMEM((rows, DIM), f32), pltpu.VMEM((rows, 2 * DIM), f32), ORDER],
    )
    back = exchange(result.reshape(MEMBERS, tokens, DIM))
    return call(unpack, jax.ShapeDtypeStruct((tokens, HEADS * DIM), bf16), [win], [back])


def solution(mesh):
    uly, blk, cfg = (mesh.shape[name] for name in ("uly", "blk", "cfg"))
    fine = Mesh(mesh.devices.reshape(uly, blk // 4, 2, 2, cfg), ("uly", "col", "f", "g", "cfg"))
    tokens = P(("cfg", "col", "f", "g", "uly"), None)
    return jax.shard_map(
        shards,
        mesh=fine,
        in_specs=(tokens, tokens, tokens, P()),
        out_specs=tokens,
        check_vma=False,
    )
```

```python
import jax
import jax.numpy as jnp
from jax import lax
from jax.experimental import pallas as pl
from jax.experimental.pallas import tpu as pltpu
from jax.sharding import Mesh
from jax.sharding import PartitionSpec as P

HEADS = 24
DIM = 128
TILE = 384
PLACES = 16
USED = 12
WHOLE = 8
MEMBERS = 2 * PLACES
CHUNK = 16
BATCH = 4
PACK_VMEM = 62 * 1024 * 1024
GROUP = ("f", "g", "uly")
EXP2_SCALE = DIM**-0.5 * 1.4426950408889634
PARAMS = pltpu.CompilerParams(vmem_limit_bytes=32 * 1024 * 1024)


def is_open(win, axis, head):
    return win[axis, head] // 2


def fill_order(win, order):
    for place in range(2 * PLACES):
        order[place] = 0

    def put(head, carry):
        joined, apart = carry
        wide = is_open(win, 2, head)
        both = wide * is_open(win, 0, head) * is_open(win, 1, head)
        place = jnp.where(both > 0, joined, USED - 1 - apart)
        order[jnp.where(wide > 0, place, PLACES + head - joined - apart)] = head
        return joined + both, apart + wide - both

    joined, _ = lax.fori_loop(0, HEADS, put, (jnp.int32(0), jnp.int32(0)))
    for place in range(WHOLE, USED):
        order[place + USED - WHOLE] = order[place]
    return joined


def pack(count, win_hbm, *refs):
    sources = refs[:count]
    out, win, held, staged, order, win_done, done, out_done = refs[-8:]
    first = pltpu.make_async_copy(win_hbm, win, win_done)
    first.start()
    copies = []
    for part, source in enumerate(sources):
        for chunk in range(source.shape[0] // CHUNK):
            rows = pl.ds(chunk * CHUNK, CHUNK)
            copy = pltpu.make_async_copy(
                source.at[rows, :], held.at[part, rows, :], done.at[part, chunk]
            )
            copy.start()
            copies.append(copy)
    first.wait()
    fill_order(win, order)
    for copy in copies:
        copy.wait()
    sent = []
    for member in range(MEMBERS):
        frame, row, uly = member // 16, member // 8 % 2, member % 8
        column = pl.multiple_of(order[row * PLACES + frame * 8 + uly] * DIM, DIM)
        for part in range(count):
            staged[member, :, part * DIM : (part + 1) * DIM] = held[part, :, pl.ds(column, DIM)]
        if member % BATCH == BATCH - 1:
            some = pl.ds(member + 1 - BATCH, BATCH)
            copy = pltpu.make_async_copy(
                staged.at[some], out.at[some], out_done.at[member // BATCH]
            )
            copy.start()
            sent.append(copy)
    for copy in sent:
        copy.wait()


class Mine:
    def __init__(self, win, info, order):
        joined = fill_order(win, order)
        place, row = info[0], info[1]
        head = order[row * PLACES + place]
        self.frames = is_open(win, 0, head) > 0
        self.heights = is_open(win, 1, head) > 0
        self.wide = row == 0
        self.split = self.wide & (place >= WHOLE) & (joined <= WHOLE)
        self.whole = jnp.logical_not(self.wide & (place >= WHOLE))
        self.used = (place < USED) | self.split
        self.half = jnp.where(self.split & (place >= USED), 1, 0)
        self.lo = jnp.where(self.split, self.half, 0)
        self.hi = jnp.where(self.split, self.half + 1, 2)

    def pair(self, index):
        by_row = self.frames & jnp.logical_not(self.heights)
        first = jnp.where(by_row, index, 2 * index)
        return first, first + jnp.where(by_row, 2, 1)

    def half_tiles(self):
        first, second = self.pair(self.half)
        return jnp.where(self.split, first, 0), jnp.where(self.split, second, 1)


def lanes(column, width):
    return jnp.broadcast_to(column, (column.shape[0], width))


def side_by_side(parts, axis):
    return parts[0] if len(parts) == 1 else jnp.concatenate(parts, axis=axis)


def score(query, kv, keys):
    parts = [
        lax.dot_general(
            query, kv[some, :DIM], (((1,), (1,)), ((), ())), preferred_element_type=jnp.float32
        )
        for some in keys
    ]
    return side_by_side(parts, 1)


def fold(scores, kv, keys, rows, peak, total, first):
    copies = scores.shape[1] // DIM
    now = lanes(jnp.max(scores, axis=1, keepdims=True), DIM)
    if not first:
        before = peak[rows, :]
        now = jnp.maximum(before, now)
    weights = jnp.exp2((scores - jnp.concatenate([now] * copies, axis=1)) * EXP2_SCALE)
    values = side_by_side([kv[some, DIM : 2 * DIM] for some in keys], 0)
    with_ones = jnp.concatenate([values, jnp.ones_like(values)], axis=1)
    added = jnp.dot(weights.astype(jnp.bfloat16), with_ones, preferred_element_type=jnp.float32)
    peak[rows, :] = now
    if first:
        total[rows, :] = added
    else:
        fade = jnp.exp2((before - now) * EXP2_SCALE)
        total[rows, :] = total[rows, :] * jnp.concatenate([fade, fade], axis=1) + added


def tile_rows(tile):
    return pl.ds(pl.multiple_of(tile * TILE, TILE), TILE)


def visit(query, kv, mine, peak, total, first=False):
    def chains(blocks, keys):
        ahead = score(query[blocks[0], :], kv, keys[0])
        for index, rows in enumerate(blocks):
            scores = ahead
            if index + 1 < len(blocks):
                ahead = score(query[blocks[index + 1], :], kv, keys[index + 1])
            fold(scores, kv, keys[index], rows, peak, total, first)

    @pl.when(mine.frames & mine.heights)
    def _():
        every = [pl.ds(0, 4 * TILE)]
        chains([pl.ds(512 * block, 512) for block in range(3)], [every] * 3)

    @pl.when(mine.frames != mine.heights)
    def _():
        def some(index, carry):
            tiles = [tile_rows(tile) for tile in mine.pair(index)]
            chains(tiles, [tiles] * 2)
            return carry

        lax.fori_loop(mine.lo, mine.hi, some, 0)

    @pl.when(jnp.logical_not(mine.frames | mine.heights))
    def _():
        def some(index, carry):
            tiles = [tile_rows(tile) for tile in mine.pair(index)]
            chains(tiles, [[tile] for tile in tiles])
            return carry

        lax.fori_loop(mine.lo, mine.hi, some, 0)


def sendable_rows(win, info, qkv, every, half, order):
    mine = Mine(win, info, order)
    first, second = mine.half_tiles()
    every[...] = qkv[:, : 2 * DIM]
    half[:TILE, :] = qkv[tile_rows(first), : 2 * DIM]
    half[TILE:, :] = qkv[tile_rows(second), : 2 * DIM]


def own_column(win, info, qkv, peak, total, order):
    mine = Mine(win, info, order)
    query = qkv.at[:, 2 * DIM :]

    @pl.when(mine.used)
    def _():
        visit(query, qkv, mine, peak, total, first=True)


def next_columns(columns, win, info, qkv, lower, upper, peak_in, total_in, out, *scratch):
    kv, peak, total, order = scratch
    mine = Mine(win, info, order)
    query = qkv.at[:, 2 * DIM :]
    sending = mine.used & mine.wide
    first, second = mine.half_tiles()

    @pl.when(mine.used & jnp.logical_not(mine.wide))
    def _():
        out[...] = (total_in[:, :DIM] / total_in[:, DIM:]).astype(jnp.bfloat16)

    @pl.when(sending)
    def _():
        peak[...] = peak_in[...]
        total[...] = total_in[...]

    for (every, half, rest), there in ((lower, info[2] > 0), (upper, info[2] < columns - 1)):

        @pl.when(sending & there)
        def _(every=every, half=half, rest=rest):
            @pl.when(mine.whole)
            def _():
                kv[...] = every[...]

            @pl.when(jnp.logical_not(mine.whole | mine.split))
            def _():
                kv[2 * TILE :, :] = rest[...]

            @pl.when(jnp.logical_not(mine.whole))
            def _():
                kv[tile_rows(first), :] = half[:TILE, :]
                kv[tile_rows(second), :] = half[TILE:, :]

            visit(query, kv, mine, peak, total)

    @pl.when(sending)
    def _():
        out[...] = (total[:, :DIM] / total[:, DIM:]).astype(jnp.bfloat16)


def unpack(win, info, received, out):
    joined = jnp.int32(0)
    for head in range(HEADS):
        joined = joined + is_open(win, 0, head) * is_open(win, 1, head) * is_open(win, 2, head)
    split = joined <= WHOLE
    joined, apart = jnp.int32(0), jnp.int32(0)
    for head in range(HEADS):
        frames, heights, wide = (is_open(win, axis, head) for axis in range(3))
        both = wide * frames * heights
        place = jnp.where(both > 0, joined, USED - 1 - apart)
        half = jnp.where((frames > 0) & (heights == 0), info[1], info[3])
        place = jnp.where(split & (place >= WHOLE), place + (USED - WHOLE) * half, place)
        place = jnp.where(wide > 0, place, head - joined - apart)
        member = place // 8 * 16 + (1 - wide) * 8 + place % 8
        out[:, head * DIM : (head + 1) * DIM] = received[member]
        joined, apart = joined + both, apart + wide - both


HBM = pl.BlockSpec(memory_space=pltpu.HBM)
SMEM = pl.BlockSpec(memory_space=pltpu.SMEM)
VMEM = pl.BlockSpec(memory_space=pltpu.VMEM)
ORDER = pltpu.SMEM((MEMBERS,), jnp.int32)


def call(kernel, shapes, scalars, operands, scratch=()):
    return pl.pallas_call(
        kernel,
        out_shape=shapes,
        in_specs=[SMEM] * len(scalars) + [VMEM] * len(operands),
        out_specs=jax.tree.map(lambda _: VMEM, shapes),
        scratch_shapes=list(scratch),
        compiler_params=PARAMS,
    )(*scalars, *operands)


def shards(queries, key_vectors, value_vectors, windows):
    tokens, width = queries.shape
    rows = MEMBERS * tokens
    columns = lax.axis_size("col")
    bf16, f32 = jnp.bfloat16, jnp.float32
    place = lax.axis_index("f") * 8 + lax.axis_index("uly")
    info = jnp.stack(
        [place, lax.axis_index("g"), lax.axis_index("col"), lax.axis_index("f")]
    ).astype(jnp.int32)
    win = windows.T
    sources = [key_vectors, value_vectors, queries]
    count = len(sources)

    def pack_kernel(*refs):
        pack(count, *refs)

    def exchange(value):
        return lax.all_to_all(value, GROUP, split_axis=0, concat_axis=0, tiled=True)

    sendable = pl.pallas_call(
        pack_kernel,
        out_shape=jax.ShapeDtypeStruct((MEMBERS, tokens, count * DIM), bf16),
        in_specs=[HBM] * (1 + count),
        out_specs=HBM,
        scratch_shapes=[
            pltpu.SMEM(win.shape, jnp.int32),
            pltpu.VMEM((count, tokens, width), bf16),
            pltpu.VMEM((MEMBERS, tokens, count * DIM), bf16),
            ORDER,
            pltpu.SemaphoreType.DMA,
            pltpu.SemaphoreType.DMA((count, tokens // CHUNK)),
            pltpu.SemaphoreType.DMA((MEMBERS // BATCH,)),
        ],
        compiler_params=pltpu.CompilerParams(vmem_limit_bytes=PACK_VMEM),
    )(win, *sources)
    qkv = exchange(sendable).reshape(rows, count * DIM)

    kv, half = call(
        sendable_rows,
        (jax.ShapeDtypeStruct((rows, 2 * DIM), bf16), jax.ShapeDtypeStruct((rows // 2, 2 * DIM), bf16)),
        [win, info],
        [qkv],
        [ORDER],
    )

    def beside(value, frame):
        up = [
            (((uly * columns + col) * 2 + frame) * 2, ((uly * columns + col + 1) * 2 + frame) * 2)
            for uly in range(8)
            for col in range(columns - 1)
        ]
        along = ("uly", "col", "f", "g")
        return lax.ppermute(value, along, up), lax.ppermute(value, along, [(b, a) for a, b in up])

    lower, upper = beside(kv, 0)
    low_half, up_half = beside(half, 1)

    column = lax.axis_index("col")

    def send_rest(kv):
        rest = kv[rows // 2 :]
        near = jnp.abs(jnp.arange(columns) - column) == 1
        sent = jnp.where(near[:, None, None], rest[None], jnp.zeros_like(rest)[None])
        got = lax.all_to_all(sent, "col", split_axis=0, concat_axis=0, tiled=True)
        return tuple(
            lax.dynamic_index_in_dim(got, jnp.clip(at, 0, columns - 1), 0, keepdims=False)
            for at in (column - 1, column + 1)
        )

    def no_rest(kv):
        return (jnp.zeros((rows // 2, 2 * DIM), bf16),) * 2

    low_rest, up_rest = lax.cond(
        jnp.sum(jnp.prod(windows // 2, axis=1)) > WHOLE, send_rest, no_rest, kv
    )

    state = (jax.ShapeDtypeStruct((rows, DIM), f32), jax.ShapeDtypeStruct((rows, 2 * DIM), f32))
    peak, total = call(own_column, state, [win, info], [qkv], [ORDER])

    def next_kernel(win, info, qkv, *refs):
        next_columns(columns, win, info, qkv, refs[:3], refs[3:6], *refs[6:])

    result = call(
        next_kernel,
        jax.ShapeDtypeStruct((rows, DIM), bf16),
        [win, info],
        [qkv, lower, low_half, low_rest, upper, up_half, up_rest, peak, total],
        [
            pltpu.VMEM((rows, 2 * DIM), bf16),
            pltpu.VMEM((rows, DIM), f32),
            pltpu.VMEM((rows, 2 * DIM), f32),
            ORDER,
        ],
    )
    back = exchange(result.reshape(MEMBERS, tokens, DIM))
    return call(
        unpack, jax.ShapeDtypeStruct((tokens, HEADS * DIM), bf16), [win, info], [back]
    )


def solution(mesh):
    uly, blk, cfg = (mesh.shape[name] for name in ("uly", "blk", "cfg"))
    fine = Mesh(mesh.devices.reshape(uly, blk // 4, 2, 2, cfg), ("uly", "col", "f", "g", "cfg"))
    tokens = P(("cfg", "col", "f", "g", "uly"), None)
    return jax.shard_map(
        shards,
        mesh=fine,
        in_specs=(tokens, tokens, tokens, P()),
        out_specs=tokens,
        check_vma=False,
    )
```

```python
import jax
import jax.numpy as jnp
from jax import lax
from jax.experimental import pallas as pl
from jax.experimental.pallas import tpu as pltpu
from jax.sharding import Mesh
from jax.sharding import PartitionSpec as P

HEADS = 24
DIM = 128
TILE = 384
PLACES = 16
USED = 12
MEMBERS = 2 * PLACES
CHUNK = 16
BATCH = 4
PACK_VMEM = 62 * 1024 * 1024
GROUP = ("f", "g", "uly")
EXP2_SCALE = DIM**-0.5 * 1.4426950408889634
PARAMS = pltpu.CompilerParams(vmem_limit_bytes=32 * 1024 * 1024)


def fill_order(win, order):
    for place in range(MEMBERS):
        order[place] = 0

    def put(head, wide):
        is_wide = win[2, head] // 2
        order[jnp.where(is_wide > 0, wide, PLACES + head - wide)] = head
        return wide + is_wide

    lax.fori_loop(0, HEADS, put, jnp.int32(0))


def pack(count, win_hbm, *refs):
    sources = refs[:count]
    out, win, held, staged, order, win_done, done, out_done = refs[-8:]
    first = pltpu.make_async_copy(win_hbm, win, win_done)
    first.start()
    copies = []
    for part, source in enumerate(sources):
        for chunk in range(source.shape[0] // CHUNK):
            rows = pl.ds(chunk * CHUNK, CHUNK)
            copy = pltpu.make_async_copy(
                source.at[rows, :], held.at[part, rows, :], done.at[part, chunk]
            )
            copy.start()
            copies.append(copy)
    first.wait()
    fill_order(win, order)
    for copy in copies:
        copy.wait()
    sent = []
    for member in range(MEMBERS):
        frame, row, uly = member // 16, member // 8 % 2, member % 8
        column = pl.multiple_of(order[row * PLACES + frame * 8 + uly] * DIM, DIM)
        for part in range(count):
            staged[member, :, part * DIM : (part + 1) * DIM] = held[part, :, pl.ds(column, DIM)]
        if member % BATCH == BATCH - 1:
            some = pl.ds(member + 1 - BATCH, BATCH)
            copy = pltpu.make_async_copy(
                staged.at[some], out.at[some], out_done.at[member // BATCH]
            )
            copy.start()
            sent.append(copy)
    for copy in sent:
        copy.wait()


def my_windows(win, info, order):
    fill_order(win, order)
    head = order[info[1] * PLACES + info[0]]
    return info[0] < USED, win[0, head] // 2 > 0, win[1, head] // 2 > 0


def lanes(column, width):
    return jnp.broadcast_to(column, (column.shape[0], width))


def side_by_side(parts, axis):
    return parts[0] if len(parts) == 1 else jnp.concatenate(parts, axis=axis)


def score(query, kv, keys):
    parts = [
        lax.dot_general(
            query, kv[some, :DIM], (((1,), (1,)), ((), ())), preferred_element_type=jnp.float32
        )
        for some in keys
    ]
    return side_by_side(parts, 1)


def fold(scores, kv, keys, rows, peak, total, first):
    copies = scores.shape[1] // DIM
    now = lanes(jnp.max(scores, axis=1, keepdims=True), DIM)
    if not first:
        before = peak[rows, :]
        now = jnp.maximum(before, now)
    weights = jnp.exp2((scores - jnp.concatenate([now] * copies, axis=1)) * EXP2_SCALE)
    values = side_by_side([kv[some, DIM : 2 * DIM] for some in keys], 0)
    with_ones = jnp.concatenate([values, jnp.ones_like(values)], axis=1)
    added = jnp.dot(weights.astype(jnp.bfloat16), with_ones, preferred_element_type=jnp.float32)
    peak[rows, :] = now
    if first:
        total[rows, :] = added
    else:
        fade = jnp.exp2((before - now) * EXP2_SCALE)
        total[rows, :] = total[rows, :] * jnp.concatenate([fade, fade], axis=1) + added


def visit(query, kv, frames, heights, peak, total, first=False):
    def chains(blocks, keys):
        ahead = score(query[blocks[0], :], kv, keys[0])
        for index, rows in enumerate(blocks):
            scores = ahead
            if index + 1 < len(blocks):
                ahead = score(query[blocks[index + 1], :], kv, keys[index + 1])
            fold(scores, kv, keys[index], rows, peak, total, first)

    def part(start, size, step):
        return pl.ds(pl.multiple_of(start, step), size)

    @pl.when(frames & heights)
    def _():
        every = [pl.ds(0, 4 * TILE)]
        chains([pl.ds(512 * block, 512) for block in range(3)], [every] * 3)

    @pl.when(frames != heights)
    def _():
        blocks, keys = [], []
        for index in range(2):
            low = jnp.where(heights, 2 * index, index)
            pair = [low * TILE, (low + jnp.where(heights, 1, 2)) * TILE]
            pair = [part(start, TILE, TILE) for start in pair]
            blocks += pair
            keys += [pair, pair]
        chains(blocks, keys)

    @pl.when(jnp.logical_not(frames | heights))
    def _():
        tiles = [pl.ds(tile * TILE, TILE) for tile in range(4)]
        chains(tiles, [[tile] for tile in tiles])


def own_column(win, info, qkv, peak, total, order):
    used, frames, heights = my_windows(win, info, order)
    query = qkv.at[:, 2 * DIM :]

    @pl.when(used)
    def _():
        visit(query, qkv, frames, heights, peak, total, first=True)


def upper_column(columns, win, info, qkv, upper, peak_in, total_in, peak, total, order):
    used, frames, heights = my_windows(win, info, order)
    query = qkv.at[:, 2 * DIM :]

    @pl.when(used)
    def _():
        peak[...] = peak_in[...]
        total[...] = total_in[...]

    @pl.when(used & (info[1] == 0) & (info[2] < columns - 1))
    def _():
        visit(query, upper, frames, heights, peak, total)


def lower_column(win, info, qkv, lower, peak_in, total_in, out, peak, total, order):
    used, frames, heights = my_windows(win, info, order)
    query = qkv.at[:, 2 * DIM :]
    reaches = used & (info[1] == 0) & (info[2] > 0)

    @pl.when(reaches)
    def _():
        peak[...] = peak_in[...]
        total[...] = total_in[...]
        visit(query, lower, frames, heights, peak, total)
        out[...] = (total[:, :DIM] / total[:, DIM:]).astype(jnp.bfloat16)

    @pl.when(used & jnp.logical_not(reaches))
    def _():
        out[...] = (total_in[:, :DIM] / total_in[:, DIM:]).astype(jnp.bfloat16)


def unpack(win, received, out):
    wide = jnp.int32(0)
    for head in range(HEADS):
        is_wide = win[2, head] // 2
        place = jnp.where(is_wide > 0, wide, head - wide)
        member = place // 8 * 16 + (1 - is_wide) * 8 + place % 8
        out[:, head * DIM : (head + 1) * DIM] = received[member]
        wide = wide + is_wide


HBM = pl.BlockSpec(memory_space=pltpu.HBM)
SMEM = pl.BlockSpec(memory_space=pltpu.SMEM)
VMEM = pl.BlockSpec(memory_space=pltpu.VMEM)
ORDER = pltpu.SMEM((MEMBERS,), jnp.int32)


def call(kernel, shapes, scalars, operands, scratch=()):
    return pl.pallas_call(
        kernel,
        out_shape=shapes,
        in_specs=[SMEM] * len(scalars) + [VMEM] * len(operands),
        out_specs=jax.tree.map(lambda _: VMEM, shapes),
        scratch_shapes=list(scratch),
        compiler_params=PARAMS,
    )(*scalars, *operands)


def shards(queries, key_vectors, value_vectors, windows):
    tokens, width = queries.shape
    rows = MEMBERS * tokens
    columns = lax.axis_size("col")
    bf16, f32 = jnp.bfloat16, jnp.float32
    place = lax.axis_index("f") * 8 + lax.axis_index("uly")
    info = jnp.stack([place, lax.axis_index("g"), lax.axis_index("col")]).astype(jnp.int32)
    win = windows.T
    sources = [key_vectors, value_vectors, queries]
    count = len(sources)

    def pack_kernel(*refs):
        pack(count, *refs)

    def exchange(value):
        return lax.all_to_all(value, GROUP, split_axis=0, concat_axis=0, tiled=True)

    sendable = pl.pallas_call(
        pack_kernel,
        out_shape=jax.ShapeDtypeStruct((MEMBERS, tokens, count * DIM), bf16),
        in_specs=[HBM] * (1 + count),
        out_specs=HBM,
        scratch_shapes=[
            pltpu.SMEM(win.shape, jnp.int32),
            pltpu.VMEM((count, tokens, width), bf16),
            pltpu.VMEM((MEMBERS, tokens, count * DIM), bf16),
            ORDER,
            pltpu.SemaphoreType.DMA,
            pltpu.SemaphoreType.DMA((count, tokens // CHUNK)),
            pltpu.SemaphoreType.DMA((MEMBERS // BATCH,)),
        ],
        compiler_params=pltpu.CompilerParams(vmem_limit_bytes=PACK_VMEM),
    )(win, *sources)
    qkv = exchange(sendable).reshape(rows, count * DIM)

    sending = [
        ((uly * columns + col) * 2 + frame) * 2
        for uly in range(8)
        for col in range(columns - 1)
        for frame in range(2)
        if frame * 8 + uly < USED
    ]
    along = ("uly", "col", "f", "g")
    kv = qkv[:, : 2 * DIM]
    lower = lax.ppermute(kv, along, [(member, member + 4) for member in sending])
    upper = lax.ppermute(kv, along, [(member + 4, member) for member in sending])

    state = (jax.ShapeDtypeStruct((rows, DIM), f32), jax.ShapeDtypeStruct((rows, 2 * DIM), f32))
    peak, total = call(own_column, state, [win, info], [qkv], [ORDER])

    def upper_kernel(*refs):
        upper_column(columns, *refs)

    peak, total = call(upper_kernel, state, [win, info], [qkv, upper, peak, total], [ORDER])
    result = call(
        lower_column,
        jax.ShapeDtypeStruct((rows, DIM), bf16),
        [win, info],
        [qkv, lower, peak, total],
        [pltpu.VMEM((rows, DIM), f32), pltpu.VMEM((rows, 2 * DIM), f32), ORDER],
    )
    back = exchange(result.reshape(MEMBERS, tokens, DIM))
    return call(unpack, jax.ShapeDtypeStruct((tokens, HEADS * DIM), bf16), [win], [back])


def solution(mesh):
    uly, blk, cfg = (mesh.shape[name] for name in ("uly", "blk", "cfg"))
    fine = Mesh(mesh.devices.reshape(uly, blk // 4, 2, 2, cfg), ("uly", "col", "f", "g", "cfg"))
    tokens = P(("cfg", "col", "f", "g", "uly"), None)
    return jax.shard_map(
        shards,
        mesh=fine,
        in_specs=(tokens, tokens, tokens, P()),
        out_specs=tokens,
        check_vma=False,
    )
```

```python
import jax
import jax.numpy as jnp
from jax import lax
from jax.experimental import pallas as pl
from jax.experimental.pallas import tpu as pltpu
from jax.sharding import Mesh
from jax.sharding import PartitionSpec as P

HEADS = 24
DIM = 128
TILE = 384
PLACES = 16
USED = 12
MEMBERS = 2 * PLACES
CHUNK = 16
BATCH = 4
PACK_VMEM = 62 * 1024 * 1024
GROUP = ("f", "g", "uly")
EXP2_SCALE = DIM**-0.5 * 1.4426950408889634
PARAMS = pltpu.CompilerParams(vmem_limit_bytes=32 * 1024 * 1024)


def fill_order(win, order):
    for place in range(MEMBERS):
        order[place] = 0

    def put(head, wide):
        is_wide = win[2, head] // 2
        order[jnp.where(is_wide > 0, wide, PLACES + head - wide)] = head
        return wide + is_wide

    lax.fori_loop(0, HEADS, put, jnp.int32(0))


def pack(count, win_hbm, *refs):
    sources = refs[:count]
    out, win, held, staged, order, win_done, done, out_done = refs[-8:]
    first = pltpu.make_async_copy(win_hbm, win, win_done)
    first.start()
    copies = []
    for part, source in enumerate(sources):
        for chunk in range(source.shape[0] // CHUNK):
            rows = pl.ds(chunk * CHUNK, CHUNK)
            copy = pltpu.make_async_copy(
                source.at[rows, :], held.at[part, rows, :], done.at[part, chunk]
            )
            copy.start()
            copies.append(copy)
    first.wait()
    fill_order(win, order)
    for copy in copies:
        copy.wait()
    sent = []
    for member in range(MEMBERS):
        frame, row, uly = member // 16, member // 8 % 2, member % 8
        column = pl.multiple_of(order[row * PLACES + frame * 8 + uly] * DIM, DIM)
        for part in range(count):
            staged[member, :, part * DIM : (part + 1) * DIM] = held[part, :, pl.ds(column, DIM)]
        if member % BATCH == BATCH - 1:
            some = pl.ds(member + 1 - BATCH, BATCH)
            copy = pltpu.make_async_copy(
                staged.at[some], out.at[some], out_done.at[member // BATCH]
            )
            copy.start()
            sent.append(copy)
    for copy in sent:
        copy.wait()


def my_windows(win, info, order):
    fill_order(win, order)
    head = order[info[1] * PLACES + info[0]]
    return info[0] < USED, win[0, head] // 2 > 0, win[1, head] // 2 > 0


def lanes(column, width):
    return jnp.broadcast_to(column, (column.shape[0], width))


def side_by_side(parts, axis):
    return parts[0] if len(parts) == 1 else jnp.concatenate(parts, axis=axis)


def score(query, kv, keys):
    parts = [
        lax.dot_general(
            query, kv[some, :DIM], (((1,), (1,)), ((), ())), preferred_element_type=jnp.float32
        )
        for some in keys
    ]
    return side_by_side(parts, 1)


def fold(scores, kv, keys, rows, peak, total, first):
    copies = scores.shape[1] // DIM
    now = lanes(jnp.max(scores, axis=1, keepdims=True), DIM)
    if not first:
        before = peak[rows, :]
        now = jnp.maximum(before, now)
    weights = jnp.exp2((scores - jnp.concatenate([now] * copies, axis=1)) * EXP2_SCALE)
    values = side_by_side([kv[some, DIM : 2 * DIM] for some in keys], 0)
    with_ones = jnp.concatenate([values, jnp.ones_like(values)], axis=1)
    added = jnp.dot(weights.astype(jnp.bfloat16), with_ones, preferred_element_type=jnp.float32)
    peak[rows, :] = now
    if first:
        total[rows, :] = added
    else:
        fade = jnp.exp2((before - now) * EXP2_SCALE)
        total[rows, :] = total[rows, :] * jnp.concatenate([fade, fade], axis=1) + added


def visit(query, kv, frame, frames, heights, peak, total):
    def chains(blocks):
        ahead = score(query[blocks[0][0], :], kv, blocks[0][1])
        for index, (rows, keys) in enumerate(blocks):
            scores = ahead
            if index + 1 < len(blocks):
                ahead = score(query[blocks[index + 1][0], :], kv, blocks[index + 1][1])
            fold(scores, kv, keys, rows, peak, total, False)

    def tile(index):
        return pl.ds(index * TILE, TILE)

    both = [pl.ds(0, 2 * TILE)]
    mine = [tile(2 * frame + row) for row in range(2)]
    across = [tile(2 * (1 - frame) + row) for row in range(2)]

    @pl.when(frames & heights)
    def _():
        chains([(pl.ds(512 * block, 512), both) for block in range(3)])

    @pl.when(frames & jnp.logical_not(heights))
    def _():
        chains([(rows[row], [tile(row)]) for rows in (mine, across) for row in range(2)])

    @pl.when(heights & jnp.logical_not(frames))
    def _():
        chains([(rows, both) for rows in mine])

    @pl.when(jnp.logical_not(frames | heights))
    def _():
        chains([(mine[row], [tile(row)]) for row in range(2)])


def begin(query, kv, frames, heights, peak, total):
    def chains(blocks, keys):
        ahead = score(query[blocks[0], :], kv, keys[0])
        for index, rows in enumerate(blocks):
            scores = ahead
            if index + 1 < len(blocks):
                ahead = score(query[blocks[index + 1], :], kv, keys[index + 1])
            fold(scores, kv, keys[index], rows, peak, total, True)

    def part(start, size, step):
        return pl.ds(pl.multiple_of(start, step), size)

    @pl.when(frames & heights)
    def _():
        every = [pl.ds(0, 4 * TILE)]
        chains([pl.ds(512 * block, 512) for block in range(3)], [every] * 3)

    @pl.when(frames != heights)
    def _():
        blocks, keys = [], []
        for index in range(2):
            low = jnp.where(heights, 2 * index, index)
            pair = [low * TILE, (low + jnp.where(heights, 1, 2)) * TILE]
            pair = [part(start, TILE, TILE) for start in pair]
            blocks += pair
            keys += [pair, pair]
        chains(blocks, keys)

    @pl.when(jnp.logical_not(frames | heights))
    def _():
        tiles = [pl.ds(tile * TILE, TILE) for tile in range(4)]
        chains(tiles, [[tile] for tile in tiles])


def own_column(win, info, qkv, peak, total, order):
    used, frames, heights = my_windows(win, info, order)
    query = qkv.at[:, 2 * DIM :]

    @pl.when(used)
    def _():
        begin(query, qkv, frames, heights, peak, total)


def next_columns(columns, frame, win, info, qkv, lower, upper, peak_in, total_in, *refs):
    out, (peak, total, order) = refs[:-3], refs[-3:]
    used, frames, heights = my_windows(win, info, order)
    query = qkv.at[:, 2 * DIM :]
    wide = used & (info[1] == 0)

    @pl.when(used)
    def _():
        peak[...] = peak_in[...]
        total[...] = total_in[...]

    @pl.when(wide & (info[2] > 0))
    def _():
        visit(query, lower, frame, frames, heights, peak, total)

    @pl.when(wide & (info[2] < columns - 1))
    def _():
        visit(query, upper, frame, frames, heights, peak, total)

    for result in out:

        @pl.when(used)
        def _(result=result):
            result[...] = (total[:, :DIM] / total[:, DIM:]).astype(jnp.bfloat16)


def unpack(win, received, out):
    wide = jnp.int32(0)
    for head in range(HEADS):
        is_wide = win[2, head] // 2
        place = jnp.where(is_wide > 0, wide, head - wide)
        member = place // 8 * 16 + (1 - is_wide) * 8 + place % 8
        out[:, head * DIM : (head + 1) * DIM] = received[member]
        wide = wide + is_wide


HBM = pl.BlockSpec(memory_space=pltpu.HBM)
SMEM = pl.BlockSpec(memory_space=pltpu.SMEM)
VMEM = pl.BlockSpec(memory_space=pltpu.VMEM)
ORDER = pltpu.SMEM((MEMBERS,), jnp.int32)


def call(kernel, shapes, scalars, operands, scratch=()):
    return pl.pallas_call(
        kernel,
        out_shape=shapes,
        in_specs=[SMEM] * len(scalars) + [VMEM] * len(operands),
        out_specs=jax.tree.map(lambda _: VMEM, shapes),
        scratch_shapes=list(scratch),
        compiler_params=PARAMS,
    )(*scalars, *operands)


def shards(queries, key_vectors, value_vectors, windows):
    tokens, width = queries.shape
    rows = MEMBERS * tokens
    columns = lax.axis_size("col")
    bf16, f32 = jnp.bfloat16, jnp.float32
    place = lax.axis_index("f") * 8 + lax.axis_index("uly")
    info = jnp.stack([place, lax.axis_index("g"), lax.axis_index("col")]).astype(jnp.int32)
    win = windows.T
    sources = [key_vectors, value_vectors, queries]
    count = len(sources)

    def pack_kernel(*refs):
        pack(count, *refs)

    def exchange(value):
        return lax.all_to_all(value, GROUP, split_axis=0, concat_axis=0, tiled=True)

    sendable = pl.pallas_call(
        pack_kernel,
        out_shape=jax.ShapeDtypeStruct((MEMBERS, tokens, count * DIM), bf16),
        in_specs=[HBM] * (1 + count),
        out_specs=HBM,
        scratch_shapes=[
            pltpu.SMEM(win.shape, jnp.int32),
            pltpu.VMEM((count, tokens, width), bf16),
            pltpu.VMEM((MEMBERS, tokens, count * DIM), bf16),
            ORDER,
            pltpu.SemaphoreType.DMA,
            pltpu.SemaphoreType.DMA((count, tokens // CHUNK)),
            pltpu.SemaphoreType.DMA((MEMBERS // BATCH,)),
        ],
        compiler_params=pltpu.CompilerParams(vmem_limit_bytes=PACK_VMEM),
    )(win, *sources)
    qkv = exchange(sendable).reshape(rows, count * DIM)

    sending = [
        ((uly * columns + col) * 2 + frame) * 2
        for uly in range(8)
        for col in range(columns - 1)
        for frame in range(2)
        if frame * 8 + uly < USED
    ]
    along = ("uly", "col", "f", "g")
    beside = []
    for frame in range(2):
        kv = qkv[frame * rows // 2 : (frame + 1) * rows // 2, : 2 * DIM]
        lower = lax.ppermute(kv, along, [(member, member + 4) for member in sending])
        upper = lax.ppermute(kv, along, [(member + 4, member) for member in sending])
        beside.append([lower, upper])

    state = (jax.ShapeDtypeStruct((rows, DIM), f32), jax.ShapeDtypeStruct((rows, 2 * DIM), f32))
    peak, total = call(own_column, state, [win, info], [qkv], [ORDER])

    def first_kernel(*refs):
        next_columns(columns, 0, *refs)

    def last_kernel(*refs):
        next_columns(columns, 1, *refs)

    peak, total = call(first_kernel, state, [win, info], [qkv, *beside[0], peak, total], [ORDER])
    result = call(
        last_kernel,
        jax.ShapeDtypeStruct((rows, DIM), bf16),
        [win, info],
        [qkv, *beside[1], peak, total],
        [pltpu.VMEM((rows, DIM), f32), pltpu.VMEM((rows, 2 * DIM), f32), ORDER],
    )
    back = exchange(result.reshape(MEMBERS, tokens, DIM))
    return call(unpack, jax.ShapeDtypeStruct((tokens, HEADS * DIM), bf16), [win], [back])


def solution(mesh):
    uly, blk, cfg = (mesh.shape[name] for name in ("uly", "blk", "cfg"))
    fine = Mesh(mesh.devices.reshape(uly, blk // 4, 2, 2, cfg), ("uly", "col", "f", "g", "cfg"))
    tokens = P(("cfg", "col", "f", "g", "uly"), None)
    return jax.shard_map(
        shards,
        mesh=fine,
        in_specs=(tokens, tokens, tokens, P()),
        out_specs=tokens,
        check_vma=False,
    )
```

```python
import jax
import jax.numpy as jnp
from jax import lax
from jax.experimental import pallas as pl
from jax.experimental.pallas import tpu as pltpu
from jax.sharding import Mesh
from jax.sharding import PartitionSpec as P

HEADS = 24
DIM = 128
TILE = 384
PLACES = 16
USED = 12
OWN, LOWER, UPPER, JOINED, PAIRED, FRAMES, HEAD = 0, 1, 2, 3, 4, 5, 8
MEMBERS = 2 * PLACES
CHUNK = 16
BATCH = 4
PACK_VMEM = 62 * 1024 * 1024
GROUP = ("f", "g", "uly")
EXP2_SCALE = DIM**-0.5 * 1.4426950408889634
PARAMS = pltpu.CompilerParams(vmem_limit_bytes=32 * 1024 * 1024)


def is_open(win, axis, head):
    return win[axis, head] // 2


def fill_order(win, order, facts):
    for place in range(2 * PLACES):
        order[place] = 0

    def put(head, carry):
        joined, apart = carry
        wide = is_open(win, 2, head)
        both = wide * is_open(win, 0, head) * is_open(win, 1, head)
        turn = jnp.where(both > 0, joined, USED - 1 - apart)
        place = jnp.where(turn < 4, turn + 4, jnp.where(turn < 8, turn - 4, turn))
        place = jnp.where(wide > 0, place, head - joined - apart)
        order[(1 - wide) * PLACES + place] = head
        facts[HEAD + head] = place // 8 * 16 + (1 - wide) * 8 + place % 8
        return joined + both, apart + wide - both

    lax.fori_loop(0, HEADS, put, (jnp.int32(0), jnp.int32(0)))


def state_facts(columns, win, info, order, facts):
    place, row, column = info[0], info[1], info[2]
    head = order[row * PLACES + place]
    frames, heights = is_open(win, 0, head), is_open(win, 1, head)
    used = jnp.where(place < USED, 1, 0)
    wide = used * (1 - row)
    facts[OWN] = used
    facts[LOWER] = jnp.where(column > 0, wide, 0)
    facts[UPPER] = jnp.where(column < columns - 1, wide, 0)
    facts[JOINED] = frames * heights
    facts[PAIRED] = frames + heights - 2 * frames * heights
    facts[FRAMES] = frames


def pack(columns, count, win_hbm, info_hbm, *refs):
    sources = refs[:count]
    out, facts, win, info, held, staged, order, few_done, done, out_done = refs[-10:]
    few = [
        pltpu.make_async_copy(win_hbm, win, few_done.at[0]),
        pltpu.make_async_copy(info_hbm, info, few_done.at[1]),
    ]
    for copy in few:
        copy.start()
    copies = []
    for part, source in enumerate(sources):
        for chunk in range(source.shape[0] // CHUNK):
            rows = pl.ds(chunk * CHUNK, CHUNK)
            copy = pltpu.make_async_copy(
                source.at[rows, :], held.at[part, rows, :], done.at[part, chunk]
            )
            copy.start()
            copies.append(copy)
    for copy in few:
        copy.wait()
    fill_order(win, order, facts)
    state_facts(columns, win, info, order, facts)
    for copy in copies:
        copy.wait()
    sent = []
    for member in range(MEMBERS):
        frame, row, uly = member // 16, member // 8 % 2, member % 8
        column = pl.multiple_of(order[row * PLACES + frame * 8 + uly] * DIM, DIM)
        for part in range(count):
            staged[member, :, part * DIM : (part + 1) * DIM] = held[part, :, pl.ds(column, DIM)]
        if member % BATCH == BATCH - 1:
            some = pl.ds(member + 1 - BATCH, BATCH)
            copy = pltpu.make_async_copy(
                staged.at[some], out.at[some], out_done.at[member // BATCH]
            )
            copy.start()
            sent.append(copy)
    for copy in sent:
        copy.wait()


def lanes(column, width):
    return jnp.broadcast_to(column, (column.shape[0], width))


def side_by_side(parts, axis):
    return parts[0] if len(parts) == 1 else jnp.concatenate(parts, axis=axis)


def score(query, kv, keys):
    parts = [
        lax.dot_general(
            query, kv[some, :DIM], (((1,), (1,)), ((), ())), preferred_element_type=jnp.float32
        )
        for some in keys
    ]
    return side_by_side(parts, 1)


def fold(scores, kv, keys, rows, before, write):
    copies = scores.shape[1] // DIM
    now = lanes(jnp.max(scores, axis=1, keepdims=True), DIM)
    if before:
        peak = before[0][rows, :]
        now = jnp.maximum(peak, now)
    weights = jnp.exp2((scores - jnp.concatenate([now] * copies, axis=1)) * EXP2_SCALE)
    values = side_by_side([kv[some, DIM : 2 * DIM] for some in keys], 0)
    with_ones = jnp.concatenate([values, jnp.ones_like(values)], axis=1)
    total = jnp.dot(weights.astype(jnp.bfloat16), with_ones, preferred_element_type=jnp.float32)
    if before:
        fade = jnp.exp2((peak - now) * EXP2_SCALE)
        total = before[1][rows, :] * jnp.concatenate([fade, fade], axis=1) + total
    write(rows, now, total)


def visit(query, kv, facts, before, write):
    def chains(blocks, keys):
        ahead = score(query[blocks[0], :], kv, keys[0])
        for index, rows in enumerate(blocks):
            scores = ahead
            if index + 1 < len(blocks):
                ahead = score(query[blocks[index + 1], :], kv, keys[index + 1])
            fold(scores, kv, keys[index], rows, before, write)

    def tile_rows(tile):
        return pl.ds(pl.multiple_of(tile * TILE, TILE), TILE)

    @pl.when(facts[JOINED] > 0)
    def _():
        every = [pl.ds(0, 4 * TILE)]
        chains([pl.ds(512 * block, 512) for block in range(3)], [every] * 3)

    @pl.when(facts[PAIRED] > 0)
    def _():
        blocks, keys = [], []
        for index in range(2):
            low = jnp.where(facts[FRAMES] > 0, index, 2 * index)
            pair = [tile_rows(low), tile_rows(low + jnp.where(facts[FRAMES] > 0, 2, 1))]
            blocks += pair
            keys += [pair, pair]
        chains(blocks, keys)

    @pl.when(facts[JOINED] + facts[PAIRED] == 0)
    def _():
        tiles = [pl.ds(tile * TILE, TILE) for tile in range(4)]
        chains(tiles, [[tile] for tile in tiles])


def keep(peak, total):
    def write(rows, now, sums):
        peak[rows, :] = now
        total[rows, :] = sums

    return write


def divided(total):
    return (total[:, :DIM] / total[:, DIM:]).astype(jnp.bfloat16)


def own_column(facts, qkv, peak, total):
    @pl.when(facts[OWN] > 0)
    def _():
        visit(qkv.at[:, 2 * DIM :], qkv, facts, None, keep(peak, total))


def upper_column(facts, qkv, upper, peak_in, total_in, peak, total):
    @pl.when(facts[UPPER] > 0)
    def _():
        visit(qkv.at[:, 2 * DIM :], upper, facts, (peak_in, total_in), keep(peak, total))

    @pl.when(facts[OWN] > facts[UPPER])
    def _():
        peak[...] = peak_in[...]
        total[...] = total_in[...]


def lower_column(facts, qkv, lower, peak_in, total_in, out):
    def write(rows, now, sums):
        out[rows, :] = divided(sums)

    @pl.when(facts[LOWER] > 0)
    def _():
        visit(qkv.at[:, 2 * DIM :], lower, facts, (peak_in, total_in), write)

    @pl.when(facts[OWN] > facts[LOWER])
    def _():
        out[...] = divided(total_in[...])


def unpack(facts, received, out):
    for head in range(HEADS):
        out[:, head * DIM : (head + 1) * DIM] = received[facts[HEAD + head]]


HBM = pl.BlockSpec(memory_space=pltpu.HBM)
SMEM = pl.BlockSpec(memory_space=pltpu.SMEM)
VMEM = pl.BlockSpec(memory_space=pltpu.VMEM)
ORDER = pltpu.SMEM((MEMBERS,), jnp.int32)


def call(kernel, shapes, scalars, operands, scratch=()):
    return pl.pallas_call(
        kernel,
        out_shape=shapes,
        in_specs=[SMEM] * len(scalars) + [VMEM] * len(operands),
        out_specs=jax.tree.map(lambda _: VMEM, shapes),
        scratch_shapes=list(scratch),
        compiler_params=PARAMS,
    )(*scalars, *operands)


def shards(queries, key_vectors, value_vectors, windows):
    tokens, width = queries.shape
    rows = MEMBERS * tokens
    columns = lax.axis_size("col")
    bf16, f32 = jnp.bfloat16, jnp.float32
    place = lax.axis_index("f") * 8 + lax.axis_index("uly")
    info = jnp.stack([place, lax.axis_index("g"), lax.axis_index("col")]).astype(jnp.int32)
    win = windows.T
    sources = [key_vectors, value_vectors, queries]
    count = len(sources)

    def pack_kernel(*refs):
        pack(columns, count, *refs)

    def exchange(value):
        return lax.all_to_all(value, GROUP, split_axis=0, concat_axis=0, tiled=True)

    sendable, facts = pl.pallas_call(
        pack_kernel,
        out_shape=(
            jax.ShapeDtypeStruct((MEMBERS, tokens, count * DIM), bf16),
            jax.ShapeDtypeStruct((HEAD + HEADS,), jnp.int32),
        ),
        in_specs=[HBM] * (2 + count),
        out_specs=(HBM, SMEM),
        scratch_shapes=[
            pltpu.SMEM(win.shape, jnp.int32),
            pltpu.SMEM(info.shape, jnp.int32),
            pltpu.VMEM((count, tokens, width), bf16),
            pltpu.VMEM((MEMBERS, tokens, count * DIM), bf16),
            ORDER,
            pltpu.SemaphoreType.DMA((2,)),
            pltpu.SemaphoreType.DMA((count, tokens // CHUNK)),
            pltpu.SemaphoreType.DMA((MEMBERS // BATCH,)),
        ],
        compiler_params=pltpu.CompilerParams(vmem_limit_bytes=PACK_VMEM),
    )(win, info, *sources)
    qkv = exchange(sendable).reshape(rows, count * DIM)

    sending = [
        ((uly * columns + col) * 2 + frame) * 2
        for uly in range(8)
        for col in range(columns - 1)
        for frame in range(2)
        if frame * 8 + uly < USED
    ]
    along = ("uly", "col", "f", "g")
    kv = qkv[:, : 2 * DIM]
    lower = lax.ppermute(kv, along, [(member, member + 4) for member in sending])
    upper = lax.ppermute(kv, along, [(member + 4, member) for member in sending])

    state = (jax.ShapeDtypeStruct((rows, DIM), f32), jax.ShapeDtypeStruct((rows, 2 * DIM), f32))
    peak, total = call(own_column, state, [facts], [qkv])
    peak, total = call(upper_column, state, [facts], [qkv, upper, peak, total])
    result = call(
        lower_column, jax.ShapeDtypeStruct((rows, DIM), bf16), [facts], [qkv, lower, peak, total]
    )
    back = exchange(result.reshape(MEMBERS, tokens, DIM))
    return call(unpack, jax.ShapeDtypeStruct((tokens, HEADS * DIM), bf16), [facts], [back])


def solution(mesh):
    uly, blk, cfg = (mesh.shape[name] for name in ("uly", "blk", "cfg"))
    fine = Mesh(mesh.devices.reshape(uly, blk // 4, 2, 2, cfg), ("uly", "col", "f", "g", "cfg"))
    tokens = P(("cfg", "col", "f", "g", "uly"), None)
    return jax.shard_map(
        shards,
        mesh=fine,
        in_specs=(tokens, tokens, tokens, P()),
        out_specs=tokens,
        check_vma=False,
    )
```

```python
import jax
import jax.numpy as jnp
from jax import lax
from jax.experimental import pallas as pl
from jax.experimental.pallas import tpu as pltpu
from jax.sharding import Mesh
from jax.sharding import PartitionSpec as P

HEADS = 24
DIM = 128
TILE = 384
PLACES = 16
USED = 12
OWN, LOWER, UPPER, JOINED, PAIRED, FRAMES, HEAD = 0, 1, 2, 3, 4, 5, 8
MEMBERS = 2 * PLACES
CHUNK = 16
BATCH = 4
RUN = 8
PACK_VMEM = 62 * 1024 * 1024
GROUP = ("f", "g", "uly")
EXP2_SCALE = DIM**-0.5 * 1.4426950408889634
PARAMS = pltpu.CompilerParams(vmem_limit_bytes=32 * 1024 * 1024)


def is_open(win, axis, head):
    return win[axis, head] // 2


def fill_order(win, order, facts=None):
    for place in range(2 * PLACES):
        order[place] = 0

    def put(head, carry):
        joined, apart = carry
        wide = is_open(win, 2, head)
        both = wide * is_open(win, 0, head) * is_open(win, 1, head)
        turn = jnp.where(both > 0, joined, USED - 1 - apart)
        place = jnp.where(turn < 4, turn + 4, jnp.where(turn < 8, turn - 4, turn))
        place = jnp.where(wide > 0, place, head - joined - apart)
        order[(1 - wide) * PLACES + place] = head
        if facts is not None:
            facts[HEAD + head] = place // 8 * 16 + (1 - wide) * 8 + place % 8
        return joined + both, apart + wide - both

    lax.fori_loop(0, HEADS, put, (jnp.int32(0), jnp.int32(0)))


def state_facts(columns, win, info, facts, order):
    fill_order(win, order, facts)
    place, row, column = info[0], info[1], info[2]
    head = order[row * PLACES + place]
    frames, heights = is_open(win, 0, head), is_open(win, 1, head)
    used = jnp.where(place < USED, 1, 0)
    wide = used * (1 - row)
    facts[OWN] = used
    facts[LOWER] = jnp.where(column > 0, wide, 0)
    facts[UPPER] = jnp.where(column < columns - 1, wide, 0)
    facts[JOINED] = frames * heights
    facts[PAIRED] = frames + heights - 2 * frames * heights
    facts[FRAMES] = frames


def pack(count, win_hbm, *refs):
    sources = refs[:count]
    out, win, held, staged, order, win_done, done, out_done = refs[-8:]
    first = pltpu.make_async_copy(win_hbm, win, win_done)
    first.start()
    copies = []
    for part, source in enumerate(sources):
        for chunk in range(source.shape[0] // CHUNK):
            rows = pl.ds(chunk * CHUNK, CHUNK)
            copy = pltpu.make_async_copy(
                source.at[rows, :], held.at[part, rows, :], done.at[part, chunk]
            )
            copy.start()
            copies.append(copy)
    first.wait()
    fill_order(win, order)
    for copy in copies:
        copy.wait()
    sent = []
    for member in range(MEMBERS):
        frame, row, uly = member // 16, member // 8 % 2, member % 8
        column = pl.multiple_of(order[row * PLACES + frame * 8 + uly] * DIM, DIM)
        for part in range(count):
            staged[member, :, part * DIM : (part + 1) * DIM] = held[part, :, pl.ds(column, DIM)]
        if member % BATCH == BATCH - 1:
            some = pl.ds(member + 1 - BATCH, BATCH)
            copy = pltpu.make_async_copy(
                staged.at[some], out.at[some], out_done.at[member // BATCH]
            )
            copy.start()
            sent.append(copy)
    for copy in sent:
        copy.wait()


def lanes(column, width):
    return jnp.broadcast_to(column, (column.shape[0], width))


def side_by_side(parts, axis):
    return parts[0] if len(parts) == 1 else jnp.concatenate(parts, axis=axis)


def score(query, kv, keys):
    parts = [
        lax.dot_general(
            query, kv[some, :DIM], (((1,), (1,)), ((), ())), preferred_element_type=jnp.float32
        )
        for some in keys
    ]
    return side_by_side(parts, 1)


def fold(scores, kv, keys, rows, before, write):
    copies = scores.shape[1] // DIM
    now = lanes(jnp.max(scores, axis=1, keepdims=True), DIM)
    if before:
        peak = before[0][rows, :]
        now = jnp.maximum(peak, now)
    weights = jnp.exp2((scores - jnp.concatenate([now] * copies, axis=1)) * EXP2_SCALE)
    values = side_by_side([kv[some, DIM : 2 * DIM] for some in keys], 0)
    with_ones = jnp.concatenate([values, jnp.ones_like(values)], axis=1)
    total = jnp.dot(weights.astype(jnp.bfloat16), with_ones, preferred_element_type=jnp.float32)
    if before:
        fade = jnp.exp2((peak - now) * EXP2_SCALE)
        total = before[1][rows, :] * jnp.concatenate([fade, fade], axis=1) + total
    write(rows, now, total)


def visit(query, kv, facts, before, write):
    def chains(blocks, keys):
        ahead = score(query[blocks[0], :], kv, keys[0])
        for index, rows in enumerate(blocks):
            scores = ahead
            if index + 1 < len(blocks):
                ahead = score(query[blocks[index + 1], :], kv, keys[index + 1])
            fold(scores, kv, keys[index], rows, before, write)

    def tile_rows(tile):
        return pl.ds(pl.multiple_of(tile * TILE, TILE), TILE)

    @pl.when(facts[JOINED] > 0)
    def _():
        every = [pl.ds(0, 4 * TILE)]
        chains([pl.ds(512 * block, 512) for block in range(3)], [every] * 3)

    @pl.when(facts[PAIRED] > 0)
    def _():
        blocks, keys = [], []
        for index in range(2):
            low = jnp.where(facts[FRAMES] > 0, index, 2 * index)
            pair = [tile_rows(low), tile_rows(low + jnp.where(facts[FRAMES] > 0, 2, 1))]
            blocks += pair
            keys += [pair, pair]
        chains(blocks, keys)

    @pl.when(facts[JOINED] + facts[PAIRED] == 0)
    def _():
        tiles = [pl.ds(tile * TILE, TILE) for tile in range(4)]
        chains(tiles, [[tile] for tile in tiles])


def keep(peak, total):
    def write(rows, now, sums):
        peak[rows, :] = now
        total[rows, :] = sums

    return write


def divided(total):
    return (total[:, :DIM] / total[:, DIM:]).astype(jnp.bfloat16)


def own_column(facts, qkv, peak, total):
    @pl.when(facts[OWN] > 0)
    def _():
        visit(qkv.at[:, 2 * DIM :], qkv, facts, None, keep(peak, total))


def upper_column(facts, qkv, upper, peak_in, total_in, peak, total):
    @pl.when(facts[UPPER] > 0)
    def _():
        visit(qkv.at[:, 2 * DIM :], upper, facts, (peak_in, total_in), keep(peak, total))

    @pl.when(facts[OWN] > facts[UPPER])
    def _():
        peak[...] = peak_in[...]
        total[...] = total_in[...]


def lower_column(facts, qkv, lower, peak_in, total_in, out):
    def write(rows, now, sums):
        out[rows, :] = divided(sums)

    @pl.when(facts[LOWER] > 0)
    def _():
        visit(qkv.at[:, 2 * DIM :], lower, facts, (peak_in, total_in), write)

    @pl.when(facts[OWN] > facts[LOWER])
    def _():
        out[...] = divided(total_in[...])


def unpack(facts, received, out, staged, done):
    copies = []
    for head in range(HEADS):
        staged[:, head * DIM : (head + 1) * DIM] = received[facts[HEAD + head]]
        if head % RUN == RUN - 1:
            columns = pl.ds((head + 1 - RUN) * DIM, RUN * DIM)
            copy = pltpu.make_async_copy(
                staged.at[:, columns], out.at[:, columns], done.at[head // RUN]
            )
            copy.start()
            copies.append(copy)
    for copy in copies:
        copy.wait()


HBM = pl.BlockSpec(memory_space=pltpu.HBM)
SMEM = pl.BlockSpec(memory_space=pltpu.SMEM)
VMEM = pl.BlockSpec(memory_space=pltpu.VMEM)
ORDER = pltpu.SMEM((MEMBERS,), jnp.int32)


def call(kernel, shapes, scalars, operands, scratch=()):
    return pl.pallas_call(
        kernel,
        out_shape=shapes,
        in_specs=[SMEM] * len(scalars) + [VMEM] * len(operands),
        out_specs=jax.tree.map(lambda _: VMEM, shapes),
        scratch_shapes=list(scratch),
        compiler_params=PARAMS,
    )(*scalars, *operands)


def shards(queries, key_vectors, value_vectors, windows):
    tokens, width = queries.shape
    rows = MEMBERS * tokens
    columns = lax.axis_size("col")
    bf16, f32 = jnp.bfloat16, jnp.float32
    place = lax.axis_index("f") * 8 + lax.axis_index("uly")
    info = jnp.stack([place, lax.axis_index("g"), lax.axis_index("col")]).astype(jnp.int32)
    win = windows.T
    sources = [key_vectors, value_vectors, queries]
    count = len(sources)

    def pack_kernel(*refs):
        pack(count, *refs)

    def exchange(value):
        return lax.all_to_all(value, GROUP, split_axis=0, concat_axis=0, tiled=True)

    sendable = pl.pallas_call(
        pack_kernel,
        out_shape=jax.ShapeDtypeStruct((MEMBERS, tokens, count * DIM), bf16),
        in_specs=[HBM] * (1 + count),
        out_specs=HBM,
        scratch_shapes=[
            pltpu.SMEM(win.shape, jnp.int32),
            pltpu.VMEM((count, tokens, width), bf16),
            pltpu.VMEM((MEMBERS, tokens, count * DIM), bf16),
            ORDER,
            pltpu.SemaphoreType.DMA,
            pltpu.SemaphoreType.DMA((count, tokens // CHUNK)),
            pltpu.SemaphoreType.DMA((MEMBERS // BATCH,)),
        ],
        compiler_params=pltpu.CompilerParams(vmem_limit_bytes=PACK_VMEM),
    )(win, *sources)
    qkv = exchange(sendable).reshape(rows, count * DIM)

    sending = [
        ((uly * columns + col) * 2 + frame) * 2
        for uly in range(8)
        for col in range(columns - 1)
        for frame in range(2)
        if frame * 8 + uly < USED
    ]
    along = ("uly", "col", "f", "g")
    kv = qkv[:, : 2 * DIM]
    lower = lax.ppermute(kv, along, [(member, member + 4) for member in sending])
    upper = lax.ppermute(kv, along, [(member + 4, member) for member in sending])

    state = (jax.ShapeDtypeStruct((rows, DIM), f32), jax.ShapeDtypeStruct((rows, 2 * DIM), f32))
    def facts_kernel(*refs):
        state_facts(columns, *refs)

    facts = pl.pallas_call(
        facts_kernel,
        out_shape=jax.ShapeDtypeStruct((HEAD + HEADS,), jnp.int32),
        in_specs=[SMEM, SMEM],
        out_specs=SMEM,
        scratch_shapes=[ORDER],
        compiler_params=PARAMS,
    )(win, info)
    peak, total = call(own_column, state, [facts], [qkv])
    peak, total = call(upper_column, state, [facts], [qkv, upper, peak, total])
    result = call(
        lower_column, jax.ShapeDtypeStruct((rows, DIM), bf16), [facts], [qkv, lower, peak, total]
    )
    back = exchange(result.reshape(MEMBERS, tokens, DIM))
    return pl.pallas_call(
        unpack,
        out_shape=jax.ShapeDtypeStruct((tokens, width), bf16),
        in_specs=[SMEM, VMEM],
        out_specs=HBM,
        scratch_shapes=[
            pltpu.VMEM((tokens, width), bf16),
            pltpu.SemaphoreType.DMA((HEADS // RUN,)),
        ],
        compiler_params=PARAMS,
    )(facts, back)


def solution(mesh):
    uly, blk, cfg = (mesh.shape[name] for name in ("uly", "blk", "cfg"))
    fine = Mesh(mesh.devices.reshape(uly, blk // 4, 2, 2, cfg), ("uly", "col", "f", "g", "cfg"))
    tokens = P(("cfg", "col", "f", "g", "uly"), None)
    return jax.shard_map(
        shards,
        mesh=fine,
        in_specs=(tokens, tokens, tokens, P()),
        out_specs=tokens,
        check_vma=False,
    )
```

```python
import jax
import jax.numpy as jnp
from jax import lax
from jax.experimental import pallas as pl
from jax.experimental.pallas import tpu as pltpu
from jax.sharding import Mesh
from jax.sharding import PartitionSpec as P

HEADS = 24
DIM = 128
TILE = 384
PLACES = 16
USED = 12
WHOLE = 8
OWN, LOWER, UPPER, JOINED, PAIRED, FRAMES, LO, HI, HALVED, REST, FIRST, SECOND, HEAD = range(13)
MEMBERS = 2 * PLACES
CHUNK = 16
BATCH = 4
RUN = 8
PACK_VMEM = 62 * 1024 * 1024
GROUP = ("f", "g", "uly")
EXP2_SCALE = DIM**-0.5 * 1.4426950408889634
PARAMS = pltpu.CompilerParams(vmem_limit_bytes=32 * 1024 * 1024)


def is_open(win, axis, head):
    return win[axis, head] // 2


def fill_order(win, order, told=None):
    for place in range(2 * PLACES):
        order[place] = 0

    def put(head, carry):
        joined, apart = carry
        frames, heights, wide = (is_open(win, axis, head) for axis in range(3))
        both = wide * frames * heights
        place = jnp.where(both > 0, joined, USED - 1 - apart)
        place = jnp.where(wide > 0, place, head - joined - apart)
        order[(1 - wide) * PLACES + place] = head
        if told is not None:
            told(head, wide, place, frames, heights)
        return joined + both, apart + wide - both

    lax.fori_loop(0, HEADS, put, (jnp.int32(0), jnp.int32(0)))
    for place in range(WHOLE, USED):
        order[place + USED - WHOLE] = order[place]


def state_facts(columns, win, info, facts, order):
    place, row, column, frame = info[0], info[1], info[2], info[3]

    def count(head, joined):
        return joined + is_open(win, 0, head) * is_open(win, 1, head) * is_open(win, 2, head)

    split = jnp.where(lax.fori_loop(0, HEADS, count, jnp.int32(0)) <= WHOLE, 1, 0)

    def told(head, wide, at, frames, heights):
        half = jnp.where(frames > heights, row, frame)
        at = jnp.where(wide * split * at >= WHOLE, at + (USED - WHOLE) * half, at)
        facts[HEAD + head] = at // 8 * 16 + (1 - wide) * 8 + at % 8

    fill_order(win, order, told)
    head = order[row * PLACES + place]
    frames, heights = is_open(win, 0, head), is_open(win, 1, head)
    shared = jnp.where(place >= WHOLE, 1 - row, 0)
    halved = shared * split
    half = jnp.where(place >= USED, halved, 0)
    used = jnp.where((place < USED) | (halved > 0), 1, 0)
    wide = used * (1 - row)
    facts[OWN] = used
    facts[LOWER] = jnp.where(column > 0, wide, 0)
    facts[UPPER] = jnp.where(column < columns - 1, wide, 0)
    facts[JOINED] = frames * heights
    facts[PAIRED] = frames + heights - 2 * frames * heights
    facts[FRAMES] = frames
    facts[LO] = half
    facts[HI] = jnp.where(halved > 0, half + 1, 2)
    facts[HALVED] = shared
    facts[REST] = shared * (1 - split)
    by_row = halved * jnp.where(frames > heights, 1, 0)
    first = jnp.where(by_row > 0, half, 2 * half)
    facts[FIRST] = first
    facts[SECOND] = first + 1 + by_row


def pack(count, win_hbm, *refs):
    sources = refs[:count]
    out, win, held, staged, order, win_done, done, out_done = refs[-8:]
    first = pltpu.make_async_copy(win_hbm, win, win_done)
    first.start()
    copies = []
    for part, source in enumerate(sources):
        for chunk in range(source.shape[0] // CHUNK):
            rows = pl.ds(chunk * CHUNK, CHUNK)
            copy = pltpu.make_async_copy(
                source.at[rows, :], held.at[part, rows, :], done.at[part, chunk]
            )
            copy.start()
            copies.append(copy)
    first.wait()
    fill_order(win, order)
    for copy in copies:
        copy.wait()
    sent = []
    for member in range(MEMBERS):
        frame, row, uly = member // 16, member // 8 % 2, member % 8
        column = pl.multiple_of(order[row * PLACES + frame * 8 + uly] * DIM, DIM)
        for part in range(count):
            staged[member, :, part * DIM : (part + 1) * DIM] = held[part, :, pl.ds(column, DIM)]
        if member % BATCH == BATCH - 1:
            some = pl.ds(member + 1 - BATCH, BATCH)
            copy = pltpu.make_async_copy(
                staged.at[some], out.at[some], out_done.at[member // BATCH]
            )
            copy.start()
            sent.append(copy)
    for copy in sent:
        copy.wait()


def lanes(column, width):
    return jnp.broadcast_to(column, (column.shape[0], width))


def side_by_side(parts, axis):
    return parts[0] if len(parts) == 1 else jnp.concatenate(parts, axis=axis)


def score(query, kv, keys):
    parts = [
        lax.dot_general(
            query, kv[some, :DIM], (((1,), (1,)), ((), ())), preferred_element_type=jnp.float32
        )
        for some in keys
    ]
    return side_by_side(parts, 1)


def fold(scores, kv, keys, rows, before, write):
    copies = scores.shape[1] // DIM
    now = lanes(jnp.max(scores, axis=1, keepdims=True), DIM)
    if before:
        peak = before[0][rows, :]
        now = jnp.maximum(peak, now)
    weights = jnp.exp2((scores - jnp.concatenate([now] * copies, axis=1)) * EXP2_SCALE)
    values = side_by_side([kv[some, DIM : 2 * DIM] for some in keys], 0)
    with_ones = jnp.concatenate([values, jnp.ones_like(values)], axis=1)
    total = jnp.dot(weights.astype(jnp.bfloat16), with_ones, preferred_element_type=jnp.float32)
    if before:
        fade = jnp.exp2((peak - now) * EXP2_SCALE)
        total = before[1][rows, :] * jnp.concatenate([fade, fade], axis=1) + total
    write(rows, now, total)


def tile_rows(tile):
    return pl.ds(pl.multiple_of(tile * TILE, TILE), TILE)


def visit(query, kv, facts, before, write):
    def chains(blocks, keys):
        ahead = score(query[blocks[0], :], kv, keys[0])
        for index, rows in enumerate(blocks):
            scores = ahead
            if index + 1 < len(blocks):
                ahead = score(query[blocks[index + 1], :], kv, keys[index + 1])
            fold(scores, kv, keys[index], rows, before, write)

    @pl.when(facts[JOINED] > 0)
    def _():
        every = [pl.ds(0, 4 * TILE)]
        chains([pl.ds(512 * block, 512) for block in range(3)], [every] * 3)

    for index in range(2):
        here = (facts[LO] <= index) & (index < facts[HI])

        @pl.when(here & (facts[PAIRED] > 0))
        def _(index=index):
            low = jnp.where(facts[FRAMES] > 0, index, 2 * index)
            pair = [tile_rows(low), tile_rows(low + jnp.where(facts[FRAMES] > 0, 2, 1))]
            chains(pair, [pair, pair])

        @pl.when(here & (facts[JOINED] + facts[PAIRED] == 0))
        def _(index=index):
            tiles = [pl.ds(tile * TILE, TILE) for tile in (2 * index, 2 * index + 1)]
            chains(tiles, [[tile] for tile in tiles])


def keep(peak, total):
    def write(rows, now, sums):
        peak[rows, :] = now
        total[rows, :] = sums

    return write


def divided(total):
    return (total[:, :DIM] / total[:, DIM:]).astype(jnp.bfloat16)


def own_column(facts, qkv, peak, total):
    @pl.when(facts[OWN] > 0)
    def _():
        visit(qkv.at[:, 2 * DIM :], qkv, facts, None, keep(peak, total))


def cut_half(facts, qkv, half):
    half[:TILE, :] = qkv[tile_rows(facts[FIRST]), : 2 * DIM]
    half[TILE:, :] = qkv[tile_rows(facts[SECOND]), : 2 * DIM]


def put_together(facts, every, half, rest, kv):
    @pl.when(facts[HALVED] == 0)
    def _():
        kv[...] = every[...]

    @pl.when(facts[HALVED] > 0)
    def _():
        kv[tile_rows(facts[FIRST]), :] = half[:TILE, :]
        kv[tile_rows(facts[SECOND]), :] = half[TILE:, :]

    @pl.when(facts[REST] > 0)
    def _():
        kv[2 * TILE :, :] = rest[...]


def upper_column(facts, qkv, every, half, rest, peak_in, total_in, peak, total, kv):
    @pl.when(facts[UPPER] > 0)
    def _():
        put_together(facts, every, half, rest, kv)
        visit(qkv.at[:, 2 * DIM :], kv, facts, (peak_in, total_in), keep(peak, total))

    @pl.when(facts[OWN] > facts[UPPER])
    def _():
        peak[...] = peak_in[...]
        total[...] = total_in[...]


def lower_column(facts, qkv, every, half, rest, peak_in, total_in, out, kv):
    def write(rows, now, sums):
        out[rows, :] = divided(sums)

    @pl.when(facts[LOWER] > 0)
    def _():
        put_together(facts, every, half, rest, kv)
        visit(qkv.at[:, 2 * DIM :], kv, facts, (peak_in, total_in), write)

    @pl.when(facts[OWN] > facts[LOWER])
    def _():
        out[...] = divided(total_in[...])


def unpack(facts, received, out, staged, done):
    copies = []
    for head in range(HEADS):
        staged[:, head * DIM : (head + 1) * DIM] = received[facts[HEAD + head]]
        if head % RUN == RUN - 1:
            columns = pl.ds((head + 1 - RUN) * DIM, RUN * DIM)
            copy = pltpu.make_async_copy(
                staged.at[:, columns], out.at[:, columns], done.at[head // RUN]
            )
            copy.start()
            copies.append(copy)
    for copy in copies:
        copy.wait()


HBM = pl.BlockSpec(memory_space=pltpu.HBM)
SMEM = pl.BlockSpec(memory_space=pltpu.SMEM)
VMEM = pl.BlockSpec(memory_space=pltpu.VMEM)
ORDER = pltpu.SMEM((MEMBERS,), jnp.int32)


def call(kernel, shapes, scalars, operands, scratch=(), after=()):
    def body(*refs):
        given = len(scalars) + len(operands)
        kernel(*refs[:given], *refs[given + len(after) :])

    return pl.pallas_call(
        body,
        out_shape=shapes,
        in_specs=[SMEM] * len(scalars) + [VMEM] * len(operands) + [HBM] * len(after),
        out_specs=jax.tree.map(lambda _: VMEM, shapes),
        scratch_shapes=list(scratch),
        compiler_params=PARAMS,
    )(*scalars, *operands, *after)


def shards(queries, key_vectors, value_vectors, windows):
    tokens, width = queries.shape
    rows = MEMBERS * tokens
    columns = lax.axis_size("col")
    bf16, f32 = jnp.bfloat16, jnp.float32
    place = lax.axis_index("f") * 8 + lax.axis_index("uly")
    info = jnp.stack(
        [place, lax.axis_index("g"), lax.axis_index("col"), lax.axis_index("f")]
    ).astype(jnp.int32)
    win = windows.T
    sources = [key_vectors, value_vectors, queries]
    count = len(sources)

    def pack_kernel(*refs):
        pack(count, *refs)

    def exchange(value):
        return lax.all_to_all(value, GROUP, split_axis=0, concat_axis=0, tiled=True)

    sendable = pl.pallas_call(
        pack_kernel,
        out_shape=jax.ShapeDtypeStruct((MEMBERS, tokens, count * DIM), bf16),
        in_specs=[HBM] * (1 + count),
        out_specs=HBM,
        scratch_shapes=[
            pltpu.SMEM(win.shape, jnp.int32),
            pltpu.VMEM((count, tokens, width), bf16),
            pltpu.VMEM((MEMBERS, tokens, count * DIM), bf16),
            ORDER,
            pltpu.SemaphoreType.DMA,
            pltpu.SemaphoreType.DMA((count, tokens // CHUNK)),
            pltpu.SemaphoreType.DMA((MEMBERS // BATCH,)),
        ],
        compiler_params=pltpu.CompilerParams(vmem_limit_bytes=PACK_VMEM),
    )(win, *sources)
    qkv = exchange(sendable).reshape(rows, count * DIM)

    def facts_kernel(*refs):
        state_facts(columns, *refs)

    facts = pl.pallas_call(
        facts_kernel,
        out_shape=jax.ShapeDtypeStruct((HEAD + HEADS,), jnp.int32),
        in_specs=[SMEM, SMEM],
        out_specs=SMEM,
        scratch_shapes=[ORDER],
        compiler_params=PARAMS,
    )(win, info)

    def beside(value, frame):
        up = [
            (((uly * columns + col) * 2 + frame) * 2, ((uly * columns + col + 1) * 2 + frame) * 2)
            for uly in range(8)
            for col in range(columns - 1)
        ]
        along = ("uly", "col", "f", "g")
        return lax.ppermute(value, along, up), lax.ppermute(value, along, [(b, a) for a, b in up])

    lower, upper = beside(qkv[:, : 2 * DIM], 0)
    half = call(cut_half, jax.ShapeDtypeStruct((rows // 2, 2 * DIM), bf16), [facts], [qkv])
    low_half, up_half = beside(half, 1)

    column = lax.axis_index("col")

    def send_rest(qkv):
        rest = qkv[rows // 2 :, : 2 * DIM]
        near = jnp.abs(jnp.arange(columns) - column) == 1
        sent = jnp.where(near[:, None, None], rest[None], jnp.zeros_like(rest)[None])
        got = lax.all_to_all(sent, "col", split_axis=0, concat_axis=0, tiled=True)
        return tuple(
            lax.dynamic_index_in_dim(got, jnp.clip(at, 0, columns - 1), 0, keepdims=False)
            for at in (column - 1, column + 1)
        )

    def no_rest(qkv):
        return (jnp.zeros((rows // 2, 2 * DIM), bf16),) * 2

    low_rest, up_rest = lax.cond(
        jnp.sum(jnp.prod(windows // 2, axis=1)) > WHOLE, send_rest, no_rest, qkv
    )

    state = (jax.ShapeDtypeStruct((rows, DIM), f32), jax.ShapeDtypeStruct((rows, 2 * DIM), f32))
    peak, total = call(own_column, state, [facts], [qkv], after=[low_rest, up_rest])
    joined = [pltpu.VMEM((rows, 2 * DIM), bf16)]
    peak, total = call(
        upper_column, state, [facts], [qkv, upper, up_half, up_rest, peak, total], joined
    )
    result = call(
        lower_column,
        jax.ShapeDtypeStruct((rows, DIM), bf16),
        [facts],
        [qkv, lower, low_half, low_rest, peak, total],
        joined,
    )
    back = exchange(result.reshape(MEMBERS, tokens, DIM))
    return pl.pallas_call(
        unpack,
        out_shape=jax.ShapeDtypeStruct((tokens, width), bf16),
        in_specs=[SMEM, VMEM],
        out_specs=HBM,
        scratch_shapes=[
            pltpu.VMEM((tokens, width), bf16),
            pltpu.SemaphoreType.DMA((HEADS // RUN,)),
        ],
        compiler_params=PARAMS,
    )(facts, back)


def solution(mesh):
    uly, blk, cfg = (mesh.shape[name] for name in ("uly", "blk", "cfg"))
    fine = Mesh(mesh.devices.reshape(uly, blk // 4, 2, 2, cfg), ("uly", "col", "f", "g", "cfg"))
    tokens = P(("cfg", "col", "f", "g", "uly"), None)
    return jax.shard_map(
        shards,
        mesh=fine,
        in_specs=(tokens, tokens, tokens, P()),
        out_specs=tokens,
        check_vma=False,
    )
```

```python
import jax
import jax.numpy as jnp
from jax import lax
from jax.experimental import pallas as pl
from jax.experimental.pallas import tpu as pltpu
from jax.sharding import Mesh
from jax.sharding import PartitionSpec as P

HEADS = 24
DIM = 128
TILE = 384
PLACES = 16
USED = 12
WHOLE = 8
OWN, LOWER, UPPER, JOINED, PAIRED, FRAMES, LO, HI, HALVED, REST, FIRST, SECOND, HEAD = range(13)
MEMBERS = 2 * PLACES
CHUNK = 16
BATCH = 4
RUN = 8
PACK_VMEM = 62 * 1024 * 1024
GROUP = ("f", "g", "uly")
EXP2_SCALE = DIM**-0.5 * 1.4426950408889634
PARAMS = pltpu.CompilerParams(vmem_limit_bytes=32 * 1024 * 1024)


def is_open(win, axis, head):
    return win[axis, head] // 2


def fill_order(win, order, told=None):
    for place in range(2 * PLACES):
        order[place] = 0

    def put(head, carry):
        joined, apart = carry
        frames, heights, wide = (is_open(win, axis, head) for axis in range(3))
        both = wide * frames * heights
        place = jnp.where(both > 0, joined, USED - 1 - apart)
        place = jnp.where(wide > 0, place, head - joined - apart)
        order[(1 - wide) * PLACES + place] = head
        if told is not None:
            told(head, wide, place, frames, heights)
        return joined + both, apart + wide - both

    lax.fori_loop(0, HEADS, put, (jnp.int32(0), jnp.int32(0)))
    for place in range(WHOLE, USED):
        order[place + USED - WHOLE] = order[place]


def state_facts(columns, win, info, facts, order):
    place, row, column, frame = info[0], info[1], info[2], info[3]

    def count(head, joined):
        return joined + is_open(win, 0, head) * is_open(win, 1, head) * is_open(win, 2, head)

    split = jnp.where(lax.fori_loop(0, HEADS, count, jnp.int32(0)) <= WHOLE, 1, 0)

    def told(head, wide, at, frames, heights):
        half = jnp.where(frames > heights, row, frame)
        at = jnp.where(wide * split * at >= WHOLE, at + (USED - WHOLE) * half, at)
        facts[HEAD + head] = at // 8 * 16 + (1 - wide) * 8 + at % 8

    fill_order(win, order, told)
    head = order[row * PLACES + place]
    frames, heights = is_open(win, 0, head), is_open(win, 1, head)
    shared = jnp.where(place >= WHOLE, 1 - row, 0)
    halved = shared * split
    half = jnp.where(place >= USED, halved, 0)
    used = jnp.where((place < USED) | (halved > 0), 1, 0)
    wide = used * (1 - row)
    facts[OWN] = used
    facts[LOWER] = jnp.where(column > 0, wide, 0)
    facts[UPPER] = jnp.where(column < columns - 1, wide, 0)
    facts[JOINED] = frames * heights
    facts[PAIRED] = frames + heights - 2 * frames * heights
    facts[FRAMES] = frames
    facts[LO] = half
    facts[HI] = jnp.where(halved > 0, half + 1, 2)
    facts[HALVED] = shared
    facts[REST] = shared * (1 - split)
    by_row = halved * jnp.where(frames > heights, 1, 0)
    first = jnp.where(by_row > 0, half, 2 * half)
    facts[FIRST] = first
    facts[SECOND] = first + 1 + by_row


def pack(count, win_hbm, *refs):
    sources = refs[:count]
    out, win, held, staged, order, win_done, done, out_done = refs[-8:]
    first = pltpu.make_async_copy(win_hbm, win, win_done)
    first.start()
    copies = []
    for part, source in enumerate(sources):
        for chunk in range(source.shape[0] // CHUNK):
            rows = pl.ds(chunk * CHUNK, CHUNK)
            copy = pltpu.make_async_copy(
                source.at[rows, :], held.at[part, rows, :], done.at[part, chunk]
            )
            copy.start()
            copies.append(copy)
    first.wait()
    fill_order(win, order)
    for copy in copies:
        copy.wait()
    sent = []
    for member in range(MEMBERS):
        frame, row, uly = member // 16, member // 8 % 2, member % 8
        column = pl.multiple_of(order[row * PLACES + frame * 8 + uly] * DIM, DIM)
        for part in range(count):
            staged[member, :, part * DIM : (part + 1) * DIM] = held[part, :, pl.ds(column, DIM)]
        if member % BATCH == BATCH - 1:
            some = pl.ds(member + 1 - BATCH, BATCH)
            copy = pltpu.make_async_copy(
                staged.at[some], out.at[some], out_done.at[member // BATCH]
            )
            copy.start()
            sent.append(copy)
    for copy in sent:
        copy.wait()


def lanes(column, width):
    return jnp.broadcast_to(column, (column.shape[0], width))


def side_by_side(parts, axis):
    return parts[0] if len(parts) == 1 else jnp.concatenate(parts, axis=axis)


def score(query, kv, keys):
    parts = [
        lax.dot_general(
            query, kv[some, :DIM], (((1,), (1,)), ((), ())), preferred_element_type=jnp.float32
        )
        for some in keys
    ]
    return side_by_side(parts, 1)


def fold(scores, kv, keys, rows, before, write):
    copies = scores.shape[1] // DIM
    now = lanes(jnp.max(scores, axis=1, keepdims=True), DIM)
    if before:
        peak = before[0][rows, :]
        now = jnp.maximum(peak, now)
    weights = jnp.exp2((scores - jnp.concatenate([now] * copies, axis=1)) * EXP2_SCALE)
    values = side_by_side([kv[some, DIM : 2 * DIM] for some in keys], 0)
    with_ones = jnp.concatenate([values, jnp.ones_like(values)], axis=1)
    total = jnp.dot(weights.astype(jnp.bfloat16), with_ones, preferred_element_type=jnp.float32)
    if before:
        fade = jnp.exp2((peak - now) * EXP2_SCALE)
        total = before[1][rows, :] * jnp.concatenate([fade, fade], axis=1) + total
    write(rows, now, total)


def tile_rows(tile):
    return pl.ds(pl.multiple_of(tile * TILE, TILE), TILE)


def visit(query, kv, facts, before, write):
    def chains(blocks, keys):
        ahead = score(query[blocks[0], :], kv, keys[0])
        for index, rows in enumerate(blocks):
            scores = ahead
            if index + 1 < len(blocks):
                ahead = score(query[blocks[index + 1], :], kv, keys[index + 1])
            fold(scores, kv, keys[index], rows, before, write)

    @pl.when(facts[JOINED] > 0)
    def _():
        every = [pl.ds(0, 4 * TILE)]
        chains([pl.ds(512 * block, 512) for block in range(3)], [every] * 3)

    for index in range(2):
        here = (facts[LO] <= index) & (index < facts[HI])

        @pl.when(here & (facts[PAIRED] > 0))
        def _(index=index):
            low = jnp.where(facts[FRAMES] > 0, index, 2 * index)
            pair = [tile_rows(low), tile_rows(low + jnp.where(facts[FRAMES] > 0, 2, 1))]
            chains(pair, [pair, pair])

        @pl.when(here & (facts[JOINED] + facts[PAIRED] == 0))
        def _(index=index):
            tiles = [pl.ds(tile * TILE, TILE) for tile in (2 * index, 2 * index + 1)]
            chains(tiles, [[tile] for tile in tiles])


def keep(peak, total):
    def write(rows, now, sums):
        peak[rows, :] = now
        total[rows, :] = sums

    return write


def divided(total):
    return (total[:, :DIM] / total[:, DIM:]).astype(jnp.bfloat16)


def own_column(facts, qkv, peak, total):
    @pl.when(facts[OWN] > 0)
    def _():
        visit(qkv.at[:, 2 * DIM :], qkv, facts, None, keep(peak, total))


def cut_half(facts, qkv, half):
    half[:TILE, :] = qkv[tile_rows(facts[FIRST]), : 2 * DIM]
    half[TILE:, :] = qkv[tile_rows(facts[SECOND]), : 2 * DIM]


def put_together(facts, every, half, rest, kv):
    @pl.when(facts[HALVED] == 0)
    def _():
        kv[...] = every[...]

    @pl.when(facts[HALVED] > 0)
    def _():
        kv[tile_rows(facts[FIRST]), :] = half[:TILE, :]
        kv[tile_rows(facts[SECOND]), :] = half[TILE:, :]

    @pl.when(facts[REST] > 0)
    def _():
        kv[2 * TILE :, :] = rest[...]


def upper_column(facts, qkv, every, half, rest, peak_in, total_in, peak, total, kv):
    @pl.when(facts[UPPER] > 0)
    def _():
        put_together(facts, every, half, rest, kv)
        visit(qkv.at[:, 2 * DIM :], kv, facts, (peak_in, total_in), keep(peak, total))

    @pl.when(facts[OWN] > facts[UPPER])
    def _():
        peak[...] = peak_in[...]
        total[...] = total_in[...]


def lower_column(facts, qkv, every, half, rest, peak_in, total_in, out, kv):
    def write(rows, now, sums):
        out[rows, :] = divided(sums)

    @pl.when(facts[LOWER] > 0)
    def _():
        put_together(facts, every, half, rest, kv)
        visit(qkv.at[:, 2 * DIM :], kv, facts, (peak_in, total_in), write)

    @pl.when(facts[OWN] > facts[LOWER])
    def _():
        out[...] = divided(total_in[...])


def unpack(facts, received, out, staged, done):
    copies = []
    for head in range(HEADS):
        staged[:, head * DIM : (head + 1) * DIM] = received[facts[HEAD + head]]
        if head % RUN == RUN - 1:
            columns = pl.ds((head + 1 - RUN) * DIM, RUN * DIM)
            copy = pltpu.make_async_copy(
                staged.at[:, columns], out.at[:, columns], done.at[head // RUN]
            )
            copy.start()
            copies.append(copy)
    for copy in copies:
        copy.wait()


HBM = pl.BlockSpec(memory_space=pltpu.HBM)
SMEM = pl.BlockSpec(memory_space=pltpu.SMEM)
VMEM = pl.BlockSpec(memory_space=pltpu.VMEM)
ORDER = pltpu.SMEM((MEMBERS,), jnp.int32)


def call(kernel, shapes, scalars, operands, scratch=(), after=()):
    def body(*refs):
        given = len(scalars) + len(operands)
        kernel(*refs[:given], *refs[given + len(after) :])

    return pl.pallas_call(
        body,
        out_shape=shapes,
        in_specs=[SMEM] * len(scalars) + [VMEM] * len(operands) + [HBM] * len(after),
        out_specs=jax.tree.map(lambda _: VMEM, shapes),
        scratch_shapes=list(scratch),
        compiler_params=PARAMS,
    )(*scalars, *operands, *after)


def shards(queries, key_vectors, value_vectors, windows):
    tokens, width = queries.shape
    rows = MEMBERS * tokens
    columns = lax.axis_size("col")
    bf16, f32 = jnp.bfloat16, jnp.float32
    place = lax.axis_index("f") * 8 + lax.axis_index("uly")
    info = jnp.stack(
        [place, lax.axis_index("g"), lax.axis_index("col"), lax.axis_index("f")]
    ).astype(jnp.int32)
    win = windows.T
    sources = [key_vectors, value_vectors, queries]
    count = len(sources)

    def pack_kernel(*refs):
        pack(count, *refs)

    def exchange(value):
        return lax.all_to_all(value, GROUP, split_axis=0, concat_axis=0, tiled=True)

    sendable = pl.pallas_call(
        pack_kernel,
        out_shape=jax.ShapeDtypeStruct((MEMBERS, tokens, count * DIM), bf16),
        in_specs=[HBM] * (1 + count),
        out_specs=HBM,
        scratch_shapes=[
            pltpu.SMEM(win.shape, jnp.int32),
            pltpu.VMEM((count, tokens, width), bf16),
            pltpu.VMEM((MEMBERS, tokens, count * DIM), bf16),
            ORDER,
            pltpu.SemaphoreType.DMA,
            pltpu.SemaphoreType.DMA((count, tokens // CHUNK)),
            pltpu.SemaphoreType.DMA((MEMBERS // BATCH,)),
        ],
        compiler_params=pltpu.CompilerParams(vmem_limit_bytes=PACK_VMEM),
    )(win, *sources)
    qkv = exchange(sendable)
    def facts_kernel(*refs):
        state_facts(columns, *refs)

    facts = pl.pallas_call(
        facts_kernel,
        out_shape=jax.ShapeDtypeStruct((HEAD + HEADS,), jnp.int32),
        in_specs=[SMEM, SMEM],
        out_specs=SMEM,
        scratch_shapes=[ORDER],
        compiler_params=PARAMS,
    )(win, info)

    whole = jnp.sum(jnp.prod(windows // 2, axis=1)) > WHOLE
    qkv, facts, whole = lax.optimization_barrier((qkv, facts, whole))
    qkv = qkv.reshape(rows, count * DIM)

    def beside(value, frame):
        up = [
            (((uly * columns + col) * 2 + frame) * 2, ((uly * columns + col + 1) * 2 + frame) * 2)
            for uly in range(8)
            for col in range(columns - 1)
        ]
        along = ("uly", "col", "f", "g")
        return lax.ppermute(value, along, up), lax.ppermute(value, along, [(b, a) for a, b in up])

    lower, upper = beside(qkv[:, : 2 * DIM], 0)
    half = call(cut_half, jax.ShapeDtypeStruct((rows // 2, 2 * DIM), bf16), [facts], [qkv])
    low_half, up_half = beside(half, 1)

    column = lax.axis_index("col")

    def send_rest(qkv):
        rest = qkv[rows // 2 :, : 2 * DIM]
        near = jnp.abs(jnp.arange(columns) - column) == 1
        sent = jnp.where(near[:, None, None], rest[None], jnp.zeros_like(rest)[None])
        got = lax.all_to_all(sent, "col", split_axis=0, concat_axis=0, tiled=True)
        return tuple(
            lax.dynamic_index_in_dim(got, jnp.clip(at, 0, columns - 1), 0, keepdims=False)
            for at in (column - 1, column + 1)
        )

    def no_rest(qkv):
        return (jnp.zeros((rows // 2, 2 * DIM), bf16),) * 2

    low_rest, up_rest = lax.cond(whole, send_rest, no_rest, qkv)

    state = (jax.ShapeDtypeStruct((rows, DIM), f32), jax.ShapeDtypeStruct((rows, 2 * DIM), f32))
    peak, total = call(own_column, state, [facts], [qkv], after=[low_rest, up_rest])
    joined = [pltpu.VMEM((rows, 2 * DIM), bf16)]
    peak, total = call(
        upper_column, state, [facts], [qkv, upper, up_half, up_rest, peak, total], joined
    )
    result = call(
        lower_column,
        jax.ShapeDtypeStruct((rows, DIM), bf16),
        [facts],
        [qkv, lower, low_half, low_rest, peak, total],
        joined,
    )
    back = exchange(result.reshape(MEMBERS, tokens, DIM))
    return pl.pallas_call(
        unpack,
        out_shape=jax.ShapeDtypeStruct((tokens, width), bf16),
        in_specs=[SMEM, VMEM],
        out_specs=HBM,
        scratch_shapes=[
            pltpu.VMEM((tokens, width), bf16),
            pltpu.SemaphoreType.DMA((HEADS // RUN,)),
        ],
        compiler_params=PARAMS,
    )(facts, back)


def solution(mesh):
    uly, blk, cfg = (mesh.shape[name] for name in ("uly", "blk", "cfg"))
    fine = Mesh(mesh.devices.reshape(uly, blk // 4, 2, 2, cfg), ("uly", "col", "f", "g", "cfg"))
    tokens = P(("cfg", "col", "f", "g", "uly"), None)
    return jax.shard_map(
        shards,
        mesh=fine,
        in_specs=(tokens, tokens, tokens, P()),
        out_specs=tokens,
        check_vma=False,
    )
```

```python
import jax
import jax.numpy as jnp
from jax import lax
from jax.experimental import pallas as pl
from jax.experimental.pallas import tpu as pltpu
from jax.sharding import Mesh
from jax.sharding import PartitionSpec as P

HEADS = 24
DIM = 128
TILE = 384
PLACES = 16
USED = 12
WHOLE = 8
OWN, ONE, TWO, JOINED, PAIRED, FRAMES, LO, HI, HALVED, REST, FIRST, SECOND, HEAD = range(13)
MEMBERS = 2 * PLACES
CHUNK = 16
BATCH = 4
RUN = 8
PACK_VMEM = 62 * 1024 * 1024
GROUP = ("f", "g", "uly")
EXP2_SCALE = DIM**-0.5 * 1.4426950408889634
PARAMS = pltpu.CompilerParams(vmem_limit_bytes=20 * 1024 * 1024)


def is_open(win, axis, head):
    return win[axis, head] // 2


def fill_order(win, order, told=None):
    for place in range(2 * PLACES):
        order[place] = 0

    def put(head, carry):
        joined, apart = carry
        frames, heights, wide = (is_open(win, axis, head) for axis in range(3))
        both = wide * frames * heights
        place = jnp.where(both > 0, joined, USED - 1 - apart)
        place = jnp.where(wide > 0, place, head - joined - apart)
        order[(1 - wide) * PLACES + place] = head
        if told is not None:
            told(head, wide, place, frames, heights)
        return joined + both, apart + wide - both

    lax.fori_loop(0, HEADS, put, (jnp.int32(0), jnp.int32(0)))
    for place in range(WHOLE, USED):
        order[place + USED - WHOLE] = order[place]


def state_facts(columns, win, info, facts, order):
    place, row, column, frame = info[0], info[1], info[2], info[3]

    def count(head, joined):
        return joined + is_open(win, 0, head) * is_open(win, 1, head) * is_open(win, 2, head)

    split = jnp.where(lax.fori_loop(0, HEADS, count, jnp.int32(0)) <= WHOLE, 1, 0)

    def told(head, wide, at, frames, heights):
        half = jnp.where(frames > heights, row, frame)
        at = jnp.where(wide * split * at >= WHOLE, at + (USED - WHOLE) * half, at)
        facts[HEAD + head] = at // 8 * 16 + (1 - wide) * 8 + at % 8

    fill_order(win, order, told)
    head = order[row * PLACES + place]
    frames, heights = is_open(win, 0, head), is_open(win, 1, head)
    shared = jnp.where(place >= WHOLE, 1 - row, 0)
    halved = shared * split
    half = jnp.where(place >= USED, halved, 0)
    used = jnp.where((place < USED) | (halved > 0), 1, 0)
    wide = used * (1 - row)
    facts[OWN] = used
    lower = jnp.where(column > 0, wide, 0)
    upper = jnp.where(column < columns - 1, wide, 0)
    facts[ONE] = jnp.where(shared > 0, lower, upper)
    facts[TWO] = jnp.where(shared > 0, upper, lower)
    facts[JOINED] = frames * heights
    facts[PAIRED] = frames + heights - 2 * frames * heights
    facts[FRAMES] = frames
    facts[LO] = half
    facts[HI] = jnp.where(halved > 0, half + 1, 2)
    facts[HALVED] = shared
    facts[REST] = shared * (1 - split)
    by_row = halved * jnp.where(frames > heights, 1, 0)
    first = jnp.where(by_row > 0, half, 2 * half)
    facts[FIRST] = first
    facts[SECOND] = first + 1 + by_row


def pack(count, win_hbm, *refs):
    sources = refs[:count]
    out, win, held, staged, order, win_done, done, out_done = refs[-8:]
    first = pltpu.make_async_copy(win_hbm, win, win_done)
    first.start()
    copies = []
    for part, source in enumerate(sources):
        for chunk in range(source.shape[0] // CHUNK):
            rows = pl.ds(chunk * CHUNK, CHUNK)
            copy = pltpu.make_async_copy(
                source.at[rows, :], held.at[part, rows, :], done.at[part, chunk]
            )
            copy.start()
            copies.append(copy)
    first.wait()
    fill_order(win, order)
    for copy in copies:
        copy.wait()
    sent = []
    for member in range(MEMBERS):
        frame, row, uly = member // 16, member // 8 % 2, member % 8
        column = pl.multiple_of(order[row * PLACES + frame * 8 + uly] * DIM, DIM)
        for part in range(count):
            staged[member, :, part * DIM : (part + 1) * DIM] = held[part, :, pl.ds(column, DIM)]
        if member % BATCH == BATCH - 1:
            some = pl.ds(member + 1 - BATCH, BATCH)
            copy = pltpu.make_async_copy(
                staged.at[some], out.at[some], out_done.at[member // BATCH]
            )
            copy.start()
            sent.append(copy)
    for copy in sent:
        copy.wait()


def lanes(column, width):
    return jnp.broadcast_to(column, (column.shape[0], width))


def side_by_side(parts, axis):
    return parts[0] if len(parts) == 1 else jnp.concatenate(parts, axis=axis)


def score(query, kv, keys):
    parts = [
        lax.dot_general(
            query, kv[some, :DIM], (((1,), (1,)), ((), ())), preferred_element_type=jnp.float32
        )
        for some in keys
    ]
    return side_by_side(parts, 1)


def fold(scores, kv, keys, rows, before, write):
    copies = scores.shape[1] // DIM
    now = lanes(jnp.max(scores, axis=1, keepdims=True), DIM)
    if before:
        peak = before[0][rows, :]
        now = jnp.maximum(peak, now)
    weights = jnp.exp2((scores - jnp.concatenate([now] * copies, axis=1)) * EXP2_SCALE)
    values = side_by_side([kv[some, DIM : 2 * DIM] for some in keys], 0)
    with_ones = jnp.concatenate([values, jnp.ones_like(values)], axis=1)
    total = jnp.dot(weights.astype(jnp.bfloat16), with_ones, preferred_element_type=jnp.float32)
    if before:
        fade = jnp.exp2((peak - now) * EXP2_SCALE)
        total = before[1][rows, :] * jnp.concatenate([fade, fade], axis=1) + total
    write(rows, now, total)


def tile_rows(tile):
    return pl.ds(pl.multiple_of(tile * TILE, TILE), TILE)


def visit(query, kv, facts, before, write):
    def chains(blocks, keys):
        ahead = score(query[blocks[0], :], kv, keys[0])
        for index, rows in enumerate(blocks):
            scores = ahead
            if index + 1 < len(blocks):
                ahead = score(query[blocks[index + 1], :], kv, keys[index + 1])
            fold(scores, kv, keys[index], rows, before, write)

    @pl.when(facts[JOINED] > 0)
    def _():
        every = [pl.ds(0, 4 * TILE)]
        chains([pl.ds(512 * block, 512) for block in range(3)], [every] * 3)

    for index in range(2):
        here = (facts[LO] <= index) & (index < facts[HI])

        @pl.when(here & (facts[PAIRED] > 0))
        def _(index=index):
            low = jnp.where(facts[FRAMES] > 0, index, 2 * index)
            pair = [tile_rows(low), tile_rows(low + jnp.where(facts[FRAMES] > 0, 2, 1))]
            chains(pair, [pair, pair])

        @pl.when(here & (facts[JOINED] + facts[PAIRED] == 0))
        def _(index=index):
            tiles = [pl.ds(tile * TILE, TILE) for tile in (2 * index, 2 * index + 1)]
            chains(tiles, [[tile] for tile in tiles])


def keep(peak, total):
    def write(rows, now, sums):
        peak[rows, :] = now
        total[rows, :] = sums

    return write


def divided(total):
    return (total[:, :DIM] / total[:, DIM:]).astype(jnp.bfloat16)


def own_column(facts, qkv, peak, total):
    @pl.when(facts[OWN] > 0)
    def _():
        visit(qkv.at[:, 2 * DIM :], qkv, facts, None, keep(peak, total))


def cut(facts, qkv, half, rest):
    rest[...] = qkv[2 * TILE :, : 2 * DIM]
    half[:TILE, :] = qkv[tile_rows(facts[FIRST]), : 2 * DIM]
    half[TILE:, :] = qkv[tile_rows(facts[SECOND]), : 2 * DIM]


def put_together(facts, every, half, rest, kv):
    @pl.when(facts[HALVED] == 0)
    def _():
        kv[...] = every[...]

    @pl.when(facts[HALVED] > 0)
    def _():
        kv[tile_rows(facts[FIRST]), :] = half[:TILE, :]
        kv[tile_rows(facts[SECOND]), :] = half[TILE:, :]

    @pl.when(facts[REST] > 0)
    def _():
        kv[2 * TILE :, :] = rest[...]


def first_side(facts, qkv, every, half, rest, peak_in, total_in, peak, total, kv):
    @pl.when(facts[ONE] > 0)
    def _():
        put_together(facts, every, half, rest, kv)
        visit(qkv.at[:, 2 * DIM :], kv, facts, (peak_in, total_in), keep(peak, total))

    @pl.when(facts[OWN] > facts[ONE])
    def _():
        peak[...] = peak_in[...]
        total[...] = total_in[...]


def second_side(facts, qkv, every, half, rest, peak_in, total_in, out, kv):
    def write(rows, now, sums):
        out[rows, :] = divided(sums)

    @pl.when(facts[TWO] > 0)
    def _():
        put_together(facts, every, half, rest, kv)
        visit(qkv.at[:, 2 * DIM :], kv, facts, (peak_in, total_in), write)

    @pl.when(facts[OWN] > facts[TWO])
    def _():
        out[...] = divided(total_in[...])


def unpack(facts, received, out, staged, done):
    copies = []
    for head in range(HEADS):
        staged[:, head * DIM : (head + 1) * DIM] = received[facts[HEAD + head]]
        if head % RUN == RUN - 1:
            columns = pl.ds((head + 1 - RUN) * DIM, RUN * DIM)
            copy = pltpu.make_async_copy(
                staged.at[:, columns], out.at[:, columns], done.at[head // RUN]
            )
            copy.start()
            copies.append(copy)
    for copy in copies:
        copy.wait()


HBM = pl.BlockSpec(memory_space=pltpu.HBM)
SMEM = pl.BlockSpec(memory_space=pltpu.SMEM)
VMEM = pl.BlockSpec(memory_space=pltpu.VMEM)
ORDER = pltpu.SMEM((MEMBERS,), jnp.int32)


def call(kernel, shapes, scalars, operands, scratch=(), after=()):
    def body(*refs):
        given = len(scalars) + len(operands)
        kernel(*refs[:given], *refs[given + len(after) :])

    return pl.pallas_call(
        body,
        out_shape=shapes,
        in_specs=[SMEM] * len(scalars) + [VMEM] * len(operands) + [HBM] * len(after),
        out_specs=jax.tree.map(lambda _: VMEM, shapes),
        scratch_shapes=list(scratch),
        compiler_params=PARAMS,
    )(*scalars, *operands, *after)


def shards(queries, key_vectors, value_vectors, windows):
    tokens, width = queries.shape
    rows = MEMBERS * tokens
    columns = lax.axis_size("col")
    bf16, f32 = jnp.bfloat16, jnp.float32
    place = lax.axis_index("f") * 8 + lax.axis_index("uly")
    info = jnp.stack(
        [place, lax.axis_index("g"), lax.axis_index("col"), lax.axis_index("f")]
    ).astype(jnp.int32)
    win = windows.T
    sources = [key_vectors, value_vectors, queries]
    count = len(sources)

    def pack_kernel(*refs):
        pack(count, *refs)

    def exchange(value):
        return lax.all_to_all(value, GROUP, split_axis=0, concat_axis=0, tiled=True)

    sendable = pl.pallas_call(
        pack_kernel,
        out_shape=jax.ShapeDtypeStruct((MEMBERS, tokens, count * DIM), bf16),
        in_specs=[HBM] * (1 + count),
        out_specs=HBM,
        scratch_shapes=[
            pltpu.SMEM(win.shape, jnp.int32),
            pltpu.VMEM((count, tokens, width), bf16),
            pltpu.VMEM((MEMBERS, tokens, count * DIM), bf16),
            ORDER,
            pltpu.SemaphoreType.DMA,
            pltpu.SemaphoreType.DMA((count, tokens // CHUNK)),
            pltpu.SemaphoreType.DMA((MEMBERS // BATCH,)),
        ],
        compiler_params=pltpu.CompilerParams(vmem_limit_bytes=PACK_VMEM),
    )(win, *sources)
    qkv = exchange(sendable)
    def facts_kernel(*refs):
        state_facts(columns, *refs)

    facts = pl.pallas_call(
        facts_kernel,
        out_shape=jax.ShapeDtypeStruct((HEAD + HEADS,), jnp.int32),
        in_specs=[SMEM, SMEM],
        out_specs=SMEM,
        scratch_shapes=[ORDER],
        compiler_params=PARAMS,
    )(win, info)

    whole = jnp.sum(jnp.prod(windows // 2, axis=1)) > WHOLE
    qkv, facts, whole = lax.optimization_barrier((qkv, facts, whole))
    qkv = qkv.reshape(rows, count * DIM)

    def beside(value, frame):
        up = [
            (((uly * columns + col) * 2 + frame) * 2, ((uly * columns + col + 1) * 2 + frame) * 2)
            for uly in range(8)
            for col in range(columns - 1)
        ]
        along = ("uly", "col", "f", "g")
        return lax.ppermute(value, along, up), lax.ppermute(value, along, [(b, a) for a, b in up])

    lower, upper = beside(qkv[:, : 2 * DIM], 0)
    pair = jax.ShapeDtypeStruct((rows // 2, 2 * DIM), bf16)
    half, rest = call(cut, (pair, pair), [facts], [qkv])
    low_half, up_half = beside(half, 1)

    column = lax.axis_index("col")

    def send_rest(rest):
        near = jnp.abs(jnp.arange(columns) - column) == 1
        sent = jnp.where(near[:, None, None], rest[None], jnp.zeros_like(rest)[None])
        got = lax.all_to_all(sent, "col", split_axis=0, concat_axis=0, tiled=True)
        return tuple(
            lax.dynamic_index_in_dim(got, jnp.clip(at, 0, columns - 1), 0, keepdims=False)
            for at in (column - 1, column + 1)
        )

    def no_rest(rest):
        return (jnp.zeros_like(rest),) * 2

    low_rest, up_rest = lax.cond(whole, send_rest, no_rest, rest)

    state = (jax.ShapeDtypeStruct((rows, DIM), f32), jax.ShapeDtypeStruct((rows, 2 * DIM), f32))
    peak, total = call(own_column, state, [facts], [qkv], after=[low_rest, up_rest])
    joined = [pltpu.VMEM((rows, 2 * DIM), bf16)]
    peak, total = call(
        first_side, state, [facts], [qkv, upper, low_half, low_rest, peak, total], joined
    )
    result = call(
        second_side,
        jax.ShapeDtypeStruct((rows, DIM), bf16),
        [facts],
        [qkv, lower, up_half, up_rest, peak, total],
        joined,
    )
    back = exchange(result.reshape(MEMBERS, tokens, DIM))
    return pl.pallas_call(
        unpack,
        out_shape=jax.ShapeDtypeStruct((tokens, width), bf16),
        in_specs=[SMEM, VMEM],
        out_specs=HBM,
        scratch_shapes=[
            pltpu.VMEM((tokens, width), bf16),
            pltpu.SemaphoreType.DMA((HEADS // RUN,)),
        ],
        compiler_params=PARAMS,
    )(facts, back)


def solution(mesh):
    uly, blk, cfg = (mesh.shape[name] for name in ("uly", "blk", "cfg"))
    fine = Mesh(mesh.devices.reshape(uly, blk // 4, 2, 2, cfg), ("uly", "col", "f", "g", "cfg"))
    tokens = P(("cfg", "col", "f", "g", "uly"), None)
    return jax.shard_map(
        shards,
        mesh=fine,
        in_specs=(tokens, tokens, tokens, P()),
        out_specs=tokens,
        check_vma=False,
    )
```

```python
import jax
import jax.numpy as jnp
from jax import lax
from jax.experimental import pallas as pl
from jax.experimental.pallas import tpu as pltpu
from jax.sharding import Mesh
from jax.sharding import PartitionSpec as P

HEADS = 24
DIM = 128
TILE = 384
PLACES = 16
USED = 12
WHOLE = 8
OWN, ONE, TWO, JOINED, PAIRED, FRAMES, LO, HI, HALVED, REST, FIRST, SECOND, HEAD = range(13)
MEMBERS = 2 * PLACES
CHUNK = 16
BATCH = 4
RUN = 8
PACK_VMEM = 62 * 1024 * 1024
GROUP = ("f", "g", "uly")
EXP2_SCALE = DIM**-0.5 * 1.4426950408889634
PARAMS = pltpu.CompilerParams(vmem_limit_bytes=20 * 1024 * 1024)


def is_open(win, axis, head):
    return win[axis, head] // 2


def fill_order(win, order, told=None):
    for place in range(2 * PLACES):
        order[place] = 0

    def put(head, carry):
        joined, apart = carry
        frames, heights, wide = (is_open(win, axis, head) for axis in range(3))
        both = wide * frames * heights
        place = jnp.where(both > 0, joined, USED - 1 - apart)
        place = jnp.where(wide > 0, place, head - joined - apart)
        order[(1 - wide) * PLACES + place] = head
        if told is not None:
            told(head, wide, place, frames, heights)
        return joined + both, apart + wide - both

    lax.fori_loop(0, HEADS, put, (jnp.int32(0), jnp.int32(0)))
    for place in range(WHOLE, USED):
        order[place + USED - WHOLE] = order[place]


def state_facts(columns, win, info, facts, order):
    place, row, column, frame = info[0], info[1], info[2], info[3]

    def count(head, joined):
        return joined + is_open(win, 0, head) * is_open(win, 1, head) * is_open(win, 2, head)

    split = jnp.where(lax.fori_loop(0, HEADS, count, jnp.int32(0)) <= WHOLE, 1, 0)

    def told(head, wide, at, frames, heights):
        half = jnp.where(frames > heights, row, frame)
        at = jnp.where(wide * split * at >= WHOLE, at + (USED - WHOLE) * half, at)
        facts[HEAD + head] = at // 8 * 16 + (1 - wide) * 8 + at % 8

    fill_order(win, order, told)
    head = order[row * PLACES + place]
    frames, heights = is_open(win, 0, head), is_open(win, 1, head)
    shared = jnp.where(place >= WHOLE, 1 - row, 0)
    halved = shared * split
    half = jnp.where(place >= USED, halved, 0)
    used = jnp.where((place < USED) | (halved > 0), 1, 0)
    wide = used * (1 - row)
    facts[OWN] = used
    lower = jnp.where(column > 0, wide, 0)
    upper = jnp.where(column < columns - 1, wide, 0)
    facts[ONE] = jnp.where(shared > 0, lower, upper)
    facts[TWO] = jnp.where(shared > 0, upper, lower)
    facts[JOINED] = frames * heights
    facts[PAIRED] = frames + heights - 2 * frames * heights
    facts[FRAMES] = frames
    facts[LO] = half
    facts[HI] = jnp.where(halved > 0, half + 1, 2)
    facts[HALVED] = shared
    facts[REST] = shared * (1 - split)
    by_row = halved * jnp.where(frames > heights, 1, 0)
    first = jnp.where(by_row > 0, half, 2 * half)
    facts[FIRST] = first
    facts[SECOND] = first + 1 + by_row


def pack(count, win_hbm, *refs):
    sources = refs[:count]
    out, win, held, staged, order, win_done, done, out_done = refs[-8:]
    first = pltpu.make_async_copy(win_hbm, win, win_done)
    first.start()
    copies = []
    for part, source in enumerate(sources):
        for chunk in range(source.shape[0] // CHUNK):
            rows = pl.ds(chunk * CHUNK, CHUNK)
            copy = pltpu.make_async_copy(
                source.at[rows, :], held.at[part, rows, :], done.at[part, chunk]
            )
            copy.start()
            copies.append(copy)
    first.wait()
    fill_order(win, order)
    for copy in copies:
        copy.wait()
    sent = []
    for member in range(MEMBERS):
        frame, row, uly = member // 16, member // 8 % 2, member % 8
        column = pl.multiple_of(order[row * PLACES + frame * 8 + uly] * DIM, DIM)
        for part in range(count):
            staged[member, :, part * DIM : (part + 1) * DIM] = held[part, :, pl.ds(column, DIM)]
        if member % BATCH == BATCH - 1:
            some = pl.ds(member + 1 - BATCH, BATCH)
            copy = pltpu.make_async_copy(
                staged.at[some], out.at[some], out_done.at[member // BATCH]
            )
            copy.start()
            sent.append(copy)
    for copy in sent:
        copy.wait()


def lanes(column, width):
    return jnp.broadcast_to(column, (column.shape[0], width))


def side_by_side(parts, axis):
    return parts[0] if len(parts) == 1 else jnp.concatenate(parts, axis=axis)


def score(query, kv, keys):
    parts = [
        lax.dot_general(
            query, kv[some, :DIM], (((1,), (1,)), ((), ())), preferred_element_type=jnp.float32
        )
        for some in keys
    ]
    return side_by_side(parts, 1)


def fold(scores, kv, keys, rows, before, write):
    copies = scores.shape[1] // DIM
    now = lanes(jnp.max(scores, axis=1, keepdims=True), DIM)
    if before:
        peak = before[0][rows, :]
        now = jnp.maximum(peak, now)
    weights = jnp.exp2((scores - jnp.concatenate([now] * copies, axis=1)) * EXP2_SCALE)
    values = side_by_side([kv[some, DIM : 2 * DIM] for some in keys], 0)
    with_ones = jnp.concatenate([values, jnp.ones_like(values)], axis=1)
    total = jnp.dot(weights.astype(jnp.bfloat16), with_ones, preferred_element_type=jnp.float32)
    if before:
        fade = jnp.exp2((peak - now) * EXP2_SCALE)
        total = before[1][rows, :] * jnp.concatenate([fade, fade], axis=1) + total
    write(rows, now, total)


def tile_rows(tile):
    return pl.ds(pl.multiple_of(tile * TILE, TILE), TILE)


def visit(query, kv, facts, before, write):
    def chains(blocks, keys):
        ahead = score(query[blocks[0], :], kv, keys[0])
        for index, rows in enumerate(blocks):
            scores = ahead
            if index + 1 < len(blocks):
                ahead = score(query[blocks[index + 1], :], kv, keys[index + 1])
            fold(scores, kv, keys[index], rows, before, write)

    @pl.when(facts[JOINED] > 0)
    def _():
        every = [pl.ds(0, 4 * TILE)]
        chains([pl.ds(512 * block, 512) for block in range(3)], [every] * 3)

    for index in range(2):
        here = (facts[LO] <= index) & (index < facts[HI])

        @pl.when(here & (facts[PAIRED] > 0))
        def _(index=index):
            low = jnp.where(facts[FRAMES] > 0, index, 2 * index)
            pair = [tile_rows(low), tile_rows(low + jnp.where(facts[FRAMES] > 0, 2, 1))]
            chains(pair, [pair, pair])

        @pl.when(here & (facts[JOINED] + facts[PAIRED] == 0))
        def _(index=index):
            tiles = [pl.ds(tile * TILE, TILE) for tile in (2 * index, 2 * index + 1)]
            chains(tiles, [[tile] for tile in tiles])


def keep(peak, total):
    def write(rows, now, sums):
        peak[rows, :] = now
        total[rows, :] = sums

    return write


def divided(total):
    return (total[:, :DIM] / total[:, DIM:]).astype(jnp.bfloat16)


def own_column(facts, qkv, peak, total):
    @pl.when(facts[OWN] > 0)
    def _():
        visit(qkv.at[:, 2 * DIM :], qkv, facts, None, keep(peak, total))


def cut(facts, qkv, half, *unwritten):
    del unwritten
    half[:TILE, :] = qkv[tile_rows(facts[FIRST]), : 2 * DIM]
    half[TILE:, :] = qkv[tile_rows(facts[SECOND]), : 2 * DIM]


def put_together(facts, every, half, rest, kv, done):
    @pl.when(facts[HALVED] == 0)
    def _():
        kv[...] = every[...]

    @pl.when(facts[HALVED] > 0)
    def _():
        kv[tile_rows(facts[FIRST]), :] = half[:TILE, :]
        kv[tile_rows(facts[SECOND]), :] = half[TILE:, :]

    @pl.when(facts[REST] > 0)
    def _():
        copy = pltpu.make_async_copy(rest, kv.at[pl.ds(2 * TILE, 2 * TILE), :], done)
        copy.start()
        copy.wait()


def first_side(facts, qkv, every, half, peak_in, total_in, rest, peak, total, kv, done):
    @pl.when(facts[ONE] > 0)
    def _():
        put_together(facts, every, half, rest, kv, done)
        visit(qkv.at[:, 2 * DIM :], kv, facts, (peak_in, total_in), keep(peak, total))

    @pl.when(facts[OWN] > facts[ONE])
    def _():
        peak[...] = peak_in[...]
        total[...] = total_in[...]


def second_side(facts, qkv, every, half, peak_in, total_in, rest, out, kv, done):
    def write(rows, now, sums):
        out[rows, :] = divided(sums)

    @pl.when(facts[TWO] > 0)
    def _():
        put_together(facts, every, half, rest, kv, done)
        visit(qkv.at[:, 2 * DIM :], kv, facts, (peak_in, total_in), write)

    @pl.when(facts[OWN] > facts[TWO])
    def _():
        out[...] = divided(total_in[...])


def unpack(facts, received, out, staged, done):
    copies = []
    for head in range(HEADS):
        staged[:, head * DIM : (head + 1) * DIM] = received[facts[HEAD + head]]
        if head % RUN == RUN - 1:
            columns = pl.ds((head + 1 - RUN) * DIM, RUN * DIM)
            copy = pltpu.make_async_copy(
                staged.at[:, columns], out.at[:, columns], done.at[head // RUN]
            )
            copy.start()
            copies.append(copy)
    for copy in copies:
        copy.wait()


HBM = pl.BlockSpec(memory_space=pltpu.HBM)
SMEM = pl.BlockSpec(memory_space=pltpu.SMEM)
VMEM = pl.BlockSpec(memory_space=pltpu.VMEM)
ORDER = pltpu.SMEM((MEMBERS,), jnp.int32)


def call(kernel, shapes, operands, far=(), scratch=()):
    return pl.pallas_call(
        kernel,
        out_shape=shapes,
        in_specs=[SMEM] + [VMEM] * (len(operands) - 1) + [HBM] * len(far),
        out_specs=jax.tree.map(lambda _: VMEM, shapes),
        scratch_shapes=list(scratch),
        compiler_params=PARAMS,
    )(*operands, *far)


def shards(queries, key_vectors, value_vectors, windows):
    tokens, width = queries.shape
    rows = MEMBERS * tokens
    columns = lax.axis_size("col")
    bf16, f32 = jnp.bfloat16, jnp.float32
    place = lax.axis_index("f") * 8 + lax.axis_index("uly")
    info = jnp.stack(
        [place, lax.axis_index("g"), lax.axis_index("col"), lax.axis_index("f")]
    ).astype(jnp.int32)
    win = windows.T
    sources = [key_vectors, value_vectors, queries]
    count = len(sources)

    def pack_kernel(*refs):
        pack(count, *refs)

    def exchange(value):
        return lax.all_to_all(value, GROUP, split_axis=0, concat_axis=0, tiled=True)

    sendable = pl.pallas_call(
        pack_kernel,
        out_shape=jax.ShapeDtypeStruct((MEMBERS, tokens, count * DIM), bf16),
        in_specs=[HBM] * (1 + count),
        out_specs=HBM,
        scratch_shapes=[
            pltpu.SMEM(win.shape, jnp.int32),
            pltpu.VMEM((count, tokens, width), bf16),
            pltpu.VMEM((MEMBERS, tokens, count * DIM), bf16),
            ORDER,
            pltpu.SemaphoreType.DMA,
            pltpu.SemaphoreType.DMA((count, tokens // CHUNK)),
            pltpu.SemaphoreType.DMA((MEMBERS // BATCH,)),
        ],
        compiler_params=pltpu.CompilerParams(vmem_limit_bytes=PACK_VMEM),
    )(win, *sources)
    qkv = exchange(sendable)
    def facts_kernel(*refs):
        state_facts(columns, *refs)

    facts = pl.pallas_call(
        facts_kernel,
        out_shape=jax.ShapeDtypeStruct((HEAD + HEADS,), jnp.int32),
        in_specs=[SMEM, SMEM],
        out_specs=SMEM,
        scratch_shapes=[ORDER],
        compiler_params=PARAMS,
    )(win, info)

    whole = jnp.sum(jnp.prod(windows // 2, axis=1)) > WHOLE
    qkv, facts, whole = lax.optimization_barrier((qkv, facts, whole))
    qkv = qkv.reshape(rows, count * DIM)

    def beside(value, frame):
        up = [
            (((uly * columns + col) * 2 + frame) * 2, ((uly * columns + col + 1) * 2 + frame) * 2)
            for uly in range(8)
            for col in range(columns - 1)
        ]
        along = ("uly", "col", "f", "g")
        return lax.ppermute(value, along, up), lax.ppermute(value, along, [(b, a) for a, b in up])

    kv = qkv[:, : 2 * DIM]
    lower, upper = beside(kv, 0)
    pair = jax.ShapeDtypeStruct((rows // 2, 2 * DIM), bf16)
    half, *rests = pl.pallas_call(
        cut,
        out_shape=(pair, pair, pair),
        in_specs=[SMEM, VMEM],
        out_specs=(VMEM, HBM, HBM),
        compiler_params=PARAMS,
    )(facts, qkv)
    low_half, up_half = beside(half, 1)

    column = lax.axis_index("col")

    def send_rest(carry):
        rest = kv[rows // 2 :]
        near = jnp.abs(jnp.arange(columns) - column) == 1
        sent = jnp.where(near[:, None, None], rest[None], jnp.zeros_like(rest)[None])
        got = lax.all_to_all(sent, "col", split_axis=0, concat_axis=0, tiled=True)
        low, up = (
            lax.dynamic_index_in_dim(got, jnp.clip(at, 0, columns - 1), 0, keepdims=False)
            for at in (column - 1, column + 1)
        )
        return carry[0] - 1, low, up

    _, low_rest, up_rest = lax.while_loop(
        lambda carry: carry[0] > 0, send_rest, (whole.astype(jnp.int32), *rests)
    )

    state = (jax.ShapeDtypeStruct((rows, DIM), f32), jax.ShapeDtypeStruct((rows, 2 * DIM), f32))

    def own_kernel(facts, qkv, low_rest, up_rest, peak, total):
        del low_rest, up_rest
        own_column(facts, qkv, peak, total)

    peak, total = call(own_kernel, state, [facts, qkv], [low_rest, up_rest])
    joined = [pltpu.VMEM((rows, 2 * DIM), bf16), pltpu.SemaphoreType.DMA]
    peak, total = call(
        first_side, state, [facts, qkv, upper, low_half, peak, total], [low_rest], joined
    )
    result = call(
        second_side,
        jax.ShapeDtypeStruct((rows, DIM), bf16),
        [facts, qkv, lower, up_half, peak, total],
        [up_rest],
        joined,
    )
    back = exchange(result.reshape(MEMBERS, tokens, DIM))
    return pl.pallas_call(
        unpack,
        out_shape=jax.ShapeDtypeStruct((tokens, width), bf16),
        in_specs=[SMEM, VMEM],
        out_specs=HBM,
        scratch_shapes=[
            pltpu.VMEM((tokens, width), bf16),
            pltpu.SemaphoreType.DMA((HEADS // RUN,)),
        ],
        compiler_params=PARAMS,
    )(facts, back)


def solution(mesh):
    uly, blk, cfg = (mesh.shape[name] for name in ("uly", "blk", "cfg"))
    fine = Mesh(mesh.devices.reshape(uly, blk // 4, 2, 2, cfg), ("uly", "col", "f", "g", "cfg"))
    tokens = P(("cfg", "col", "f", "g", "uly"), None)
    return jax.shard_map(
        shards,
        mesh=fine,
        in_specs=(tokens, tokens, tokens, P()),
        out_specs=tokens,
        check_vma=False,
    )
```

```python
import jax
import jax.numpy as jnp
from jax import lax
from jax.experimental import pallas as pl
from jax.experimental.pallas import tpu as pltpu
from jax.sharding import Mesh
from jax.sharding import PartitionSpec as P

HEADS = 24
DIM = 128
TILE = 384
PLACES = 16
USED = 12
WHOLE = 8
OWN, ONE, TWO, JOINED, PAIRED, FRAMES, LO, HI, HALVED, REST, FIRST, SECOND, HEAD = range(13)
MEMBERS = 2 * PLACES
CHUNK = 16
BATCH = 4
RUN = 8
PACK_VMEM = 62 * 1024 * 1024
GROUP = ("f", "g", "uly")
EXP2_SCALE = DIM**-0.5 * 1.4426950408889634
PARAMS = pltpu.CompilerParams(vmem_limit_bytes=20 * 1024 * 1024)


def is_open(win, axis, head):
    return win[axis, head] // 2


def fill_order(win, order, told=None):
    for place in range(2 * PLACES):
        order[place] = 0

    def put(head, carry):
        joined, apart = carry
        frames, heights, wide = (is_open(win, axis, head) for axis in range(3))
        both = wide * frames * heights
        place = jnp.where(both > 0, joined, USED - 1 - apart)
        place = jnp.where(wide > 0, place, head - joined - apart)
        order[(1 - wide) * PLACES + place] = head
        if told is not None:
            told(head, wide, place, frames, heights)
        return joined + both, apart + wide - both

    lax.fori_loop(0, HEADS, put, (jnp.int32(0), jnp.int32(0)))
    for place in range(WHOLE, USED):
        order[place + USED - WHOLE] = order[place]


def state_facts(columns, win, info, facts, order):
    place, row, column, frame = info[0], info[1], info[2], info[3]

    def count(head, joined):
        return joined + is_open(win, 0, head) * is_open(win, 1, head) * is_open(win, 2, head)

    split = jnp.where(lax.fori_loop(0, HEADS, count, jnp.int32(0)) <= WHOLE, 1, 0)

    def told(head, wide, at, frames, heights):
        half = jnp.where(frames > heights, row, frame)
        at = jnp.where(wide * split * at >= WHOLE, at + (USED - WHOLE) * half, at)
        facts[HEAD + head] = at // 8 * 16 + (1 - wide) * 8 + at % 8

    fill_order(win, order, told)
    head = order[row * PLACES + place]
    frames, heights = is_open(win, 0, head), is_open(win, 1, head)
    shared = jnp.where(place >= WHOLE, 1 - row, 0)
    halved = shared * split
    half = jnp.where(place >= USED, halved, 0)
    used = jnp.where((place < USED) | (halved > 0), 1, 0)
    wide = used * (1 - row)
    facts[OWN] = used
    lower = jnp.where(column > 0, wide, 0)
    upper = jnp.where(column < columns - 1, wide, 0)
    facts[ONE] = jnp.where(shared > 0, lower, upper)
    facts[TWO] = jnp.where(shared > 0, upper, lower)
    facts[JOINED] = frames * heights
    facts[PAIRED] = frames + heights - 2 * frames * heights
    facts[FRAMES] = frames
    facts[LO] = half
    facts[HI] = jnp.where(halved > 0, half + 1, 2)
    facts[HALVED] = shared
    facts[REST] = shared * (1 - split)
    by_row = halved * jnp.where(frames > heights, 1, 0)
    first = jnp.where(by_row > 0, half, 2 * half)
    facts[FIRST] = first
    facts[SECOND] = first + 1 + by_row


def pack(count, win_hbm, *refs):
    sources = refs[:count]
    out, win, held, staged, order, win_done, done, out_done = refs[-8:]
    first = pltpu.make_async_copy(win_hbm, win, win_done)
    first.start()
    copies = []
    for part, source in enumerate(sources):
        for chunk in range(source.shape[0] // CHUNK):
            rows = pl.ds(chunk * CHUNK, CHUNK)
            copy = pltpu.make_async_copy(
                source.at[rows, :], held.at[part, rows, :], done.at[part, chunk]
            )
            copy.start()
            copies.append(copy)
    first.wait()
    fill_order(win, order)
    for copy in copies:
        copy.wait()
    sent = []
    for member in range(MEMBERS):
        frame, row, uly = member // 16, member // 8 % 2, member % 8
        column = pl.multiple_of(order[row * PLACES + frame * 8 + uly] * DIM, DIM)
        for part in range(count):
            staged[member, :, part * DIM : (part + 1) * DIM] = held[part, :, pl.ds(column, DIM)]
        if member % BATCH == BATCH - 1:
            some = pl.ds(member + 1 - BATCH, BATCH)
            copy = pltpu.make_async_copy(
                staged.at[some], out.at[some], out_done.at[member // BATCH]
            )
            copy.start()
            sent.append(copy)
    for copy in sent:
        copy.wait()


def lanes(column, width):
    return jnp.broadcast_to(column, (column.shape[0], width))


def side_by_side(parts, axis):
    return parts[0] if len(parts) == 1 else jnp.concatenate(parts, axis=axis)


def score(query, kv, keys):
    parts = [
        lax.dot_general(
            query, kv[some, :DIM], (((1,), (1,)), ((), ())), preferred_element_type=jnp.float32
        )
        for some in keys
    ]
    return side_by_side(parts, 1)


def fold(scores, kv, keys, rows, before, write):
    copies = scores.shape[1] // DIM
    now = lanes(jnp.max(scores, axis=1, keepdims=True), DIM)
    if before:
        peak = before[0][rows, :]
        now = jnp.maximum(peak, now)
    weights = jnp.exp2((scores - jnp.concatenate([now] * copies, axis=1)) * EXP2_SCALE)
    values = side_by_side([kv[some, DIM : 2 * DIM] for some in keys], 0)
    with_ones = jnp.concatenate([values, jnp.ones_like(values)], axis=1)
    total = jnp.dot(weights.astype(jnp.bfloat16), with_ones, preferred_element_type=jnp.float32)
    if before:
        fade = jnp.exp2((peak - now) * EXP2_SCALE)
        total = before[1][rows, :] * jnp.concatenate([fade, fade], axis=1) + total
    write(rows, now, total)


def tile_rows(tile):
    return pl.ds(pl.multiple_of(tile * TILE, TILE), TILE)


def visit(query, kv, facts, before, write):
    def chains(blocks, keys):
        ahead = score(query[blocks[0], :], kv, keys[0])
        for index, rows in enumerate(blocks):
            scores = ahead
            if index + 1 < len(blocks):
                ahead = score(query[blocks[index + 1], :], kv, keys[index + 1])
            fold(scores, kv, keys[index], rows, before, write)

    @pl.when(facts[JOINED] > 0)
    def _():
        every = [pl.ds(0, 4 * TILE)]
        chains([pl.ds(512 * block, 512) for block in range(3)], [every] * 3)

    for index in range(2):
        here = (facts[LO] <= index) & (index < facts[HI])

        @pl.when(here & (facts[PAIRED] > 0))
        def _(index=index):
            low = jnp.where(facts[FRAMES] > 0, index, 2 * index)
            pair = [tile_rows(low), tile_rows(low + jnp.where(facts[FRAMES] > 0, 2, 1))]
            chains(pair, [pair, pair])

        @pl.when(here & (facts[JOINED] + facts[PAIRED] == 0))
        def _(index=index):
            tiles = [pl.ds(tile * TILE, TILE) for tile in (2 * index, 2 * index + 1)]
            chains(tiles, [[tile] for tile in tiles])


def keep(peak, total):
    def write(rows, now, sums):
        peak[rows, :] = now
        total[rows, :] = sums

    return write


def divided(total):
    return (total[:, :DIM] / total[:, DIM:]).astype(jnp.bfloat16)


def own_column(facts, qkv, peak, total):
    @pl.when(facts[OWN] > 0)
    def _():
        visit(qkv.at[:, 2 * DIM :], qkv, facts, None, keep(peak, total))


def cut(facts, qkv, half):
    half[:TILE, :] = qkv[tile_rows(facts[FIRST]), : 2 * DIM]
    half[TILE:, :] = qkv[tile_rows(facts[SECOND]), : 2 * DIM]


def put_together(facts, every, half, rest, kv, done):
    @pl.when(facts[HALVED] == 0)
    def _():
        kv[...] = every[...]

    @pl.when(facts[HALVED] > 0)
    def _():
        kv[tile_rows(facts[FIRST]), :] = half[:TILE, :]
        kv[tile_rows(facts[SECOND]), :] = half[TILE:, :]

    @pl.when(facts[REST] > 0)
    def _():
        copy = pltpu.make_async_copy(rest, kv.at[pl.ds(2 * TILE, 2 * TILE), :], done)
        copy.start()
        copy.wait()


def first_side(facts, qkv, every, half, peak_in, total_in, rest, peak, total, kv, done):
    @pl.when(facts[ONE] > 0)
    def _():
        put_together(facts, every, half, rest, kv, done)
        visit(qkv.at[:, 2 * DIM :], kv, facts, (peak_in, total_in), keep(peak, total))

    @pl.when(facts[OWN] > facts[ONE])
    def _():
        peak[...] = peak_in[...]
        total[...] = total_in[...]


def second_side(facts, qkv, every, half, peak_in, total_in, rest, out, kv, done):
    def write(rows, now, sums):
        out[rows, :] = divided(sums)

    @pl.when(facts[TWO] > 0)
    def _():
        put_together(facts, every, half, rest, kv, done)
        visit(qkv.at[:, 2 * DIM :], kv, facts, (peak_in, total_in), write)

    @pl.when(facts[OWN] > facts[TWO])
    def _():
        out[...] = divided(total_in[...])


def unpack(facts, received, out, staged, done):
    copies = []
    for head in range(HEADS):
        staged[:, head * DIM : (head + 1) * DIM] = received[facts[HEAD + head]]
        if head % RUN == RUN - 1:
            columns = pl.ds((head + 1 - RUN) * DIM, RUN * DIM)
            copy = pltpu.make_async_copy(
                staged.at[:, columns], out.at[:, columns], done.at[head // RUN]
            )
            copy.start()
            copies.append(copy)
    for copy in copies:
        copy.wait()


HBM = pl.BlockSpec(memory_space=pltpu.HBM)
SMEM = pl.BlockSpec(memory_space=pltpu.SMEM)
VMEM = pl.BlockSpec(memory_space=pltpu.VMEM)
ORDER = pltpu.SMEM((MEMBERS,), jnp.int32)


def call(kernel, shapes, operands, far=(), scratch=()):
    return pl.pallas_call(
        kernel,
        out_shape=shapes,
        in_specs=[SMEM] + [VMEM] * (len(operands) - 1) + [HBM] * len(far),
        out_specs=jax.tree.map(lambda _: VMEM, shapes),
        scratch_shapes=list(scratch),
        compiler_params=PARAMS,
    )(*operands, *far)


def shards(queries, key_vectors, value_vectors, windows):
    tokens, width = queries.shape
    rows = MEMBERS * tokens
    columns = lax.axis_size("col")
    bf16, f32 = jnp.bfloat16, jnp.float32
    place = lax.axis_index("f") * 8 + lax.axis_index("uly")
    info = jnp.stack(
        [place, lax.axis_index("g"), lax.axis_index("col"), lax.axis_index("f")]
    ).astype(jnp.int32)
    win = windows.T
    sources = [key_vectors, value_vectors, queries]
    count = len(sources)

    def pack_kernel(*refs):
        pack(count, *refs)

    def exchange(value):
        return lax.all_to_all(value, GROUP, split_axis=0, concat_axis=0, tiled=True)

    sendable = pl.pallas_call(
        pack_kernel,
        out_shape=jax.ShapeDtypeStruct((MEMBERS, tokens, count * DIM), bf16),
        in_specs=[HBM] * (1 + count),
        out_specs=HBM,
        scratch_shapes=[
            pltpu.SMEM(win.shape, jnp.int32),
            pltpu.VMEM((count, tokens, width), bf16),
            pltpu.VMEM((MEMBERS, tokens, count * DIM), bf16),
            ORDER,
            pltpu.SemaphoreType.DMA,
            pltpu.SemaphoreType.DMA((count, tokens // CHUNK)),
            pltpu.SemaphoreType.DMA((MEMBERS // BATCH,)),
        ],
        compiler_params=pltpu.CompilerParams(vmem_limit_bytes=PACK_VMEM),
    )(win, *sources)
    qkv = exchange(sendable)
    def facts_kernel(win, info, facts, low_rest, up_rest, order):
        del low_rest, up_rest
        state_facts(columns, win, info, facts, order)

    pair = jax.ShapeDtypeStruct((rows // 2, 2 * DIM), bf16)
    facts, *rests = pl.pallas_call(
        facts_kernel,
        out_shape=(jax.ShapeDtypeStruct((HEAD + HEADS,), jnp.int32), pair, pair),
        in_specs=[SMEM, SMEM],
        out_specs=(SMEM, HBM, HBM),
        scratch_shapes=[ORDER],
        compiler_params=PARAMS,
    )(win, info)

    whole = jnp.sum(jnp.prod(windows // 2, axis=1)) > WHOLE
    qkv, facts, whole = lax.optimization_barrier((qkv, facts, whole))
    qkv = qkv.reshape(rows, count * DIM)

    def beside(value, frame):
        up = [
            (((uly * columns + col) * 2 + frame) * 2, ((uly * columns + col + 1) * 2 + frame) * 2)
            for uly in range(8)
            for col in range(columns - 1)
        ]
        along = ("uly", "col", "f", "g")
        return lax.ppermute(value, along, up), lax.ppermute(value, along, [(b, a) for a, b in up])

    kv = qkv[:, : 2 * DIM]
    lower, upper = beside(kv, 0)
    half = call(cut, pair, [facts, qkv])
    low_half, up_half = beside(half, 1)

    column = lax.axis_index("col")

    def send_rest(carry):
        rest = kv[rows // 2 :]
        near = jnp.abs(jnp.arange(columns) - column) == 1
        sent = jnp.where(near[:, None, None], rest[None], jnp.zeros_like(rest)[None])
        got = lax.all_to_all(sent, "col", split_axis=0, concat_axis=0, tiled=True)
        low, up = (
            lax.dynamic_index_in_dim(got, jnp.clip(at, 0, columns - 1), 0, keepdims=False)
            for at in (column - 1, column + 1)
        )
        return carry[0] - 1, low, up

    _, low_rest, up_rest = lax.while_loop(
        lambda carry: carry[0] > 0, send_rest, (whole.astype(jnp.int32), *rests)
    )

    state = (jax.ShapeDtypeStruct((rows, DIM), f32), jax.ShapeDtypeStruct((rows, 2 * DIM), f32))

    def own_kernel(facts, qkv, low_rest, up_rest, peak, total):
        del low_rest, up_rest
        own_column(facts, qkv, peak, total)

    peak, total = call(own_kernel, state, [facts, qkv], [low_rest, up_rest])
    joined = [pltpu.VMEM((rows, 2 * DIM), bf16), pltpu.SemaphoreType.DMA]
    peak, total = call(
        first_side, state, [facts, qkv, upper, low_half, peak, total], [low_rest], joined
    )
    result = call(
        second_side,
        jax.ShapeDtypeStruct((rows, DIM), bf16),
        [facts, qkv, lower, up_half, peak, total],
        [up_rest],
        joined,
    )
    back = exchange(result.reshape(MEMBERS, tokens, DIM))
    return pl.pallas_call(
        unpack,
        out_shape=jax.ShapeDtypeStruct((tokens, width), bf16),
        in_specs=[SMEM, VMEM],
        out_specs=HBM,
        scratch_shapes=[
            pltpu.VMEM((tokens, width), bf16),
            pltpu.SemaphoreType.DMA((HEADS // RUN,)),
        ],
        compiler_params=PARAMS,
    )(facts, back)


def solution(mesh):
    uly, blk, cfg = (mesh.shape[name] for name in ("uly", "blk", "cfg"))
    fine = Mesh(mesh.devices.reshape(uly, blk // 4, 2, 2, cfg), ("uly", "col", "f", "g", "cfg"))
    tokens = P(("cfg", "col", "f", "g", "uly"), None)
    return jax.shard_map(
        shards,
        mesh=fine,
        in_specs=(tokens, tokens, tokens, P()),
        out_specs=tokens,
        check_vma=False,
    )
```

```python
import jax
import jax.numpy as jnp
from jax import lax
from jax.experimental import pallas as pl
from jax.experimental.pallas import tpu as pltpu
from jax.sharding import Mesh
from jax.sharding import PartitionSpec as P

HEADS = 24
DIM = 128
TILE = 384
PLACES = 16
USED = 12
WHOLE = 8
OWN, ONE, TWO, JOINED, PAIRED, FRAMES, LO, HI, HALVED, REST, FIRST, SECOND, HEAD = range(13)
MEMBERS = 2 * PLACES
CHUNK = 16
BATCH = 4
RUN = 8
PACK_VMEM = 62 * 1024 * 1024
GROUP = ("f", "g", "uly")
EXP2_SCALE = DIM**-0.5 * 1.4426950408889634
PARAMS = pltpu.CompilerParams(vmem_limit_bytes=20 * 1024 * 1024)


def is_open(win, axis, head):
    return win[axis, head] // 2


def fill_order(win, order, told=None):
    for place in range(2 * PLACES):
        order[place] = 0

    def put(head, carry):
        joined, apart = carry
        frames, heights, wide = (is_open(win, axis, head) for axis in range(3))
        both = wide * frames * heights
        place = jnp.where(both > 0, joined, USED - 1 - apart)
        place = jnp.where(wide > 0, place, head - joined - apart)
        order[(1 - wide) * PLACES + place] = head
        if told is not None:
            told(head, wide, place, frames, heights)
        return joined + both, apart + wide - both

    lax.fori_loop(0, HEADS, put, (jnp.int32(0), jnp.int32(0)))
    for place in range(WHOLE, USED):
        order[place + USED - WHOLE] = order[place]


def state_facts(columns, win, info, facts, order):
    place, row, column, frame = info[0], info[1], info[2], info[3]

    def count(head, joined):
        return joined + is_open(win, 0, head) * is_open(win, 1, head) * is_open(win, 2, head)

    split = jnp.where(lax.fori_loop(0, HEADS, count, jnp.int32(0)) <= WHOLE, 1, 0)

    def told(head, wide, at, frames, heights):
        half = jnp.where(frames > heights, row, frame)
        at = jnp.where(wide * split * at >= WHOLE, at + (USED - WHOLE) * half, at)
        facts[HEAD + head] = at // 8 * 16 + (1 - wide) * 8 + at % 8

    fill_order(win, order, told)
    head = order[row * PLACES + place]
    frames, heights = is_open(win, 0, head), is_open(win, 1, head)
    shared = jnp.where(place >= WHOLE, 1 - row, 0)
    halved = shared * split
    half = jnp.where(place >= USED, halved, 0)
    used = jnp.where((place < USED) | (halved > 0), 1, 0)
    wide = used * (1 - row)
    facts[OWN] = used
    lower = jnp.where(column > 0, wide, 0)
    upper = jnp.where(column < columns - 1, wide, 0)
    facts[ONE] = jnp.where(shared > 0, lower, upper)
    facts[TWO] = jnp.where(shared > 0, upper, lower)
    facts[JOINED] = frames * heights
    facts[PAIRED] = frames + heights - 2 * frames * heights
    facts[FRAMES] = frames
    facts[LO] = half
    facts[HI] = jnp.where(halved > 0, half + 1, 2)
    facts[HALVED] = shared
    facts[REST] = shared * (1 - split)
    by_row = halved * jnp.where(frames > heights, 1, 0)
    first = jnp.where(by_row > 0, half, 2 * half)
    facts[FIRST] = first
    facts[SECOND] = first + 1 + by_row


def pack(count, win_hbm, *refs):
    sources = refs[:count]
    out, win, held, staged, order, win_done, done, out_done = refs[-8:]
    first = pltpu.make_async_copy(win_hbm, win, win_done)
    first.start()
    copies = []
    for part, source in enumerate(sources):
        for chunk in range(source.shape[0] // CHUNK):
            rows = pl.ds(chunk * CHUNK, CHUNK)
            copy = pltpu.make_async_copy(
                source.at[rows, :], held.at[part, rows, :], done.at[part, chunk]
            )
            copy.start()
            copies.append(copy)
    first.wait()
    fill_order(win, order)
    for copy in copies:
        copy.wait()
    sent = []
    for member in range(MEMBERS):
        frame, row, uly = member // 16, member // 8 % 2, member % 8
        column = pl.multiple_of(order[row * PLACES + frame * 8 + uly] * DIM, DIM)
        for part in range(count):
            staged[member, :, part * DIM : (part + 1) * DIM] = held[part, :, pl.ds(column, DIM)]
        if member % BATCH == BATCH - 1:
            some = pl.ds(member + 1 - BATCH, BATCH)
            copy = pltpu.make_async_copy(
                staged.at[some], out.at[some], out_done.at[member // BATCH]
            )
            copy.start()
            sent.append(copy)
    for copy in sent:
        copy.wait()


def lanes(column, width):
    return jnp.broadcast_to(column, (column.shape[0], width))


def side_by_side(parts, axis):
    return parts[0] if len(parts) == 1 else jnp.concatenate(parts, axis=axis)


def score(query, kv, keys):
    parts = [
        lax.dot_general(
            query, kv[some, :DIM], (((1,), (1,)), ((), ())), preferred_element_type=jnp.float32
        )
        for some in keys
    ]
    return side_by_side(parts, 1)


def fold(scores, kv, keys, rows, before, write):
    copies = scores.shape[1] // DIM
    now = lanes(jnp.max(scores, axis=1, keepdims=True), DIM)
    if before:
        peak = before[0][rows, :]
        now = jnp.maximum(peak, now)
    weights = jnp.exp2((scores - jnp.concatenate([now] * copies, axis=1)) * EXP2_SCALE)
    values = side_by_side([kv[some, DIM : 2 * DIM] for some in keys], 0)
    with_ones = jnp.concatenate([values, jnp.ones_like(values)], axis=1)
    total = jnp.dot(weights.astype(jnp.bfloat16), with_ones, preferred_element_type=jnp.float32)
    if before:
        fade = jnp.exp2((peak - now) * EXP2_SCALE)
        total = before[1][rows, :] * jnp.concatenate([fade, fade], axis=1) + total
    write(rows, now, total)


def tile_rows(tile):
    return pl.ds(pl.multiple_of(tile * TILE, TILE), TILE)


def visit(query, kv, facts, before, write):
    def chains(blocks, keys):
        ahead = score(query[blocks[0], :], kv, keys[0])
        for index, rows in enumerate(blocks):
            scores = ahead
            if index + 1 < len(blocks):
                ahead = score(query[blocks[index + 1], :], kv, keys[index + 1])
            fold(scores, kv, keys[index], rows, before, write)

    @pl.when(facts[JOINED] > 0)
    def _():
        every = [pl.ds(0, 4 * TILE)]
        chains([pl.ds(512 * block, 512) for block in range(3)], [every] * 3)

    for index in range(2):
        here = (facts[LO] <= index) & (index < facts[HI])

        @pl.when(here & (facts[PAIRED] > 0))
        def _(index=index):
            low = jnp.where(facts[FRAMES] > 0, index, 2 * index)
            pair = [tile_rows(low), tile_rows(low + jnp.where(facts[FRAMES] > 0, 2, 1))]
            chains(pair, [pair, pair])

        @pl.when(here & (facts[JOINED] + facts[PAIRED] == 0))
        def _(index=index):
            tiles = [pl.ds(tile * TILE, TILE) for tile in (2 * index, 2 * index + 1)]
            chains(tiles, [[tile] for tile in tiles])


def keep(peak, total):
    def write(rows, now, sums):
        peak[rows, :] = now
        total[rows, :] = sums

    return write


def divided(total):
    return (total[:, :DIM] / total[:, DIM:]).astype(jnp.bfloat16)


def own_column(facts, qkv, peak, total):
    @pl.when(facts[OWN] > 0)
    def _():
        visit(qkv.at[:, 2 * DIM :], qkv, facts, None, keep(peak, total))


def cut(facts, qkv, half, rest):
    rest[...] = qkv[2 * TILE :, : 2 * DIM]
    half[:TILE, :] = qkv[tile_rows(facts[FIRST]), : 2 * DIM]
    half[TILE:, :] = qkv[tile_rows(facts[SECOND]), : 2 * DIM]


def put_together(facts, every, half, rest, kv, done):
    @pl.when(facts[HALVED] == 0)
    def _():
        kv[...] = every[...]

    @pl.when(facts[HALVED] > 0)
    def _():
        kv[tile_rows(facts[FIRST]), :] = half[:TILE, :]
        kv[tile_rows(facts[SECOND]), :] = half[TILE:, :]

    @pl.when(facts[REST] > 0)
    def _():
        copy = pltpu.make_async_copy(rest, kv.at[pl.ds(2 * TILE, 2 * TILE), :], done)
        copy.start()
        copy.wait()


def first_side(facts, qkv, every, half, peak_in, total_in, rest, peak, total, kv, done):
    @pl.when(facts[ONE] > 0)
    def _():
        put_together(facts, every, half, rest, kv, done)
        visit(qkv.at[:, 2 * DIM :], kv, facts, (peak_in, total_in), keep(peak, total))

    @pl.when(facts[OWN] > facts[ONE])
    def _():
        peak[...] = peak_in[...]
        total[...] = total_in[...]


def second_side(facts, qkv, every, half, peak_in, total_in, rest, out, kv, done):
    def write(rows, now, sums):
        out[rows, :] = divided(sums)

    @pl.when(facts[TWO] > 0)
    def _():
        put_together(facts, every, half, rest, kv, done)
        visit(qkv.at[:, 2 * DIM :], kv, facts, (peak_in, total_in), write)

    @pl.when(facts[OWN] > facts[TWO])
    def _():
        out[...] = divided(total_in[...])


def unpack(facts, received, out, staged, done):
    copies = []
    for head in range(HEADS):
        staged[:, head * DIM : (head + 1) * DIM] = received[facts[HEAD + head]]
        if head % RUN == RUN - 1:
            columns = pl.ds((head + 1 - RUN) * DIM, RUN * DIM)
            copy = pltpu.make_async_copy(
                staged.at[:, columns], out.at[:, columns], done.at[head // RUN]
            )
            copy.start()
            copies.append(copy)
    for copy in copies:
        copy.wait()


HBM = pl.BlockSpec(memory_space=pltpu.HBM)
SMEM = pl.BlockSpec(memory_space=pltpu.SMEM)
VMEM = pl.BlockSpec(memory_space=pltpu.VMEM)
ORDER = pltpu.SMEM((MEMBERS,), jnp.int32)


def call(kernel, shapes, operands, far=(), scratch=()):
    return pl.pallas_call(
        kernel,
        out_shape=shapes,
        in_specs=[SMEM] + [VMEM] * (len(operands) - 1) + [HBM] * len(far),
        out_specs=jax.tree.map(lambda _: VMEM, shapes),
        scratch_shapes=list(scratch),
        compiler_params=PARAMS,
    )(*operands, *far)


def shards(queries, key_vectors, value_vectors, windows):
    tokens, width = queries.shape
    rows = MEMBERS * tokens
    columns = lax.axis_size("col")
    bf16, f32 = jnp.bfloat16, jnp.float32
    place = lax.axis_index("f") * 8 + lax.axis_index("uly")
    info = jnp.stack(
        [place, lax.axis_index("g"), lax.axis_index("col"), lax.axis_index("f")]
    ).astype(jnp.int32)
    win = windows.T
    sources = [key_vectors, value_vectors, queries]
    count = len(sources)

    def pack_kernel(*refs):
        pack(count, *refs)

    def exchange(value):
        return lax.all_to_all(value, GROUP, split_axis=0, concat_axis=0, tiled=True)

    sendable = pl.pallas_call(
        pack_kernel,
        out_shape=jax.ShapeDtypeStruct((MEMBERS, tokens, count * DIM), bf16),
        in_specs=[HBM] * (1 + count),
        out_specs=HBM,
        scratch_shapes=[
            pltpu.SMEM(win.shape, jnp.int32),
            pltpu.VMEM((count, tokens, width), bf16),
            pltpu.VMEM((MEMBERS, tokens, count * DIM), bf16),
            ORDER,
            pltpu.SemaphoreType.DMA,
            pltpu.SemaphoreType.DMA((count, tokens // CHUNK)),
            pltpu.SemaphoreType.DMA((MEMBERS // BATCH,)),
        ],
        compiler_params=pltpu.CompilerParams(vmem_limit_bytes=PACK_VMEM),
    )(win, *sources)
    qkv = exchange(sendable)
    def facts_kernel(*refs):
        state_facts(columns, *refs)

    facts = pl.pallas_call(
        facts_kernel,
        out_shape=jax.ShapeDtypeStruct((HEAD + HEADS,), jnp.int32),
        in_specs=[SMEM, SMEM],
        out_specs=SMEM,
        scratch_shapes=[ORDER],
        compiler_params=PARAMS,
    )(win, info)

    whole = jnp.sum(jnp.prod(windows // 2, axis=1)) > WHOLE
    qkv, facts, whole = lax.optimization_barrier((qkv, facts, whole))
    qkv = qkv.reshape(rows, count * DIM)

    def beside(value, frame):
        up = [
            (((uly * columns + col) * 2 + frame) * 2, ((uly * columns + col + 1) * 2 + frame) * 2)
            for uly in range(8)
            for col in range(columns - 1)
        ]
        along = ("uly", "col", "f", "g")
        return lax.ppermute(value, along, up), lax.ppermute(value, along, [(b, a) for a, b in up])

    lower, upper = beside(qkv[:, : 2 * DIM], 0)
    pair = jax.ShapeDtypeStruct((rows // 2, 2 * DIM), bf16)
    half, rest = call(cut, (pair, pair), [facts, qkv])
    low_half, up_half = beside(half, 1)

    column = lax.axis_index("col")

    def send_rest(rest):
        near = jnp.abs(jnp.arange(columns) - column) == 1
        sent = jnp.where(near[:, None, None], rest[None], jnp.zeros_like(rest)[None])
        got = lax.all_to_all(sent, "col", split_axis=0, concat_axis=0, tiled=True)
        return tuple(
            lax.dynamic_index_in_dim(got, jnp.clip(at, 0, columns - 1), 0, keepdims=False)
            for at in (column - 1, column + 1)
        )

    def no_rest(rest):
        return (jnp.zeros_like(rest),) * 2

    low_rest, up_rest = lax.cond(whole, send_rest, no_rest, rest)

    state = (jax.ShapeDtypeStruct((rows, DIM), f32), jax.ShapeDtypeStruct((rows, 2 * DIM), f32))

    def own_kernel(facts, qkv, low_rest, up_rest, peak, total):
        del low_rest, up_rest
        own_column(facts, qkv, peak, total)

    peak, total = call(own_kernel, state, [facts, qkv], [low_rest, up_rest])
    joined = [pltpu.VMEM((rows, 2 * DIM), bf16), pltpu.SemaphoreType.DMA]
    peak, total = call(
        first_side, state, [facts, qkv, upper, low_half, peak, total], [low_rest], joined
    )
    result = call(
        second_side,
        jax.ShapeDtypeStruct((rows, DIM), bf16),
        [facts, qkv, lower, up_half, peak, total],
        [up_rest],
        joined,
    )
    back = exchange(result.reshape(MEMBERS, tokens, DIM))
    return pl.pallas_call(
        unpack,
        out_shape=jax.ShapeDtypeStruct((tokens, width), bf16),
        in_specs=[SMEM, VMEM],
        out_specs=HBM,
        scratch_shapes=[
            pltpu.VMEM((tokens, width), bf16),
            pltpu.SemaphoreType.DMA((HEADS // RUN,)),
        ],
        compiler_params=PARAMS,
    )(facts, back)


def solution(mesh):
    uly, blk, cfg = (mesh.shape[name] for name in ("uly", "blk", "cfg"))
    fine = Mesh(mesh.devices.reshape(uly, blk // 4, 2, 2, cfg), ("uly", "col", "f", "g", "cfg"))
    tokens = P(("cfg", "col", "f", "g", "uly"), None)
    return jax.shard_map(
        shards,
        mesh=fine,
        in_specs=(tokens, tokens, tokens, P()),
        out_specs=tokens,
        check_vma=False,
    )
```

```python
import jax
import jax.numpy as jnp
from jax import lax
from jax.experimental import pallas as pl
from jax.experimental.pallas import tpu as pltpu
from jax.sharding import Mesh
from jax.sharding import PartitionSpec as P

HEADS = 24
DIM = 128
TILE = 384
PLACES = 16
USED = 12
WHOLE = 8
OWN, ONE, TWO, JOINED, PAIRED, FRAMES, LO, HI, HALVED, REST, FIRST, SECOND, HEAD = range(13)
MEMBERS = 2 * PLACES
CHUNK = 16
BATCH = 16
RUN = 8
PACK_VMEM = 62 * 1024 * 1024
GROUP = ("f", "g", "uly")
EXP2_SCALE = DIM**-0.5 * 1.4426950408889634
PARAMS = pltpu.CompilerParams(vmem_limit_bytes=20 * 1024 * 1024)


def is_open(win, axis, head):
    return win[axis, head] // 2


def fill_order(win, order, told=None):
    for place in range(2 * PLACES):
        order[place] = 0

    def put(head, carry):
        joined, apart = carry
        frames, heights, wide = (is_open(win, axis, head) for axis in range(3))
        both = wide * frames * heights
        place = jnp.where(both > 0, joined, USED - 1 - apart)
        place = jnp.where(wide > 0, place, head - joined - apart)
        order[(1 - wide) * PLACES + place] = head
        if told is not None:
            told(head, wide, place, frames, heights)
        return joined + both, apart + wide - both

    lax.fori_loop(0, HEADS, put, (jnp.int32(0), jnp.int32(0)))
    for place in range(WHOLE, USED):
        order[place + USED - WHOLE] = order[place]


def state_facts(columns, win, info, facts, order):
    place, row, column, frame = info[0], info[1], info[2], info[3]

    def count(head, joined):
        return joined + is_open(win, 0, head) * is_open(win, 1, head) * is_open(win, 2, head)

    split = jnp.where(lax.fori_loop(0, HEADS, count, jnp.int32(0)) <= WHOLE, 1, 0)

    def told(head, wide, at, frames, heights):
        half = jnp.where(frames > heights, row, frame)
        at = jnp.where(wide * split * at >= WHOLE, at + (USED - WHOLE) * half, at)
        facts[HEAD + head] = at // 8 * 16 + (1 - wide) * 8 + at % 8

    fill_order(win, order, told)
    head = order[row * PLACES + place]
    frames, heights = is_open(win, 0, head), is_open(win, 1, head)
    shared = jnp.where(place >= WHOLE, 1 - row, 0)
    halved = shared * split
    half = jnp.where(place >= USED, halved, 0)
    used = jnp.where((place < USED) | (halved > 0), 1, 0)
    wide = used * (1 - row)
    facts[OWN] = used
    lower = jnp.where(column > 0, wide, 0)
    upper = jnp.where(column < columns - 1, wide, 0)
    facts[ONE] = jnp.where(shared > 0, lower, upper)
    facts[TWO] = jnp.where(shared > 0, upper, lower)
    facts[JOINED] = frames * heights
    facts[PAIRED] = frames + heights - 2 * frames * heights
    facts[FRAMES] = frames
    facts[LO] = half
    facts[HI] = jnp.where(halved > 0, half + 1, 2)
    facts[HALVED] = shared
    facts[REST] = shared * (1 - split)
    by_row = halved * jnp.where(frames > heights, 1, 0)
    first = jnp.where(by_row > 0, half, 2 * half)
    facts[FIRST] = first
    facts[SECOND] = first + 1 + by_row


def pack(count, win_hbm, *refs):
    sources = refs[:count]
    out, win, held, staged, order, win_done, done, out_done = refs[-8:]
    first = pltpu.make_async_copy(win_hbm, win, win_done)
    first.start()
    copies = []
    for part, source in enumerate(sources):
        for chunk in range(source.shape[0] // CHUNK):
            rows = pl.ds(chunk * CHUNK, CHUNK)
            copy = pltpu.make_async_copy(
                source.at[rows, :], held.at[part, rows, :], done.at[part, chunk]
            )
            copy.start()
            copies.append((part, copy))
    first.wait()
    fill_order(win, order)
    sent = []
    for part in range(count):
        for index, copy in copies:
            if index == part:
                copy.wait()
        column_range = pl.ds(part * DIM, DIM)
        for member in range(MEMBERS):
            frame, row, uly = member // 16, member // 8 % 2, member % 8
            column = pl.multiple_of(order[row * PLACES + frame * 8 + uly] * DIM, DIM)
            staged[member, :, part * DIM : (part + 1) * DIM] = held[part, :, pl.ds(column, DIM)]
            if member % BATCH == BATCH - 1:
                some = pl.ds(member + 1 - BATCH, BATCH)
                copy = pltpu.make_async_copy(
                    staged.at[some, :, column_range],
                    out.at[some, :, column_range],
                    out_done.at[part, member // BATCH],
                )
                copy.start()
                sent.append(copy)
    for copy in sent:
        copy.wait()


def lanes(column, width):
    return jnp.broadcast_to(column, (column.shape[0], width))


def side_by_side(parts, axis):
    return parts[0] if len(parts) == 1 else jnp.concatenate(parts, axis=axis)


def score(query, kv, keys):
    parts = [
        lax.dot_general(
            query, kv[some, :DIM], (((1,), (1,)), ((), ())), preferred_element_type=jnp.float32
        )
        for some in keys
    ]
    return side_by_side(parts, 1)


def fold(scores, kv, keys, rows, before, write):
    copies = scores.shape[1] // DIM
    now = lanes(jnp.max(scores, axis=1, keepdims=True), DIM)
    if before:
        peak = before[0][rows, :]
        now = jnp.maximum(peak, now)
    weights = jnp.exp2((scores - jnp.concatenate([now] * copies, axis=1)) * EXP2_SCALE)
    values = side_by_side([kv[some, DIM : 2 * DIM] for some in keys], 0)
    with_ones = jnp.concatenate([values, jnp.ones_like(values)], axis=1)
    total = jnp.dot(weights.astype(jnp.bfloat16), with_ones, preferred_element_type=jnp.float32)
    if before:
        fade = jnp.exp2((peak - now) * EXP2_SCALE)
        total = before[1][rows, :] * jnp.concatenate([fade, fade], axis=1) + total
    write(rows, now, total)


def tile_rows(tile):
    return pl.ds(pl.multiple_of(tile * TILE, TILE), TILE)


def visit(query, kv, facts, before, write):
    def chains(blocks, keys):
        ahead = score(query[blocks[0], :], kv, keys[0])
        for index, rows in enumerate(blocks):
            scores = ahead
            if index + 1 < len(blocks):
                ahead = score(query[blocks[index + 1], :], kv, keys[index + 1])
            fold(scores, kv, keys[index], rows, before, write)

    @pl.when(facts[JOINED] > 0)
    def _():
        every = [pl.ds(0, 4 * TILE)]
        chains([pl.ds(512 * block, 512) for block in range(3)], [every] * 3)

    for index in range(2):
        here = (facts[LO] <= index) & (index < facts[HI])

        @pl.when(here & (facts[PAIRED] > 0))
        def _(index=index):
            low = jnp.where(facts[FRAMES] > 0, index, 2 * index)
            pair = [tile_rows(low), tile_rows(low + jnp.where(facts[FRAMES] > 0, 2, 1))]
            chains(pair, [pair, pair])

        @pl.when(here & (facts[JOINED] + facts[PAIRED] == 0))
        def _(index=index):
            tiles = [pl.ds(tile * TILE, TILE) for tile in (2 * index, 2 * index + 1)]
            chains(tiles, [[tile] for tile in tiles])


def keep(peak, total):
    def write(rows, now, sums):
        peak[rows, :] = now
        total[rows, :] = sums

    return write


def divided(total):
    return (total[:, :DIM] / total[:, DIM:]).astype(jnp.bfloat16)


def own_column(facts, qkv, peak, total):
    @pl.when(facts[OWN] > 0)
    def _():
        visit(qkv.at[:, 2 * DIM :], qkv, facts, None, keep(peak, total))


def cut(facts, qkv, half, rest):
    rest[...] = qkv[2 * TILE :, : 2 * DIM]
    half[:TILE, :] = qkv[tile_rows(facts[FIRST]), : 2 * DIM]
    half[TILE:, :] = qkv[tile_rows(facts[SECOND]), : 2 * DIM]


def put_together(facts, every, half, rest, kv, done):
    @pl.when(facts[HALVED] == 0)
    def _():
        kv[...] = every[...]

    @pl.when(facts[HALVED] > 0)
    def _():
        kv[tile_rows(facts[FIRST]), :] = half[:TILE, :]
        kv[tile_rows(facts[SECOND]), :] = half[TILE:, :]

    @pl.when(facts[REST] > 0)
    def _():
        copy = pltpu.make_async_copy(rest, kv.at[pl.ds(2 * TILE, 2 * TILE), :], done)
        copy.start()
        copy.wait()


def first_side(facts, qkv, every, half, peak_in, total_in, rest, peak, total, kv, done):
    @pl.when(facts[ONE] > 0)
    def _():
        put_together(facts, every, half, rest, kv, done)
        visit(qkv.at[:, 2 * DIM :], kv, facts, (peak_in, total_in), keep(peak, total))

    @pl.when(facts[OWN] > facts[ONE])
    def _():
        peak[...] = peak_in[...]
        total[...] = total_in[...]


def second_side(facts, qkv, every, half, peak_in, total_in, rest, out, kv, done):
    def write(rows, now, sums):
        out[rows, :] = divided(sums)

    @pl.when(facts[TWO] > 0)
    def _():
        put_together(facts, every, half, rest, kv, done)
        visit(qkv.at[:, 2 * DIM :], kv, facts, (peak_in, total_in), write)

    @pl.when(facts[OWN] > facts[TWO])
    def _():
        out[...] = divided(total_in[...])


def unpack(facts, received, out, staged, done):
    copies = []
    for head in range(HEADS):
        staged[:, head * DIM : (head + 1) * DIM] = received[facts[HEAD + head]]
        if head % RUN == RUN - 1:
            columns = pl.ds((head + 1 - RUN) * DIM, RUN * DIM)
            copy = pltpu.make_async_copy(
                staged.at[:, columns], out.at[:, columns], done.at[head // RUN]
            )
            copy.start()
            copies.append(copy)
    for copy in copies:
        copy.wait()


HBM = pl.BlockSpec(memory_space=pltpu.HBM)
SMEM = pl.BlockSpec(memory_space=pltpu.SMEM)
VMEM = pl.BlockSpec(memory_space=pltpu.VMEM)
ORDER = pltpu.SMEM((MEMBERS,), jnp.int32)


def call(kernel, shapes, operands, far=(), scratch=()):
    return pl.pallas_call(
        kernel,
        out_shape=shapes,
        in_specs=[SMEM] + [VMEM] * (len(operands) - 1) + [HBM] * len(far),
        out_specs=jax.tree.map(lambda _: VMEM, shapes),
        scratch_shapes=list(scratch),
        compiler_params=PARAMS,
    )(*operands, *far)


def shards(queries, key_vectors, value_vectors, windows):
    tokens, width = queries.shape
    rows = MEMBERS * tokens
    columns = lax.axis_size("col")
    bf16, f32 = jnp.bfloat16, jnp.float32
    place = lax.axis_index("f") * 8 + lax.axis_index("uly")
    info = jnp.stack(
        [place, lax.axis_index("g"), lax.axis_index("col"), lax.axis_index("f")]
    ).astype(jnp.int32)
    win = windows.T
    sources = [key_vectors, value_vectors, queries]
    count = len(sources)

    def pack_kernel(*refs):
        pack(count, *refs)

    def exchange(value):
        return lax.all_to_all(value, GROUP, split_axis=0, concat_axis=0, tiled=True)

    sendable = pl.pallas_call(
        pack_kernel,
        out_shape=jax.ShapeDtypeStruct((MEMBERS, tokens, count * DIM), bf16),
        in_specs=[HBM] * (1 + count),
        out_specs=HBM,
        scratch_shapes=[
            pltpu.SMEM(win.shape, jnp.int32),
            pltpu.VMEM((count, tokens, width), bf16),
            pltpu.VMEM((MEMBERS, tokens, count * DIM), bf16),
            ORDER,
            pltpu.SemaphoreType.DMA,
            pltpu.SemaphoreType.DMA((count, tokens // CHUNK)),
            pltpu.SemaphoreType.DMA((count, MEMBERS // BATCH)),
        ],
        compiler_params=pltpu.CompilerParams(vmem_limit_bytes=PACK_VMEM),
    )(win, *sources)
    qkv = exchange(sendable)
    def facts_kernel(*refs):
        state_facts(columns, *refs)

    facts = pl.pallas_call(
        facts_kernel,
        out_shape=jax.ShapeDtypeStruct((HEAD + HEADS,), jnp.int32),
        in_specs=[SMEM, SMEM],
        out_specs=SMEM,
        scratch_shapes=[ORDER],
        compiler_params=PARAMS,
    )(win, info)

    whole = jnp.sum(jnp.prod(windows // 2, axis=1)) > WHOLE
    qkv, facts, whole = lax.optimization_barrier((qkv, facts, whole))
    qkv = qkv.reshape(rows, count * DIM)

    def beside(value, frame):
        up = [
            (((uly * columns + col) * 2 + frame) * 2, ((uly * columns + col + 1) * 2 + frame) * 2)
            for uly in range(8)
            for col in range(columns - 1)
        ]
        along = ("uly", "col", "f", "g")
        return lax.ppermute(value, along, up), lax.ppermute(value, along, [(b, a) for a, b in up])

    lower, upper = beside(qkv[:, : 2 * DIM], 0)
    pair = jax.ShapeDtypeStruct((rows // 2, 2 * DIM), bf16)
    half, rest = call(cut, (pair, pair), [facts, qkv])
    low_half, up_half = beside(half, 1)

    column = lax.axis_index("col")

    def send_rest(rest):
        near = jnp.abs(jnp.arange(columns) - column) == 1
        sent = jnp.where(near[:, None, None], rest[None], jnp.zeros_like(rest)[None])
        got = lax.all_to_all(sent, "col", split_axis=0, concat_axis=0, tiled=True)
        return tuple(
            lax.dynamic_index_in_dim(got, jnp.clip(at, 0, columns - 1), 0, keepdims=False)
            for at in (column - 1, column + 1)
        )

    def no_rest(rest):
        return (jnp.zeros_like(rest),) * 2

    low_rest, up_rest = lax.cond(whole, send_rest, no_rest, rest)

    state = (jax.ShapeDtypeStruct((rows, DIM), f32), jax.ShapeDtypeStruct((rows, 2 * DIM), f32))

    def own_kernel(facts, qkv, low_rest, up_rest, peak, total):
        del low_rest, up_rest
        own_column(facts, qkv, peak, total)

    peak, total = call(own_kernel, state, [facts, qkv], [low_rest, up_rest])
    joined = [pltpu.VMEM((rows, 2 * DIM), bf16), pltpu.SemaphoreType.DMA]
    peak, total = call(
        first_side, state, [facts, qkv, upper, low_half, peak, total], [low_rest], joined
    )
    result = call(
        second_side,
        jax.ShapeDtypeStruct((rows, DIM), bf16),
        [facts, qkv, lower, up_half, peak, total],
        [up_rest],
        joined,
    )
    back = exchange(result.reshape(MEMBERS, tokens, DIM))
    return pl.pallas_call(
        unpack,
        out_shape=jax.ShapeDtypeStruct((tokens, width), bf16),
        in_specs=[SMEM, VMEM],
        out_specs=HBM,
        scratch_shapes=[
            pltpu.VMEM((tokens, width), bf16),
            pltpu.SemaphoreType.DMA((HEADS // RUN,)),
        ],
        compiler_params=PARAMS,
    )(facts, back)


def solution(mesh):
    uly, blk, cfg = (mesh.shape[name] for name in ("uly", "blk", "cfg"))
    fine = Mesh(mesh.devices.reshape(uly, blk // 4, 2, 2, cfg), ("uly", "col", "f", "g", "cfg"))
    tokens = P(("cfg", "col", "f", "g", "uly"), None)
    return jax.shard_map(
        shards,
        mesh=fine,
        in_specs=(tokens, tokens, tokens, P()),
        out_specs=tokens,
        check_vma=False,
    )
```

```python
import jax
import jax.numpy as jnp
from jax import lax
from jax.experimental import pallas as pl
from jax.experimental.pallas import tpu as pltpu
from jax.sharding import Mesh
from jax.sharding import PartitionSpec as P

HEADS = 24
DIM = 128
TILE = 384
PLACES = 16
USED = 12
WHOLE = 8
OWN, ONE, TWO, JOINED, PAIRED, FRAMES, LO, HI, HALVED, REST, FIRST, SECOND, HEAD = range(13)
MEMBERS = 2 * PLACES
CHUNK = 16
BATCH = 16
RUN = 8
PACK_VMEM = 62 * 1024 * 1024
GROUP = ("f", "g", "uly")
EXP2_SCALE = DIM**-0.5 * 1.4426950408889634
PARAMS = pltpu.CompilerParams(vmem_limit_bytes=20 * 1024 * 1024)


def is_open(win, axis, head):
    return win[axis, head] >> 1


def fill_order(win, order, told=None):
    for place in range(PLACES + USED, 2 * PLACES):
        order[place] = 0
    joined, apart = jnp.int32(0), jnp.int32(0)
    for head in range(HEADS):
        frames, heights, wide = (is_open(win, axis, head) for axis in range(3))
        both = wide * frames * heights
        place = jnp.where(both > 0, joined, USED - 1 - apart)
        place = jnp.where(wide > 0, place, head - joined - apart)
        order[(1 - wide) * PLACES + place] = head
        if told is not None:
            told(head, wide, place, frames, heights)
        joined, apart = joined + both, apart + wide - both
    for place in range(WHOLE, USED):
        order[place + USED - WHOLE] = order[place]


def state_facts(columns, win, info, facts, order):
    place, row, column, frame = info[0], info[1], info[2], info[3]

    joined = jnp.int32(0)
    for head in range(HEADS):
        joined = joined + is_open(win, 0, head) * is_open(win, 1, head) * is_open(win, 2, head)
    split = jnp.where(joined <= WHOLE, 1, 0)

    def told(head, wide, at, frames, heights):
        half = jnp.where(frames > heights, row, frame)
        at = jnp.where(wide * split * at >= WHOLE, at + (USED - WHOLE) * half, at)
        facts[HEAD + head] = at // 8 * 16 + (1 - wide) * 8 + at % 8

    fill_order(win, order, told)
    head = order[row * PLACES + place]
    frames, heights = is_open(win, 0, head), is_open(win, 1, head)
    shared = jnp.where(place >= WHOLE, 1 - row, 0)
    halved = shared * split
    half = jnp.where(place >= USED, halved, 0)
    used = jnp.where((place < USED) | (halved > 0), 1, 0)
    wide = used * (1 - row)
    facts[OWN] = used
    lower = jnp.where(column > 0, wide, 0)
    upper = jnp.where(column < columns - 1, wide, 0)
    facts[ONE] = jnp.where(shared > 0, lower, upper)
    facts[TWO] = jnp.where(shared > 0, upper, lower)
    facts[JOINED] = frames * heights
    facts[PAIRED] = frames + heights - 2 * frames * heights
    facts[FRAMES] = frames
    facts[LO] = half
    facts[HI] = jnp.where(halved > 0, half + 1, 2)
    facts[HALVED] = shared
    facts[REST] = shared * (1 - split)
    by_row = halved * jnp.where(frames > heights, 1, 0)
    first = jnp.where(by_row > 0, half, 2 * half)
    facts[FIRST] = first
    facts[SECOND] = first + 1 + by_row


def pack(count, win_hbm, *refs):
    sources = refs[:count]
    out, win, held, staged, order, win_done, done, out_done = refs[-8:]
    first = pltpu.make_async_copy(win_hbm, win, win_done)
    first.start()
    copies = []
    for part, source in enumerate(sources):
        for chunk in range(source.shape[0] // CHUNK):
            rows = pl.ds(chunk * CHUNK, CHUNK)
            copy = pltpu.make_async_copy(
                source.at[rows, :], held.at[part, rows, :], done.at[part, chunk]
            )
            copy.start()
            copies.append((part, copy))
    first.wait()
    fill_order(win, order)
    sent = []
    for part in range(count):
        for index, copy in copies:
            if index == part:
                copy.wait()
        column_range = pl.ds(part * DIM, DIM)
        for member in range(MEMBERS):
            frame, row, uly = member // 16, member // 8 % 2, member % 8
            column = pl.multiple_of(order[row * PLACES + frame * 8 + uly] * DIM, DIM)
            staged[member, :, part * DIM : (part + 1) * DIM] = held[part, :, pl.ds(column, DIM)]
            if member % BATCH == BATCH - 1:
                some = pl.ds(member + 1 - BATCH, BATCH)
                copy = pltpu.make_async_copy(
                    staged.at[some, :, column_range],
                    out.at[some, :, column_range],
                    out_done.at[part, member // BATCH],
                )
                copy.start()
                sent.append(copy)
    for copy in sent:
        copy.wait()


def lanes(column, width):
    return jnp.broadcast_to(column, (column.shape[0], width))


def side_by_side(parts, axis):
    return parts[0] if len(parts) == 1 else jnp.concatenate(parts, axis=axis)


def score(query, kv, keys):
    parts = [
        lax.dot_general(
            query, kv[some, :DIM], (((1,), (1,)), ((), ())), preferred_element_type=jnp.float32
        )
        for some in keys
    ]
    return side_by_side(parts, 1)


def fold(scores, kv, keys, rows, before, write):
    copies = scores.shape[1] // DIM
    now = lanes(jnp.max(scores, axis=1, keepdims=True), DIM)
    if before:
        peak = before[0][rows, :]
        now = jnp.maximum(peak, now)
    weights = jnp.exp2((scores - jnp.concatenate([now] * copies, axis=1)) * EXP2_SCALE)
    values = side_by_side([kv[some, DIM : 2 * DIM] for some in keys], 0)
    with_ones = jnp.concatenate([values, jnp.ones_like(values)], axis=1)
    total = jnp.dot(weights.astype(jnp.bfloat16), with_ones, preferred_element_type=jnp.float32)
    if before:
        fade = jnp.exp2((peak - now) * EXP2_SCALE)
        total = before[1][rows, :] * jnp.concatenate([fade, fade], axis=1) + total
    write(rows, now, total)


def tile_rows(tile):
    return pl.ds(pl.multiple_of(tile * TILE, TILE), TILE)


def visit(query, kv, facts, before, write):
    def chains(blocks, keys):
        ahead = score(query[blocks[0], :], kv, keys[0])
        for index, rows in enumerate(blocks):
            scores = ahead
            if index + 1 < len(blocks):
                ahead = score(query[blocks[index + 1], :], kv, keys[index + 1])
            fold(scores, kv, keys[index], rows, before, write)

    @pl.when(facts[JOINED] > 0)
    def _():
        every = [pl.ds(0, 4 * TILE)]
        chains([pl.ds(TILE * block, TILE) for block in range(4)], [every] * 4)

    for index in range(2):
        here = (facts[LO] <= index) & (index < facts[HI])

        @pl.when(here & (facts[PAIRED] > 0))
        def _(index=index):
            low = jnp.where(facts[FRAMES] > 0, index, 2 * index)
            pair = [tile_rows(low), tile_rows(low + jnp.where(facts[FRAMES] > 0, 2, 1))]
            chains(pair, [pair, pair])

        @pl.when(here & (facts[JOINED] + facts[PAIRED] == 0))
        def _(index=index):
            tiles = [pl.ds(tile * TILE, TILE) for tile in (2 * index, 2 * index + 1)]
            chains(tiles, [[tile] for tile in tiles])


def keep(peak, total):
    def write(rows, now, sums):
        peak[rows, :] = now
        total[rows, :] = sums

    return write


def divided(total):
    return (total[:, :DIM] / total[:, DIM:]).astype(jnp.bfloat16)


def own_column(facts, qkv, peak, total):
    @pl.when(facts[OWN] > 0)
    def _():
        visit(qkv.at[:, 2 * DIM :], qkv, facts, None, keep(peak, total))


def cut_rest(facts, qkv, rest):
    rest[...] = qkv[2 * TILE :, : 2 * DIM]


def cut(facts, qkv, half):
    half[:TILE, :] = qkv[tile_rows(facts[FIRST]), : 2 * DIM]
    half[TILE:, :] = qkv[tile_rows(facts[SECOND]), : 2 * DIM]


def put_together(facts, every, half, rest, kv, done):
    @pl.when(facts[HALVED] == 0)
    def _():
        kv[...] = every[...]

    @pl.when(facts[HALVED] > 0)
    def _():
        kv[tile_rows(facts[FIRST]), :] = half[:TILE, :]
        kv[tile_rows(facts[SECOND]), :] = half[TILE:, :]

    @pl.when(facts[REST] > 0)
    def _():
        copy = pltpu.make_async_copy(rest, kv.at[pl.ds(2 * TILE, 2 * TILE), :], done)
        copy.start()
        copy.wait()


def first_side(facts, qkv, every, half, peak_in, total_in, rest, peak, total, kv, done):
    @pl.when(facts[ONE] > 0)
    def _():
        put_together(facts, every, half, rest, kv, done)
        visit(qkv.at[:, 2 * DIM :], kv, facts, (peak_in, total_in), keep(peak, total))

    @pl.when(facts[OWN] > facts[ONE])
    def _():
        peak[...] = peak_in[...]
        total[...] = total_in[...]


def second_side(facts, qkv, every, half, peak_in, total_in, rest, out, kv, done):
    def write(rows, now, sums):
        out[rows, :] = divided(sums)

    @pl.when(facts[TWO] > 0)
    def _():
        put_together(facts, every, half, rest, kv, done)
        visit(qkv.at[:, 2 * DIM :], kv, facts, (peak_in, total_in), write)

    @pl.when(facts[OWN] > facts[TWO])
    def _():
        out[...] = divided(total_in[...])


def unpack(facts, received, out, staged, done):
    copies = []
    for head in range(HEADS):
        staged[:, head * DIM : (head + 1) * DIM] = received[facts[HEAD + head]]
        if head % RUN == RUN - 1:
            columns = pl.ds((head + 1 - RUN) * DIM, RUN * DIM)
            copy = pltpu.make_async_copy(
                staged.at[:, columns], out.at[:, columns], done.at[head // RUN]
            )
            copy.start()
            copies.append(copy)
    for copy in copies:
        copy.wait()


HBM = pl.BlockSpec(memory_space=pltpu.HBM)
SMEM = pl.BlockSpec(memory_space=pltpu.SMEM)
VMEM = pl.BlockSpec(memory_space=pltpu.VMEM)
ORDER = pltpu.SMEM((MEMBERS,), jnp.int32)


def call(kernel, shapes, operands, far=(), scratch=()):
    return pl.pallas_call(
        kernel,
        out_shape=shapes,
        in_specs=[SMEM] + [VMEM] * (len(operands) - 1) + [HBM] * len(far),
        out_specs=jax.tree.map(lambda _: VMEM, shapes),
        scratch_shapes=list(scratch),
        compiler_params=PARAMS,
    )(*operands, *far)


def shards(queries, key_vectors, value_vectors, windows):
    tokens, width = queries.shape
    rows = MEMBERS * tokens
    columns = lax.axis_size("col")
    bf16, f32 = jnp.bfloat16, jnp.float32
    place = lax.axis_index("f") * 8 + lax.axis_index("uly")
    info = jnp.stack(
        [place, lax.axis_index("g"), lax.axis_index("col"), lax.axis_index("f")]
    ).astype(jnp.int32)
    win = windows.T
    sources = [key_vectors, value_vectors, queries]
    count = len(sources)

    def pack_kernel(*refs):
        pack(count, *refs)

    def exchange(value):
        return lax.all_to_all(value, GROUP, split_axis=0, concat_axis=0, tiled=True)

    sendable = pl.pallas_call(
        pack_kernel,
        out_shape=jax.ShapeDtypeStruct((MEMBERS, tokens, count * DIM), bf16),
        in_specs=[HBM] * (1 + count),
        out_specs=HBM,
        scratch_shapes=[
            pltpu.SMEM(win.shape, jnp.int32),
            pltpu.VMEM((count, tokens, width), bf16),
            pltpu.VMEM((MEMBERS, tokens, count * DIM), bf16),
            ORDER,
            pltpu.SemaphoreType.DMA,
            pltpu.SemaphoreType.DMA((count, tokens // CHUNK)),
            pltpu.SemaphoreType.DMA((count, MEMBERS // BATCH)),
        ],
        compiler_params=pltpu.CompilerParams(vmem_limit_bytes=PACK_VMEM),
    )(win, *sources)
    qkv = exchange(sendable)
    def facts_kernel(*refs):
        state_facts(columns, *refs)

    facts = pl.pallas_call(
        facts_kernel,
        out_shape=jax.ShapeDtypeStruct((HEAD + HEADS,), jnp.int32),
        in_specs=[SMEM, SMEM],
        out_specs=SMEM,
        scratch_shapes=[ORDER],
        compiler_params=PARAMS,
    )(win, info)

    whole = jnp.sum(jnp.prod(windows // 2, axis=1)) > WHOLE
    qkv, facts, whole = lax.optimization_barrier((qkv, facts, whole))
    qkv = qkv.reshape(rows, count * DIM)

    def beside(value, frame):
        up = [
            (((uly * columns + col) * 2 + frame) * 2, ((uly * columns + col + 1) * 2 + frame) * 2)
            for uly in range(8)
            for col in range(columns - 1)
        ]
        along = ("uly", "col", "f", "g")
        return lax.ppermute(value, along, up), lax.ppermute(value, along, [(b, a) for a, b in up])

    lower, upper = beside(qkv[:, : 2 * DIM], 0)
    pair = jax.ShapeDtypeStruct((rows // 2, 2 * DIM), bf16)
    half = call(cut, pair, [facts, qkv])
    low_half, up_half = beside(half, 1)

    column = lax.axis_index("col")

    def send_rest(rest):
        near = jnp.abs(jnp.arange(columns) - column) == 1
        sent = jnp.where(near[:, None, None], rest[None], jnp.zeros_like(rest)[None])
        got = lax.all_to_all(sent, "col", split_axis=0, concat_axis=0, tiled=True)
        return tuple(
            lax.dynamic_index_in_dim(got, jnp.clip(at, 0, columns - 1), 0, keepdims=False)
            for at in (column - 1, column + 1)
        )

    def no_rest(rest):
        return (jnp.zeros_like(rest),) * 2

    low_rest, up_rest = lax.cond(
        whole, send_rest, no_rest, call(cut_rest, pair, [facts, qkv])
    )

    state = (jax.ShapeDtypeStruct((rows, DIM), f32), jax.ShapeDtypeStruct((rows, 2 * DIM), f32))

    def own_kernel(facts, qkv, low_rest, up_rest, peak, total):
        del low_rest, up_rest
        own_column(facts, qkv, peak, total)

    peak, total = call(own_kernel, state, [facts, qkv], [low_rest, up_rest])
    joined = [pltpu.VMEM((rows, 2 * DIM), bf16), pltpu.SemaphoreType.DMA]
    peak, total = call(
        first_side, state, [facts, qkv, upper, low_half, peak, total], [low_rest], joined
    )
    result = call(
        second_side,
        jax.ShapeDtypeStruct((rows, DIM), bf16),
        [facts, qkv, lower, up_half, peak, total],
        [up_rest],
        joined,
    )
    back = exchange(result.reshape(MEMBERS, tokens, DIM))
    return pl.pallas_call(
        unpack,
        out_shape=jax.ShapeDtypeStruct((tokens, width), bf16),
        in_specs=[SMEM, VMEM],
        out_specs=HBM,
        scratch_shapes=[
            pltpu.VMEM((tokens, width), bf16),
            pltpu.SemaphoreType.DMA((HEADS // RUN,)),
        ],
        compiler_params=PARAMS,
    )(facts, back)


def solution(mesh):
    uly, blk, cfg = (mesh.shape[name] for name in ("uly", "blk", "cfg"))
    fine = Mesh(mesh.devices.reshape(uly, blk // 4, 2, 2, cfg), ("uly", "col", "f", "g", "cfg"))
    tokens = P(("cfg", "col", "f", "g", "uly"), None)
    return jax.shard_map(
        shards,
        mesh=fine,
        in_specs=(tokens, tokens, tokens, P()),
        out_specs=tokens,
        check_vma=False,
    )
```

```python
import jax
import jax.numpy as jnp
from jax import lax
from jax.experimental import pallas as pl
from jax.experimental.pallas import tpu as pltpu
from jax.sharding import Mesh
from jax.sharding import PartitionSpec as P

HEADS = 24
DIM = 128
TILE = 384
PLACES = 16
USED = 12
WHOLE = 8
OWN, ONE, TWO, JOINED, PAIRED, FRAMES, LO, HI, HALVED, REST, FIRST, SECOND, HEAD = range(13)
MEMBERS = 2 * PLACES
CHUNK = 16
BATCH = 16
RUN = 8
PACK_VMEM = 62 * 1024 * 1024
GROUP = ("f", "g", "uly")
EXP2_SCALE = DIM**-0.5 * 1.4426950408889634
PARAMS = pltpu.CompilerParams(vmem_limit_bytes=20 * 1024 * 1024)


def is_open(win, axis, head):
    return win[axis, head] >> 1


def fill_order(win, order, told=None):
    for place in range(PLACES + USED, 2 * PLACES):
        order[place] = 0
    joined, apart = jnp.int32(0), jnp.int32(0)
    for head in range(HEADS):
        frames, heights, wide = (is_open(win, axis, head) for axis in range(3))
        both = wide * frames * heights
        place = jnp.where(both > 0, joined, USED - 1 - apart)
        place = jnp.where(wide > 0, place, head - joined - apart)
        order[(1 - wide) * PLACES + place] = head
        if told is not None:
            told(head, wide, place, frames, heights)
        joined, apart = joined + both, apart + wide - both
    for place in range(WHOLE, USED):
        order[place + USED - WHOLE] = order[place]


def state_facts(columns, win, info, facts, order):
    place, row, column, frame = info[0], info[1], info[2], info[3]

    joined = jnp.int32(0)
    for head in range(HEADS):
        joined = joined + is_open(win, 0, head) * is_open(win, 1, head) * is_open(win, 2, head)
    split = jnp.where(joined <= WHOLE, 1, 0)

    def told(head, wide, at, frames, heights):
        half = jnp.where(frames > heights, row, frame)
        at = jnp.where(wide * split * at >= WHOLE, at + (USED - WHOLE) * half, at)
        facts[HEAD + head] = at // 8 * 16 + (1 - wide) * 8 + at % 8

    fill_order(win, order, told)
    head = order[row * PLACES + place]
    frames, heights = is_open(win, 0, head), is_open(win, 1, head)
    shared = jnp.where(place >= WHOLE, 1 - row, 0)
    halved = shared * split
    half = jnp.where(place >= USED, halved, 0)
    used = jnp.where((place < USED) | (halved > 0), 1, 0)
    wide = used * (1 - row)
    facts[OWN] = used
    lower = jnp.where(column > 0, wide, 0)
    upper = jnp.where(column < columns - 1, wide, 0)
    facts[ONE] = jnp.where(shared > 0, lower, upper)
    facts[TWO] = jnp.where(shared > 0, upper, lower)
    facts[JOINED] = frames * heights
    facts[PAIRED] = frames + heights - 2 * frames * heights
    facts[FRAMES] = frames
    facts[LO] = half
    facts[HI] = jnp.where(halved > 0, half + 1, 2)
    facts[HALVED] = shared
    facts[REST] = shared * (1 - split)
    by_row = halved * jnp.where(frames > heights, 1, 0)
    first = jnp.where(by_row > 0, half, 2 * half)
    facts[FIRST] = first
    facts[SECOND] = first + 1 + by_row


def pack(count, win_hbm, *refs):
    sources = refs[:count]
    out, win, held, staged, order, win_done, done, out_done = refs[-8:]
    first = pltpu.make_async_copy(win_hbm, win, win_done)
    first.start()
    copies = []
    for part, source in enumerate(sources):
        for chunk in range(source.shape[0] // CHUNK):
            rows = pl.ds(chunk * CHUNK, CHUNK)
            copy = pltpu.make_async_copy(
                source.at[rows, :], held.at[part, rows, :], done.at[part, chunk]
            )
            copy.start()
            copies.append((part, copy))
    first.wait()
    fill_order(win, order)
    sent = []
    for part in range(count):
        for index, copy in copies:
            if index == part:
                copy.wait()
        column_range = pl.ds(part * DIM, DIM)
        for member in range(MEMBERS):
            frame, row, uly = member // 16, member // 8 % 2, member % 8
            column = pl.multiple_of(order[row * PLACES + frame * 8 + uly] * DIM, DIM)
            staged[member, :, part * DIM : (part + 1) * DIM] = held[part, :, pl.ds(column, DIM)]
            if member % BATCH == BATCH - 1:
                some = pl.ds(member + 1 - BATCH, BATCH)
                copy = pltpu.make_async_copy(
                    staged.at[some, :, column_range],
                    out.at[some, :, column_range],
                    out_done.at[part, member // BATCH],
                )
                copy.start()
                sent.append(copy)
    for copy in sent:
        copy.wait()


def lanes(column, width):
    return jnp.broadcast_to(column, (column.shape[0], width))


def side_by_side(parts, axis):
    return parts[0] if len(parts) == 1 else jnp.concatenate(parts, axis=axis)


def score(query, kv, keys):
    parts = [
        lax.dot_general(
            query, kv[some, :DIM], (((1,), (1,)), ((), ())), preferred_element_type=jnp.float32
        )
        for some in keys
    ]
    return side_by_side(parts, 1)


def fold(scores, kv, keys, rows, before, write):
    copies = scores.shape[1] // DIM
    now = lanes(jnp.max(scores, axis=1, keepdims=True), DIM)
    if before:
        peak = before[0][rows, :]
        now = jnp.maximum(peak, now)
    weights = jnp.exp2((scores - jnp.concatenate([now] * copies, axis=1)) * EXP2_SCALE)
    values = side_by_side([kv[some, DIM : 2 * DIM] for some in keys], 0)
    with_ones = jnp.concatenate([values, jnp.ones_like(values)], axis=1)
    total = jnp.dot(weights.astype(jnp.bfloat16), with_ones, preferred_element_type=jnp.float32)
    if before:
        fade = jnp.exp2((peak - now) * EXP2_SCALE)
        total = before[1][rows, :] * jnp.concatenate([fade, fade], axis=1) + total
    write(rows, now, total)


def tile_rows(tile):
    return pl.ds(pl.multiple_of(tile * TILE, TILE), TILE)


def visit(query, kv, facts, before, write):
    def chains(blocks, keys):
        ahead = score(query[blocks[0], :], kv, keys[0])
        for index, rows in enumerate(blocks):
            scores = ahead
            if index + 1 < len(blocks):
                ahead = score(query[blocks[index + 1], :], kv, keys[index + 1])
            fold(scores, kv, keys[index], rows, before, write)

    @pl.when(facts[JOINED] > 0)
    def _():
        every = [pl.ds(0, 4 * TILE)]
        chains([pl.ds(TILE * block, TILE) for block in range(4)], [every] * 4)

    for index in range(2):
        here = (facts[LO] <= index) & (index < facts[HI])

        @pl.when(here & (facts[PAIRED] > 0))
        def _(index=index):
            low = jnp.where(facts[FRAMES] > 0, index, 2 * index)
            pair = [tile_rows(low), tile_rows(low + jnp.where(facts[FRAMES] > 0, 2, 1))]
            chains(pair, [pair, pair])

        @pl.when(here & (facts[JOINED] + facts[PAIRED] == 0))
        def _(index=index):
            tiles = [pl.ds(tile * TILE, TILE) for tile in (2 * index, 2 * index + 1)]
            chains(tiles, [[tile] for tile in tiles])


def keep(peak, total):
    def write(rows, now, sums):
        peak[rows, :] = now
        total[rows, :] = sums

    return write


def divided(total):
    return (total[:, :DIM] / total[:, DIM:]).astype(jnp.bfloat16)


def own_column(facts, qkv, peak, total):
    @pl.when(facts[OWN] > 0)
    def _():
        visit(qkv.at[:, 2 * DIM :], qkv, facts, None, keep(peak, total))


def cut_rest(facts, qkv, rest):
    rest[...] = qkv[2 * TILE :, : 2 * DIM]


def cut(facts, qkv, half):
    half[:TILE, :] = qkv[tile_rows(facts[FIRST]), : 2 * DIM]
    half[TILE:, :] = qkv[tile_rows(facts[SECOND]), : 2 * DIM]


def put_together(facts, every, half, rest, kv, done):
    @pl.when(facts[HALVED] == 0)
    def _():
        kv[...] = every[...]

    @pl.when(facts[HALVED] > 0)
    def _():
        copies = [
            pltpu.make_async_copy(
                half.at[pl.ds(number * TILE, TILE), :],
                kv.at[tile_rows(facts[which]), :],
                done.at[number],
            )
            for number, which in enumerate((FIRST, SECOND))
        ]
        for copy in copies:
            copy.start()
        for copy in copies:
            copy.wait()

    @pl.when(facts[REST] > 0)
    def _():
        copy = pltpu.make_async_copy(rest, kv.at[pl.ds(2 * TILE, 2 * TILE), :], done.at[2])
        copy.start()
        copy.wait()


def first_side(facts, qkv, every, peak_in, total_in, half, rest, peak, total, kv, done):
    @pl.when(facts[ONE] > 0)
    def _():
        put_together(facts, every, half, rest, kv, done)
        visit(qkv.at[:, 2 * DIM :], kv, facts, (peak_in, total_in), keep(peak, total))

    @pl.when(facts[OWN] > facts[ONE])
    def _():
        peak[...] = peak_in[...]
        total[...] = total_in[...]


def second_side(facts, qkv, every, peak_in, total_in, half, rest, out, kv, done):
    def write(rows, now, sums):
        out[rows, :] = divided(sums)

    @pl.when(facts[TWO] > 0)
    def _():
        put_together(facts, every, half, rest, kv, done)
        visit(qkv.at[:, 2 * DIM :], kv, facts, (peak_in, total_in), write)

    @pl.when(facts[OWN] > facts[TWO])
    def _():
        out[...] = divided(total_in[...])


def unpack(facts, received, out, staged, done):
    copies = []
    for head in range(HEADS):
        staged[:, head * DIM : (head + 1) * DIM] = received[facts[HEAD + head]]
        if head % RUN == RUN - 1:
            columns = pl.ds((head + 1 - RUN) * DIM, RUN * DIM)
            copy = pltpu.make_async_copy(
                staged.at[:, columns], out.at[:, columns], done.at[head // RUN]
            )
            copy.start()
            copies.append(copy)
    for copy in copies:
        copy.wait()


HBM = pl.BlockSpec(memory_space=pltpu.HBM)
SMEM = pl.BlockSpec(memory_space=pltpu.SMEM)
VMEM = pl.BlockSpec(memory_space=pltpu.VMEM)
ORDER = pltpu.SMEM((MEMBERS,), jnp.int32)


def call(kernel, shapes, operands, far=(), scratch=()):
    return pl.pallas_call(
        kernel,
        out_shape=shapes,
        in_specs=[SMEM] + [VMEM] * (len(operands) - 1) + [HBM] * len(far),
        out_specs=jax.tree.map(lambda _: VMEM, shapes),
        scratch_shapes=list(scratch),
        compiler_params=PARAMS,
    )(*operands, *far)


def shards(queries, key_vectors, value_vectors, windows):
    tokens, width = queries.shape
    rows = MEMBERS * tokens
    columns = lax.axis_size("col")
    bf16, f32 = jnp.bfloat16, jnp.float32
    place = lax.axis_index("f") * 8 + lax.axis_index("uly")
    info = jnp.stack(
        [place, lax.axis_index("g"), lax.axis_index("col"), lax.axis_index("f")]
    ).astype(jnp.int32)
    win = windows.T
    sources = [key_vectors, value_vectors, queries]
    count = len(sources)

    def pack_kernel(*refs):
        pack(count, *refs)

    def exchange(value):
        return lax.all_to_all(value, GROUP, split_axis=0, concat_axis=0, tiled=True)

    sendable = pl.pallas_call(
        pack_kernel,
        out_shape=jax.ShapeDtypeStruct((MEMBERS, tokens, count * DIM), bf16),
        in_specs=[HBM] * (1 + count),
        out_specs=HBM,
        scratch_shapes=[
            pltpu.SMEM(win.shape, jnp.int32),
            pltpu.VMEM((count, tokens, width), bf16),
            pltpu.VMEM((MEMBERS, tokens, count * DIM), bf16),
            ORDER,
            pltpu.SemaphoreType.DMA,
            pltpu.SemaphoreType.DMA((count, tokens // CHUNK)),
            pltpu.SemaphoreType.DMA((count, MEMBERS // BATCH)),
        ],
        compiler_params=pltpu.CompilerParams(vmem_limit_bytes=PACK_VMEM),
    )(win, *sources)
    qkv = exchange(sendable)
    def facts_kernel(*refs):
        state_facts(columns, *refs)

    facts = pl.pallas_call(
        facts_kernel,
        out_shape=jax.ShapeDtypeStruct((HEAD + HEADS,), jnp.int32),
        in_specs=[SMEM, SMEM],
        out_specs=SMEM,
        scratch_shapes=[ORDER],
        compiler_params=PARAMS,
    )(win, info)

    whole = jnp.sum(jnp.prod(windows // 2, axis=1)) > WHOLE
    qkv, facts, whole = lax.optimization_barrier((qkv, facts, whole))
    qkv = qkv.reshape(rows, count * DIM)

    def beside(value, frame):
        up = [
            (((uly * columns + col) * 2 + frame) * 2, ((uly * columns + col + 1) * 2 + frame) * 2)
            for uly in range(8)
            for col in range(columns - 1)
        ]
        along = ("uly", "col", "f", "g")
        return lax.ppermute(value, along, up), lax.ppermute(value, along, [(b, a) for a, b in up])

    lower, upper = beside(qkv[:, : 2 * DIM], 0)
    pair = jax.ShapeDtypeStruct((rows // 2, 2 * DIM), bf16)
    half = call(cut, pair, [facts, qkv])
    low_half, up_half = beside(half, 1)

    column = lax.axis_index("col")

    def send_rest(rest):
        near = jnp.abs(jnp.arange(columns) - column) == 1
        sent = jnp.where(near[:, None, None], rest[None], jnp.zeros_like(rest)[None])
        got = lax.all_to_all(sent, "col", split_axis=0, concat_axis=0, tiled=True)
        return tuple(
            lax.dynamic_index_in_dim(got, jnp.clip(at, 0, columns - 1), 0, keepdims=False)
            for at in (column - 1, column + 1)
        )

    def no_rest(rest):
        return (jnp.zeros_like(rest),) * 2

    low_rest, up_rest = lax.cond(
        whole, send_rest, no_rest, call(cut_rest, pair, [facts, qkv])
    )

    state = (jax.ShapeDtypeStruct((rows, DIM), f32), jax.ShapeDtypeStruct((rows, 2 * DIM), f32))

    def own_kernel(facts, qkv, low_rest, up_rest, peak, total):
        del low_rest, up_rest
        own_column(facts, qkv, peak, total)

    peak, total = call(own_kernel, state, [facts, qkv], [low_rest, up_rest])
    joined = [pltpu.VMEM((rows, 2 * DIM), bf16), pltpu.SemaphoreType.DMA((3,))]
    peak, total = call(
        first_side, state, [facts, qkv, upper, peak, total], [low_half, low_rest], joined
    )
    result = call(
        second_side,
        jax.ShapeDtypeStruct((rows, DIM), bf16),
        [facts, qkv, lower, peak, total],
        [up_half, up_rest],
        joined,
    )
    back = exchange(result.reshape(MEMBERS, tokens, DIM))
    return pl.pallas_call(
        unpack,
        out_shape=jax.ShapeDtypeStruct((tokens, width), bf16),
        in_specs=[SMEM, VMEM],
        out_specs=HBM,
        scratch_shapes=[
            pltpu.VMEM((tokens, width), bf16),
            pltpu.SemaphoreType.DMA((HEADS // RUN,)),
        ],
        compiler_params=PARAMS,
    )(facts, back)


def solution(mesh):
    uly, blk, cfg = (mesh.shape[name] for name in ("uly", "blk", "cfg"))
    fine = Mesh(mesh.devices.reshape(uly, blk // 4, 2, 2, cfg), ("uly", "col", "f", "g", "cfg"))
    tokens = P(("cfg", "col", "f", "g", "uly"), None)
    return jax.shard_map(
        shards,
        mesh=fine,
        in_specs=(tokens, tokens, tokens, P()),
        out_specs=tokens,
        check_vma=False,
    )
```

```python
import jax
import jax.numpy as jnp
from jax import lax
from jax.experimental import pallas as pl
from jax.experimental.pallas import tpu as pltpu
from jax.sharding import Mesh
from jax.sharding import PartitionSpec as P

HEADS = 24
DIM = 128
TILE = 384
PLACES = 16
USED = 12
WHOLE = 8
OWN, ONE, TWO, JOINED, PAIRED, FRAMES, LO, HI, HALVED, REST, FIRST, SECOND, HEAD = range(13)
MEMBERS = 2 * PLACES
CHUNK = 16
BATCH = 16
RUN = 8
PACK_VMEM = 62 * 1024 * 1024
GROUP = ("f", "g", "uly")
EXP2_SCALE = DIM**-0.5 * 1.4426950408889634
PARAMS = pltpu.CompilerParams(vmem_limit_bytes=12 * 1024 * 1024)


def is_open(win, axis, head):
    return win[axis, head] >> 1


def fill_order(win, order, told=None):
    for place in range(PLACES + USED, 2 * PLACES):
        order[place] = 0
    joined, apart = jnp.int32(0), jnp.int32(0)
    for head in range(HEADS):
        frames, heights, wide = (is_open(win, axis, head) for axis in range(3))
        both = wide * frames * heights
        place = jnp.where(both > 0, joined, USED - 1 - apart)
        place = jnp.where(wide > 0, place, head - joined - apart)
        order[(1 - wide) * PLACES + place] = head
        if told is not None:
            told(head, wide, place, frames, heights)
        joined, apart = joined + both, apart + wide - both
    for place in range(WHOLE, USED):
        order[place + USED - WHOLE] = order[place]


def state_facts(columns, win, info, facts, order):
    place, row, column, frame = info[0], info[1], info[2], info[3]

    joined = jnp.int32(0)
    for head in range(HEADS):
        joined = joined + is_open(win, 0, head) * is_open(win, 1, head) * is_open(win, 2, head)
    split = jnp.where(joined <= WHOLE, 1, 0)

    def told(head, wide, at, frames, heights):
        half = jnp.where(frames > heights, row, frame)
        at = jnp.where(wide * split * at >= WHOLE, at + (USED - WHOLE) * half, at)
        facts[HEAD + head] = at // 8 * 16 + (1 - wide) * 8 + at % 8

    fill_order(win, order, told)
    head = order[row * PLACES + place]
    frames, heights = is_open(win, 0, head), is_open(win, 1, head)
    shared = jnp.where(place >= WHOLE, 1 - row, 0)
    halved = shared * split
    half = jnp.where(place >= USED, halved, 0)
    used = jnp.where((place < USED) | (halved > 0), 1, 0)
    wide = used * (1 - row)
    facts[OWN] = used
    lower = jnp.where(column > 0, wide, 0)
    upper = jnp.where(column < columns - 1, wide, 0)
    facts[ONE] = jnp.where(shared > 0, lower, upper)
    facts[TWO] = jnp.where(shared > 0, upper, lower)
    facts[JOINED] = frames * heights
    facts[PAIRED] = frames + heights - 2 * frames * heights
    facts[FRAMES] = frames
    facts[LO] = half
    facts[HI] = jnp.where(halved > 0, half + 1, 2)
    facts[HALVED] = shared
    facts[REST] = shared * (1 - split)
    by_row = halved * jnp.where(frames > heights, 1, 0)
    first = jnp.where(by_row > 0, half, 2 * half)
    facts[FIRST] = first
    facts[SECOND] = first + 1 + by_row


def pack(count, win_hbm, *refs):
    sources = refs[:count]
    out, win, held, staged, order, win_done, done, out_done = refs[-8:]
    first = pltpu.make_async_copy(win_hbm, win, win_done)
    first.start()
    copies = []
    for part, source in enumerate(sources):
        for chunk in range(source.shape[0] // CHUNK):
            rows = pl.ds(chunk * CHUNK, CHUNK)
            copy = pltpu.make_async_copy(
                source.at[rows, :], held.at[part, rows, :], done.at[part, chunk]
            )
            copy.start()
            copies.append((part, copy))
    first.wait()
    fill_order(win, order)
    sent = []
    for part in range(count):
        for index, copy in copies:
            if index == part:
                copy.wait()
        column_range = pl.ds(part * DIM, DIM)
        for member in range(MEMBERS):
            frame, row, uly = member // 16, member // 8 % 2, member % 8
            column = pl.multiple_of(order[row * PLACES + frame * 8 + uly] * DIM, DIM)
            staged[member, :, part * DIM : (part + 1) * DIM] = held[part, :, pl.ds(column, DIM)]
            if member % BATCH == BATCH - 1:
                some = pl.ds(member + 1 - BATCH, BATCH)
                copy = pltpu.make_async_copy(
                    staged.at[some, :, column_range],
                    out.at[some, :, column_range],
                    out_done.at[part, member // BATCH],
                )
                copy.start()
                sent.append(copy)
    for copy in sent:
        copy.wait()


def lanes(column, width):
    return jnp.broadcast_to(column, (column.shape[0], width))


def side_by_side(parts, axis):
    return parts[0] if len(parts) == 1 else jnp.concatenate(parts, axis=axis)


def score(query, kv, keys):
    parts = [
        lax.dot_general(
            query, kv[some, :DIM], (((1,), (1,)), ((), ())), preferred_element_type=jnp.float32
        )
        for some in keys
    ]
    return side_by_side(parts, 1)


def fold(scores, kv, keys, rows, before, write):
    copies = scores.shape[1] // DIM
    now = lanes(jnp.max(scores, axis=1, keepdims=True), DIM)
    if before:
        peak = before[0][rows, :]
        now = jnp.maximum(peak, now)
    weights = jnp.exp2((scores - jnp.concatenate([now] * copies, axis=1)) * EXP2_SCALE)
    values = side_by_side([kv[some, DIM : 2 * DIM] for some in keys], 0)
    with_ones = jnp.concatenate([values, jnp.ones_like(values)], axis=1)
    total = jnp.dot(weights.astype(jnp.bfloat16), with_ones, preferred_element_type=jnp.float32)
    if before:
        fade = jnp.exp2((peak - now) * EXP2_SCALE)
        total = before[1][rows, :] * jnp.concatenate([fade, fade], axis=1) + total
    write(rows, now, total)


def tile_rows(tile):
    return pl.ds(pl.multiple_of(tile * TILE, TILE), TILE)


def visit(query, kv, facts, before, write):
    def chains(blocks, keys):
        ahead = score(query[blocks[0], :], kv, keys[0])
        for index, rows in enumerate(blocks):
            scores = ahead
            if index + 1 < len(blocks):
                ahead = score(query[blocks[index + 1], :], kv, keys[index + 1])
            fold(scores, kv, keys[index], rows, before, write)

    @pl.when(facts[JOINED] > 0)
    def _():
        every = [pl.ds(0, 4 * TILE)]
        chains([pl.ds(TILE * block, TILE) for block in range(4)], [every] * 4)

    for index in range(2):
        here = (facts[LO] <= index) & (index < facts[HI])

        @pl.when(here & (facts[PAIRED] > 0))
        def _(index=index):
            low = jnp.where(facts[FRAMES] > 0, index, 2 * index)
            pair = [tile_rows(low), tile_rows(low + jnp.where(facts[FRAMES] > 0, 2, 1))]
            chains(pair, [pair, pair])

        @pl.when(here & (facts[JOINED] + facts[PAIRED] == 0))
        def _(index=index):
            tiles = [pl.ds(tile * TILE, TILE) for tile in (2 * index, 2 * index + 1)]
            chains(tiles, [[tile] for tile in tiles])


def keep(peak, total):
    def write(rows, now, sums):
        peak[rows, :] = now
        total[rows, :] = sums

    return write


def divided(total):
    return (total[:, :DIM] / total[:, DIM:]).astype(jnp.bfloat16)


def own_column(facts, qkv, peak, total):
    @pl.when(facts[OWN] > 0)
    def _():
        visit(qkv.at[:, 2 * DIM :], qkv, facts, None, keep(peak, total))


def cut_rest(facts, qkv, rest):
    rest[...] = qkv[2 * TILE :, : 2 * DIM]


def cut(facts, qkv, half):
    half[:TILE, :] = qkv[tile_rows(facts[FIRST]), : 2 * DIM]
    half[TILE:, :] = qkv[tile_rows(facts[SECOND]), : 2 * DIM]


def put_together(facts, every, half, rest, kv, done):
    @pl.when(facts[HALVED] == 0)
    def _():
        kv[...] = every[...]

    @pl.when(facts[HALVED] > 0)
    def _():
        kv[tile_rows(facts[FIRST]), :] = half[:TILE, :]
        kv[tile_rows(facts[SECOND]), :] = half[TILE:, :]

    @pl.when(facts[REST] > 0)
    def _():
        copy = pltpu.make_async_copy(rest, kv.at[pl.ds(2 * TILE, 2 * TILE), :], done)
        copy.start()
        copy.wait()


def first_side(facts, qkv, every, half, peak_in, total_in, rest, peak, total, kv, done):
    @pl.when(facts[ONE] > 0)
    def _():
        put_together(facts, every, half, rest, kv, done)
        visit(qkv.at[:, 2 * DIM :], kv, facts, (peak_in, total_in), keep(peak, total))

    @pl.when(facts[OWN] > facts[ONE])
    def _():
        peak[...] = peak_in[...]
        total[...] = total_in[...]


def second_side(facts, qkv, every, half, peak_in, total_in, rest, out, kv, done):
    def write(rows, now, sums):
        out[rows, :] = divided(sums)

    @pl.when(facts[TWO] > 0)
    def _():
        put_together(facts, every, half, rest, kv, done)
        visit(qkv.at[:, 2 * DIM :], kv, facts, (peak_in, total_in), write)

    @pl.when(facts[OWN] > facts[TWO])
    def _():
        out[...] = divided(total_in[...])


def unpack(facts, received, out, staged, done):
    copies = []
    for head in range(HEADS):
        staged[:, head * DIM : (head + 1) * DIM] = received[facts[HEAD + head]]
        if head % RUN == RUN - 1:
            columns = pl.ds((head + 1 - RUN) * DIM, RUN * DIM)
            copy = pltpu.make_async_copy(
                staged.at[:, columns], out.at[:, columns], done.at[head // RUN]
            )
            copy.start()
            copies.append(copy)
    for copy in copies:
        copy.wait()


HBM = pl.BlockSpec(memory_space=pltpu.HBM)
SMEM = pl.BlockSpec(memory_space=pltpu.SMEM)
VMEM = pl.BlockSpec(memory_space=pltpu.VMEM)
ORDER = pltpu.SMEM((MEMBERS,), jnp.int32)


def call(kernel, shapes, operands, far=(), scratch=()):
    return pl.pallas_call(
        kernel,
        out_shape=shapes,
        in_specs=[SMEM] + [VMEM] * (len(operands) - 1) + [HBM] * len(far),
        out_specs=jax.tree.map(lambda _: VMEM, shapes),
        scratch_shapes=list(scratch),
        compiler_params=PARAMS,
    )(*operands, *far)


def shards(queries, key_vectors, value_vectors, windows):
    tokens, width = queries.shape
    rows = MEMBERS * tokens
    columns = lax.axis_size("col")
    bf16, f32 = jnp.bfloat16, jnp.float32
    place = lax.axis_index("f") * 8 + lax.axis_index("uly")
    info = jnp.stack(
        [place, lax.axis_index("g"), lax.axis_index("col"), lax.axis_index("f")]
    ).astype(jnp.int32)
    win = windows.T
    sources = [key_vectors, value_vectors, queries]
    count = len(sources)

    def pack_kernel(*refs):
        pack(count, *refs)

    def exchange(value):
        return lax.all_to_all(value, GROUP, split_axis=0, concat_axis=0, tiled=True)

    sendable = pl.pallas_call(
        pack_kernel,
        out_shape=jax.ShapeDtypeStruct((MEMBERS, tokens, count * DIM), bf16),
        in_specs=[HBM] * (1 + count),
        out_specs=HBM,
        scratch_shapes=[
            pltpu.SMEM(win.shape, jnp.int32),
            pltpu.VMEM((count, tokens, width), bf16),
            pltpu.VMEM((MEMBERS, tokens, count * DIM), bf16),
            ORDER,
            pltpu.SemaphoreType.DMA,
            pltpu.SemaphoreType.DMA((count, tokens // CHUNK)),
            pltpu.SemaphoreType.DMA((count, MEMBERS // BATCH)),
        ],
        compiler_params=pltpu.CompilerParams(vmem_limit_bytes=PACK_VMEM),
    )(win, *sources)
    qkv = exchange(sendable)
    def facts_kernel(*refs):
        state_facts(columns, *refs)

    facts = pl.pallas_call(
        facts_kernel,
        out_shape=jax.ShapeDtypeStruct((HEAD + HEADS,), jnp.int32),
        in_specs=[SMEM, SMEM],
        out_specs=SMEM,
        scratch_shapes=[ORDER],
        compiler_params=PARAMS,
    )(win, info)

    whole = jnp.sum(jnp.prod(windows // 2, axis=1)) > WHOLE
    qkv, facts, whole = lax.optimization_barrier((qkv, facts, whole))
    qkv = qkv.reshape(rows, count * DIM)

    def beside(value, frame):
        up = [
            (((uly * columns + col) * 2 + frame) * 2, ((uly * columns + col + 1) * 2 + frame) * 2)
            for uly in range(8)
            for col in range(columns - 1)
        ]
        along = ("uly", "col", "f", "g")
        return lax.ppermute(value, along, up), lax.ppermute(value, along, [(b, a) for a, b in up])

    lower, upper = beside(qkv[:, : 2 * DIM], 0)
    pair = jax.ShapeDtypeStruct((rows // 2, 2 * DIM), bf16)
    half = call(cut, pair, [facts, qkv])
    low_half, up_half = beside(half, 1)

    column = lax.axis_index("col")

    def send_rest(rest):
        near = jnp.abs(jnp.arange(columns) - column) == 1
        sent = jnp.where(near[:, None, None], rest[None], jnp.zeros_like(rest)[None])
        got = lax.all_to_all(sent, "col", split_axis=0, concat_axis=0, tiled=True)
        return tuple(
            lax.dynamic_index_in_dim(got, jnp.clip(at, 0, columns - 1), 0, keepdims=False)
            for at in (column - 1, column + 1)
        )

    def no_rest(rest):
        return (jnp.zeros_like(rest),) * 2

    low_rest, up_rest = lax.cond(
        whole, send_rest, no_rest, call(cut_rest, pair, [facts, qkv])
    )

    state = (jax.ShapeDtypeStruct((rows, DIM), f32), jax.ShapeDtypeStruct((rows, 2 * DIM), f32))

    def own_kernel(facts, qkv, low_rest, up_rest, peak, total):
        del low_rest, up_rest
        own_column(facts, qkv, peak, total)

    peak, total = call(own_kernel, state, [facts, qkv], [low_rest, up_rest])
    joined = [pltpu.VMEM((rows, 2 * DIM), bf16), pltpu.SemaphoreType.DMA]
    peak, total = call(
        first_side, state, [facts, qkv, upper, low_half, peak, total], [low_rest], joined
    )
    result = call(
        second_side,
        jax.ShapeDtypeStruct((rows, DIM), bf16),
        [facts, qkv, lower, up_half, peak, total],
        [up_rest],
        joined,
    )
    back = exchange(result.reshape(MEMBERS, tokens, DIM))
    return pl.pallas_call(
        unpack,
        out_shape=jax.ShapeDtypeStruct((tokens, width), bf16),
        in_specs=[SMEM, VMEM],
        out_specs=HBM,
        scratch_shapes=[
            pltpu.VMEM((tokens, width), bf16),
            pltpu.SemaphoreType.DMA((HEADS // RUN,)),
        ],
        compiler_params=PARAMS,
    )(facts, back)


def solution(mesh):
    uly, blk, cfg = (mesh.shape[name] for name in ("uly", "blk", "cfg"))
    fine = Mesh(mesh.devices.reshape(uly, blk // 4, 2, 2, cfg), ("uly", "col", "f", "g", "cfg"))
    tokens = P(("cfg", "col", "f", "g", "uly"), None)
    return jax.shard_map(
        shards,
        mesh=fine,
        in_specs=(tokens, tokens, tokens, P()),
        out_specs=tokens,
        check_vma=False,
    )
```

```python
import jax
import jax.numpy as jnp
from jax import lax
from jax.experimental import pallas as pl
from jax.experimental.pallas import tpu as pltpu
from jax.sharding import Mesh
from jax.sharding import PartitionSpec as P

HEADS = 24
DIM = 128
TILE = 384
PLACES = 16
USED = 12
WHOLE = 8
OWN, ONE, TWO, JOINED, PAIRED, FRAMES, LO, HI, HALVED, REST, FIRST, SECOND, HEAD = range(13)
MEMBERS = 2 * PLACES
CHUNK = 16
BATCH = 16
RUN = 8
PACK_VMEM = 62 * 1024 * 1024
GROUP = ("f", "g", "uly")
EXP2_SCALE = DIM**-0.5 * 1.4426950408889634
PARAMS = pltpu.CompilerParams(vmem_limit_bytes=20 * 1024 * 1024)


def is_open(win, axis, head):
    return win[axis, head] >> 1


def fill_order(win, order, told=None):
    for place in range(PLACES + USED, 2 * PLACES):
        order[place] = 0
    joined, apart = jnp.int32(0), jnp.int32(0)
    for head in range(HEADS):
        frames, heights, wide = (is_open(win, axis, head) for axis in range(3))
        both = wide * frames * heights
        place = jnp.where(both > 0, joined, USED - 1 - apart)
        place = jnp.where(wide > 0, place, head - joined - apart)
        order[(1 - wide) * PLACES + place] = head
        if told is not None:
            told(head, wide, place, frames, heights)
        joined, apart = joined + both, apart + wide - both
    for place in range(WHOLE, USED):
        order[place + USED - WHOLE] = order[place]


def state_facts(columns, win, info, facts, order):
    place, row, column, frame = info[0], info[1], info[2], info[3]

    joined = jnp.int32(0)
    for head in range(HEADS):
        joined = joined + is_open(win, 0, head) * is_open(win, 1, head) * is_open(win, 2, head)
    split = jnp.where(joined <= WHOLE, 1, 0)

    def told(head, wide, at, frames, heights):
        half = jnp.where(frames > heights, row, frame)
        at = jnp.where(wide * split * at >= WHOLE, at + (USED - WHOLE) * half, at)
        facts[HEAD + head] = at // 8 * 16 + (1 - wide) * 8 + at % 8

    fill_order(win, order, told)
    head = order[row * PLACES + place]
    frames, heights = is_open(win, 0, head), is_open(win, 1, head)
    shared = jnp.where(place >= WHOLE, 1 - row, 0)
    halved = shared * split
    half = jnp.where(place >= USED, halved, 0)
    used = jnp.where((place < USED) | (halved > 0), 1, 0)
    wide = used * (1 - row)
    facts[OWN] = used
    lower = jnp.where(column > 0, wide, 0)
    upper = jnp.where(column < columns - 1, wide, 0)
    facts[ONE] = jnp.where(shared > 0, lower, upper)
    facts[TWO] = jnp.where(shared > 0, upper, lower)
    facts[JOINED] = frames * heights
    facts[PAIRED] = frames + heights - 2 * frames * heights
    facts[FRAMES] = frames
    facts[LO] = half
    facts[HI] = jnp.where(halved > 0, half + 1, 2)
    facts[HALVED] = shared
    facts[REST] = shared * (1 - split)
    by_row = halved * jnp.where(frames > heights, 1, 0)
    first = jnp.where(by_row > 0, half, 2 * half)
    facts[FIRST] = first
    facts[SECOND] = first + 1 + by_row


def pack(count, win_hbm, *refs):
    sources = refs[:count]
    out, win, held, staged, order, win_done, done, out_done = refs[-8:]
    first = pltpu.make_async_copy(win_hbm, win, win_done)
    first.start()
    copies = []
    for part, source in enumerate(sources):
        for chunk in range(source.shape[0] // CHUNK):
            rows = pl.ds(chunk * CHUNK, CHUNK)
            copy = pltpu.make_async_copy(
                source.at[rows, :], held.at[part, rows, :], done.at[part, chunk]
            )
            copy.start()
            copies.append((part, copy))
    first.wait()
    fill_order(win, order)
    sent = []
    for part in range(count):
        for index, copy in copies:
            if index == part:
                copy.wait()
        column_range = pl.ds(part * DIM, DIM)
        for member in range(MEMBERS):
            frame, row, uly = member // 16, member // 8 % 2, member % 8
            column = pl.multiple_of(order[row * PLACES + frame * 8 + uly] * DIM, DIM)
            staged[member, :, part * DIM : (part + 1) * DIM] = held[part, :, pl.ds(column, DIM)]
            if member % BATCH == BATCH - 1:
                some = pl.ds(member + 1 - BATCH, BATCH)
                copy = pltpu.make_async_copy(
                    staged.at[some, :, column_range],
                    out.at[some, :, column_range],
                    out_done.at[part, member // BATCH],
                )
                copy.start()
                sent.append(copy)
    for copy in sent:
        copy.wait()


def lanes(column, width):
    return jnp.broadcast_to(column, (column.shape[0], width))


def side_by_side(parts, axis):
    return parts[0] if len(parts) == 1 else jnp.concatenate(parts, axis=axis)


def score(query, kv, keys):
    parts = [
        lax.dot_general(
            query, kv[some, :DIM], (((1,), (1,)), ((), ())), preferred_element_type=jnp.float32
        )
        for some in keys
    ]
    return side_by_side(parts, 1)


def fold(scores, kv, keys, rows, before, write):
    copies = scores.shape[1] // DIM
    now = lanes(jnp.max(scores, axis=1, keepdims=True), DIM)
    if before:
        peak = before[0][rows, :]
        now = jnp.maximum(peak, now)
    weights = jnp.exp2((scores - jnp.concatenate([now] * copies, axis=1)) * EXP2_SCALE)
    values = side_by_side([kv[some, DIM : 2 * DIM] for some in keys], 0)
    with_ones = jnp.concatenate([values, jnp.ones_like(values)], axis=1)
    total = jnp.dot(weights.astype(jnp.bfloat16), with_ones, preferred_element_type=jnp.float32)
    if before:
        fade = jnp.exp2((peak - now) * EXP2_SCALE)
        total = before[1][rows, :] * jnp.concatenate([fade, fade], axis=1) + total
    write(rows, now, total)


def tile_rows(tile):
    return pl.ds(pl.multiple_of(tile * TILE, TILE), TILE)


def visit(query, kv, facts, before, write):
    def chains(blocks, keys):
        ahead = score(query[blocks[0], :], kv, keys[0])
        for index, rows in enumerate(blocks):
            scores = ahead
            if index + 1 < len(blocks):
                ahead = score(query[blocks[index + 1], :], kv, keys[index + 1])
            fold(scores, kv, keys[index], rows, before, write)

    @pl.when(facts[JOINED] > 0)
    def _():
        every = [pl.ds(0, 4 * TILE)]
        chains([pl.ds(TILE * block, TILE) for block in range(4)], [every] * 4)

    for index in range(2):
        here = (facts[LO] <= index) & (index < facts[HI])

        @pl.when(here & (facts[PAIRED] > 0))
        def _(index=index):
            low = jnp.where(facts[FRAMES] > 0, index, 2 * index)
            pair = [tile_rows(low), tile_rows(low + jnp.where(facts[FRAMES] > 0, 2, 1))]
            chains(pair, [pair, pair])

        @pl.when(here & (facts[JOINED] + facts[PAIRED] == 0))
        def _(index=index):
            tiles = [pl.ds(tile * TILE, TILE) for tile in (2 * index, 2 * index + 1)]
            chains(tiles, [[tile] for tile in tiles])


def keep(peak, total):
    def write(rows, now, sums):
        peak[rows, :] = now
        total[rows, :] = sums

    return write


def divided(total):
    return (total[:, :DIM] / total[:, DIM:]).astype(jnp.bfloat16)


def own_column(facts, qkv, peak, total):
    @pl.when(facts[OWN] > 0)
    def _():
        visit(qkv.at[:, 2 * DIM :], qkv, facts, None, keep(peak, total))


def cut_rest(facts, qkv, rest):
    rest[...] = qkv[2 * TILE :, : 2 * DIM]


def cut(facts, qkv, half):
    half[:TILE, :] = qkv[tile_rows(facts[FIRST]), : 2 * DIM]
    half[TILE:, :] = qkv[tile_rows(facts[SECOND]), : 2 * DIM]


def put_together(facts, every, half, rest, kv, done, near):
    @pl.when(facts[HALVED] == 0)
    def _():
        kv[...] = every[...]

    @pl.when(facts[HALVED] > 0)
    def _():
        if near:
            kv[tile_rows(facts[FIRST]), :] = half[:TILE, :]
            kv[tile_rows(facts[SECOND]), :] = half[TILE:, :]
            return
        copies = [
            pltpu.make_async_copy(
                half.at[pl.ds(number * TILE, TILE), :],
                kv.at[tile_rows(facts[which]), :],
                done.at[number],
            )
            for number, which in enumerate((FIRST, SECOND))
        ]
        for copy in copies:
            copy.start()
        for copy in copies:
            copy.wait()

    @pl.when(facts[REST] > 0)
    def _():
        copy = pltpu.make_async_copy(rest, kv.at[pl.ds(2 * TILE, 2 * TILE), :], done.at[2])
        copy.start()
        copy.wait()


def first_side(facts, qkv, every, peak_in, total_in, half, rest, peak, total, kv, done):
    @pl.when(facts[ONE] > 0)
    def _():
        put_together(facts, every, half, rest, kv, done, False)
        visit(qkv.at[:, 2 * DIM :], kv, facts, (peak_in, total_in), keep(peak, total))

    @pl.when(facts[OWN] > facts[ONE])
    def _():
        peak[...] = peak_in[...]
        total[...] = total_in[...]


def second_side(facts, qkv, every, half, peak_in, total_in, rest, out, kv, done):
    def write(rows, now, sums):
        out[rows, :] = divided(sums)

    @pl.when(facts[TWO] > 0)
    def _():
        put_together(facts, every, half, rest, kv, done, True)
        visit(qkv.at[:, 2 * DIM :], kv, facts, (peak_in, total_in), write)

    @pl.when(facts[OWN] > facts[TWO])
    def _():
        out[...] = divided(total_in[...])


def unpack(facts, received, out, staged, done):
    copies = []
    for head in range(HEADS):
        staged[:, head * DIM : (head + 1) * DIM] = received[facts[HEAD + head]]
        if head % RUN == RUN - 1:
            columns = pl.ds((head + 1 - RUN) * DIM, RUN * DIM)
            copy = pltpu.make_async_copy(
                staged.at[:, columns], out.at[:, columns], done.at[head // RUN]
            )
            copy.start()
            copies.append(copy)
    for copy in copies:
        copy.wait()


HBM = pl.BlockSpec(memory_space=pltpu.HBM)
SMEM = pl.BlockSpec(memory_space=pltpu.SMEM)
VMEM = pl.BlockSpec(memory_space=pltpu.VMEM)
ORDER = pltpu.SMEM((MEMBERS,), jnp.int32)


def call(kernel, shapes, operands, far=(), scratch=()):
    return pl.pallas_call(
        kernel,
        out_shape=shapes,
        in_specs=[SMEM] + [VMEM] * (len(operands) - 1) + [HBM] * len(far),
        out_specs=jax.tree.map(lambda _: VMEM, shapes),
        scratch_shapes=list(scratch),
        compiler_params=PARAMS,
    )(*operands, *far)


def shards(queries, key_vectors, value_vectors, windows):
    tokens, width = queries.shape
    rows = MEMBERS * tokens
    columns = lax.axis_size("col")
    bf16, f32 = jnp.bfloat16, jnp.float32
    place = lax.axis_index("f") * 8 + lax.axis_index("uly")
    info = jnp.stack(
        [place, lax.axis_index("g"), lax.axis_index("col"), lax.axis_index("f")]
    ).astype(jnp.int32)
    win = windows.T
    sources = [key_vectors, value_vectors, queries]
    count = len(sources)

    def pack_kernel(*refs):
        pack(count, *refs)

    def exchange(value):
        return lax.all_to_all(value, GROUP, split_axis=0, concat_axis=0, tiled=True)

    sendable = pl.pallas_call(
        pack_kernel,
        out_shape=jax.ShapeDtypeStruct((MEMBERS, tokens, count * DIM), bf16),
        in_specs=[HBM] * (1 + count),
        out_specs=HBM,
        scratch_shapes=[
            pltpu.SMEM(win.shape, jnp.int32),
            pltpu.VMEM((count, tokens, width), bf16),
            pltpu.VMEM((MEMBERS, tokens, count * DIM), bf16),
            ORDER,
            pltpu.SemaphoreType.DMA,
            pltpu.SemaphoreType.DMA((count, tokens // CHUNK)),
            pltpu.SemaphoreType.DMA((count, MEMBERS // BATCH)),
        ],
        compiler_params=pltpu.CompilerParams(vmem_limit_bytes=PACK_VMEM),
    )(win, *sources)
    qkv = exchange(sendable)
    def facts_kernel(*refs):
        state_facts(columns, *refs)

    facts = pl.pallas_call(
        facts_kernel,
        out_shape=jax.ShapeDtypeStruct((HEAD + HEADS,), jnp.int32),
        in_specs=[SMEM, SMEM],
        out_specs=SMEM,
        scratch_shapes=[ORDER],
        compiler_params=PARAMS,
    )(win, info)

    whole = jnp.sum(jnp.prod(windows // 2, axis=1)) > WHOLE
    qkv, facts, whole = lax.optimization_barrier((qkv, facts, whole))
    qkv = qkv.reshape(rows, count * DIM)

    def beside(value, frame):
        up = [
            (((uly * columns + col) * 2 + frame) * 2, ((uly * columns + col + 1) * 2 + frame) * 2)
            for uly in range(8)
            for col in range(columns - 1)
        ]
        along = ("uly", "col", "f", "g")
        return lax.ppermute(value, along, up), lax.ppermute(value, along, [(b, a) for a, b in up])

    lower, upper = beside(qkv[:, : 2 * DIM], 0)
    pair = jax.ShapeDtypeStruct((rows // 2, 2 * DIM), bf16)
    half = call(cut, pair, [facts, qkv])
    low_half, up_half = beside(half, 1)

    column = lax.axis_index("col")

    def send_rest(rest):
        near = jnp.abs(jnp.arange(columns) - column) == 1
        sent = jnp.where(near[:, None, None], rest[None], jnp.zeros_like(rest)[None])
        got = lax.all_to_all(sent, "col", split_axis=0, concat_axis=0, tiled=True)
        return tuple(
            lax.dynamic_index_in_dim(got, jnp.clip(at, 0, columns - 1), 0, keepdims=False)
            for at in (column - 1, column + 1)
        )

    def no_rest(rest):
        return (jnp.zeros_like(rest),) * 2

    low_rest, up_rest = lax.cond(
        whole, send_rest, no_rest, call(cut_rest, pair, [facts, qkv])
    )

    state = (jax.ShapeDtypeStruct((rows, DIM), f32), jax.ShapeDtypeStruct((rows, 2 * DIM), f32))

    def own_kernel(facts, qkv, low_rest, up_rest, peak, total):
        del low_rest, up_rest
        own_column(facts, qkv, peak, total)

    peak, total = call(own_kernel, state, [facts, qkv], [low_rest, up_rest])
    joined = [pltpu.VMEM((rows, 2 * DIM), bf16), pltpu.SemaphoreType.DMA((3,))]
    peak, total = call(
        first_side, state, [facts, qkv, upper, peak, total], [low_half, low_rest], joined
    )
    result = call(
        second_side,
        jax.ShapeDtypeStruct((rows, DIM), bf16),
        [facts, qkv, lower, up_half, peak, total],
        [up_rest],
        joined,
    )
    back = exchange(result.reshape(MEMBERS, tokens, DIM))
    return pl.pallas_call(
        unpack,
        out_shape=jax.ShapeDtypeStruct((tokens, width), bf16),
        in_specs=[SMEM, VMEM],
        out_specs=HBM,
        scratch_shapes=[
            pltpu.VMEM((tokens, width), bf16),
            pltpu.SemaphoreType.DMA((HEADS // RUN,)),
        ],
        compiler_params=PARAMS,
    )(facts, back)


def solution(mesh):
    uly, blk, cfg = (mesh.shape[name] for name in ("uly", "blk", "cfg"))
    fine = Mesh(mesh.devices.reshape(uly, blk // 4, 2, 2, cfg), ("uly", "col", "f", "g", "cfg"))
    tokens = P(("cfg", "col", "f", "g", "uly"), None)
    return jax.shard_map(
        shards,
        mesh=fine,
        in_specs=(tokens, tokens, tokens, P()),
        out_specs=tokens,
        check_vma=False,
    )
```

```python
import jax
import jax.numpy as jnp
from jax import lax
from jax.experimental import pallas as pl
from jax.experimental.pallas import tpu as pltpu
from jax.sharding import Mesh
from jax.sharding import PartitionSpec as P

HEADS = 24
DIM = 128
TILE = 384
PLACES = 16
USED = 12
WHOLE = 8
OWN, ONE, TWO, JOINED, PAIRED, FRAMES, LO, HI, HALVED, REST, FIRST, SECOND, HEAD = range(13)
MEMBERS = 2 * PLACES
CHUNK = 16
BATCH = 16
RUN = 8
PACK_VMEM = 62 * 1024 * 1024
GROUP = ("f", "g", "uly")
EXP2_SCALE = DIM**-0.5 * 1.4426950408889634
PARAMS = pltpu.CompilerParams(vmem_limit_bytes=20 * 1024 * 1024)


def is_open(win, axis, head):
    return win[axis, head] >> 1


def fill_order(win, order, told=None):
    for place in range(PLACES + USED, 2 * PLACES):
        order[place] = 0
    joined, apart = jnp.int32(0), jnp.int32(0)
    for head in range(HEADS):
        frames, heights, wide = (is_open(win, axis, head) for axis in range(3))
        both = wide * frames * heights
        place = jnp.where(both > 0, joined, USED - 1 - apart)
        place = jnp.where(wide > 0, place, head - joined - apart)
        order[(1 - wide) * PLACES + place] = head
        if told is not None:
            told(head, wide, place, frames, heights)
        joined, apart = joined + both, apart + wide - both
    for place in range(WHOLE, USED):
        order[place + USED - WHOLE] = order[place]


def state_facts(columns, win, info, facts, order):
    place, row, column, frame = info[0], info[1], info[2], info[3]

    joined = jnp.int32(0)
    for head in range(HEADS):
        joined = joined + is_open(win, 0, head) * is_open(win, 1, head) * is_open(win, 2, head)
    split = jnp.where(joined <= WHOLE, 1, 0)

    def told(head, wide, at, frames, heights):
        half = jnp.where(frames > heights, row, frame)
        at = jnp.where(wide * split * at >= WHOLE, at + (USED - WHOLE) * half, at)
        facts[HEAD + head] = at // 8 * 16 + (1 - wide) * 8 + at % 8

    fill_order(win, order, told)
    head = order[row * PLACES + place]
    frames, heights = is_open(win, 0, head), is_open(win, 1, head)
    shared = jnp.where(place >= WHOLE, 1 - row, 0)
    halved = shared * split
    half = jnp.where(place >= USED, halved, 0)
    used = jnp.where((place < USED) | (halved > 0), 1, 0)
    wide = used * (1 - row)
    facts[OWN] = used
    lower = jnp.where(column > 0, wide, 0)
    upper = jnp.where(column < columns - 1, wide, 0)
    facts[ONE] = jnp.where(shared > 0, lower, upper)
    facts[TWO] = jnp.where(shared > 0, upper, lower)
    facts[JOINED] = frames * heights
    facts[PAIRED] = frames + heights - 2 * frames * heights
    facts[FRAMES] = frames
    facts[LO] = half
    facts[HI] = jnp.where(halved > 0, half + 1, 2)
    facts[HALVED] = shared
    facts[REST] = shared * (1 - split)
    by_row = halved * jnp.where(frames > heights, 1, 0)
    first = jnp.where(by_row > 0, half, 2 * half)
    facts[FIRST] = first
    facts[SECOND] = first + 1 + by_row


def pack(count, win_hbm, *refs):
    sources = refs[:count]
    out, win, held, staged, order, win_done, done, out_done = refs[-8:]
    first = pltpu.make_async_copy(win_hbm, win, win_done)
    first.start()
    copies = []
    for part, source in enumerate(sources):
        for chunk in range(source.shape[0] // CHUNK):
            rows = pl.ds(chunk * CHUNK, CHUNK)
            copy = pltpu.make_async_copy(
                source.at[rows, :], held.at[part, rows, :], done.at[part, chunk]
            )
            copy.start()
            copies.append((part, copy))
    first.wait()
    fill_order(win, order)
    sent = []
    for part in range(count):
        for index, copy in copies:
            if index == part:
                copy.wait()
        column_range = pl.ds(part * DIM, DIM)
        for member in range(MEMBERS):
            frame, row, uly = member // 16, member // 8 % 2, member % 8
            column = pl.multiple_of(order[row * PLACES + frame * 8 + uly] * DIM, DIM)
            staged[member, :, part * DIM : (part + 1) * DIM] = held[part, :, pl.ds(column, DIM)]
            if member % BATCH == BATCH - 1:
                some = pl.ds(member + 1 - BATCH, BATCH)
                copy = pltpu.make_async_copy(
                    staged.at[some, :, column_range],
                    out.at[some, :, column_range],
                    out_done.at[part, member // BATCH],
                )
                copy.start()
                sent.append(copy)
    for copy in sent:
        copy.wait()


def lanes(column, width):
    return jnp.broadcast_to(column, (column.shape[0], width))


def side_by_side(parts, axis):
    return parts[0] if len(parts) == 1 else jnp.concatenate(parts, axis=axis)


def score(query, kv, keys):
    parts = [
        lax.dot_general(
            query, kv[some, :DIM], (((1,), (1,)), ((), ())), preferred_element_type=jnp.float32
        )
        for some in keys
    ]
    return side_by_side(parts, 1)


def fold(scores, kv, keys, rows, before, write):
    copies = scores.shape[1] // DIM
    now = lanes(jnp.max(scores, axis=1, keepdims=True), DIM)
    if before:
        peak = before[0][rows, :]
        now = jnp.maximum(peak, now)
    weights = jnp.exp2((scores - jnp.concatenate([now] * copies, axis=1)) * EXP2_SCALE)
    values = side_by_side([kv[some, DIM : 2 * DIM] for some in keys], 0)
    with_ones = jnp.concatenate([values, jnp.ones_like(values)], axis=1)
    total = jnp.dot(weights.astype(jnp.bfloat16), with_ones, preferred_element_type=jnp.float32)
    if before:
        fade = jnp.exp2((peak - now) * EXP2_SCALE)
        total = before[1][rows, :] * jnp.concatenate([fade, fade], axis=1) + total
    write(rows, now, total)


def tile_rows(tile):
    return pl.ds(pl.multiple_of(tile * TILE, TILE), TILE)


def visit(query, kv, facts, before, write):
    def chains(blocks, keys):
        ahead = score(query[blocks[0], :], kv, keys[0])
        for index, rows in enumerate(blocks):
            scores = ahead
            if index + 1 < len(blocks):
                ahead = score(query[blocks[index + 1], :], kv, keys[index + 1])
            fold(scores, kv, keys[index], rows, before, write)

    @pl.when(facts[JOINED] > 0)
    def _():
        every = [pl.ds(0, 4 * TILE)]
        chains([pl.ds(TILE * block, TILE) for block in range(4)], [every] * 4)

    for index in range(2):
        here = (facts[LO] <= index) & (index < facts[HI])

        @pl.when(here & (facts[PAIRED] > 0))
        def _(index=index):
            low = jnp.where(facts[FRAMES] > 0, index, 2 * index)
            pair = [tile_rows(low), tile_rows(low + jnp.where(facts[FRAMES] > 0, 2, 1))]
            chains(pair, [pair, pair])

        @pl.when(here & (facts[JOINED] + facts[PAIRED] == 0))
        def _(index=index):
            tiles = [pl.ds(tile * TILE, TILE) for tile in (2 * index, 2 * index + 1)]
            chains(tiles, [[tile] for tile in tiles])


def keep(peak, total):
    def write(rows, now, sums):
        peak[rows, :] = now
        total[rows, :] = sums

    return write


def divided(total):
    return (total[:, :DIM] / total[:, DIM:]).astype(jnp.bfloat16)


def own_column(facts, qkv, peak, total):
    @pl.when(facts[OWN] > 0)
    def _():
        visit(qkv.at[:, 2 * DIM :], qkv, facts, None, keep(peak, total))


def cut(facts, qkv, half):
    half[:TILE, :] = qkv[tile_rows(facts[FIRST]), : 2 * DIM]
    half[TILE:, :] = qkv[tile_rows(facts[SECOND]), : 2 * DIM]


def put_together(facts, every, half, rest, kv, done, near):
    @pl.when(facts[HALVED] == 0)
    def _():
        kv[...] = every[...]

    @pl.when(facts[HALVED] > 0)
    def _():
        if near:
            kv[tile_rows(facts[FIRST]), :] = half[:TILE, :]
            kv[tile_rows(facts[SECOND]), :] = half[TILE:, :]
            return
        copies = [
            pltpu.make_async_copy(
                half.at[pl.ds(number * TILE, TILE), :],
                kv.at[tile_rows(facts[which]), :],
                done.at[number],
            )
            for number, which in enumerate((FIRST, SECOND))
        ]
        for copy in copies:
            copy.start()
        for copy in copies:
            copy.wait()

    @pl.when(facts[REST] > 0)
    def _():
        copy = pltpu.make_async_copy(rest, kv.at[pl.ds(2 * TILE, 2 * TILE), :], done.at[2])
        copy.start()
        copy.wait()


def first_side(facts, qkv, every, peak_in, total_in, half, rest, peak, total, kv, done):
    @pl.when(facts[ONE] > 0)
    def _():
        put_together(facts, every, half, rest, kv, done, False)
        visit(qkv.at[:, 2 * DIM :], kv, facts, (peak_in, total_in), keep(peak, total))

    @pl.when(facts[OWN] > facts[ONE])
    def _():
        peak[...] = peak_in[...]
        total[...] = total_in[...]


def second_side(facts, qkv, every, half, peak_in, total_in, rest, out, kv, done):
    def write(rows, now, sums):
        out[rows, :] = divided(sums)

    @pl.when(facts[TWO] > 0)
    def _():
        put_together(facts, every, half, rest, kv, done, True)
        visit(qkv.at[:, 2 * DIM :], kv, facts, (peak_in, total_in), write)

    @pl.when(facts[OWN] > facts[TWO])
    def _():
        out[...] = divided(total_in[...])


def unpack(facts, received, out, staged, done):
    copies = []
    for head in range(HEADS):
        staged[:, head * DIM : (head + 1) * DIM] = received[facts[HEAD + head]]
        if head % RUN == RUN - 1:
            columns = pl.ds((head + 1 - RUN) * DIM, RUN * DIM)
            copy = pltpu.make_async_copy(
                staged.at[:, columns], out.at[:, columns], done.at[head // RUN]
            )
            copy.start()
            copies.append(copy)
    for copy in copies:
        copy.wait()


HBM = pl.BlockSpec(memory_space=pltpu.HBM)
SMEM = pl.BlockSpec(memory_space=pltpu.SMEM)
VMEM = pl.BlockSpec(memory_space=pltpu.VMEM)
ORDER = pltpu.SMEM((MEMBERS,), jnp.int32)


def call(kernel, shapes, operands, far=(), scratch=()):
    return pl.pallas_call(
        kernel,
        out_shape=shapes,
        in_specs=[SMEM] + [VMEM] * (len(operands) - 1) + [HBM] * len(far),
        out_specs=jax.tree.map(lambda _: VMEM, shapes),
        scratch_shapes=list(scratch),
        compiler_params=PARAMS,
    )(*operands, *far)


def shards(queries, key_vectors, value_vectors, windows):
    tokens, width = queries.shape
    rows = MEMBERS * tokens
    columns = lax.axis_size("col")
    bf16, f32 = jnp.bfloat16, jnp.float32
    place = lax.axis_index("f") * 8 + lax.axis_index("uly")
    info = jnp.stack(
        [place, lax.axis_index("g"), lax.axis_index("col"), lax.axis_index("f")]
    ).astype(jnp.int32)
    win = windows.T
    sources = [key_vectors, value_vectors, queries]
    count = len(sources)

    def pack_kernel(*refs):
        pack(count, *refs)

    def exchange(value):
        return lax.all_to_all(value, GROUP, split_axis=0, concat_axis=0, tiled=True)

    sendable = pl.pallas_call(
        pack_kernel,
        out_shape=jax.ShapeDtypeStruct((MEMBERS, tokens, count * DIM), bf16),
        in_specs=[HBM] * (1 + count),
        out_specs=HBM,
        scratch_shapes=[
            pltpu.SMEM(win.shape, jnp.int32),
            pltpu.VMEM((count, tokens, width), bf16),
            pltpu.VMEM((MEMBERS, tokens, count * DIM), bf16),
            ORDER,
            pltpu.SemaphoreType.DMA,
            pltpu.SemaphoreType.DMA((count, tokens // CHUNK)),
            pltpu.SemaphoreType.DMA((count, MEMBERS // BATCH)),
        ],
        compiler_params=pltpu.CompilerParams(vmem_limit_bytes=PACK_VMEM),
    )(win, *sources)
    qkv = exchange(sendable)
    def facts_kernel(*refs):
        state_facts(columns, *refs)

    facts = pl.pallas_call(
        facts_kernel,
        out_shape=jax.ShapeDtypeStruct((HEAD + HEADS,), jnp.int32),
        in_specs=[SMEM, SMEM],
        out_specs=SMEM,
        scratch_shapes=[ORDER],
        compiler_params=PARAMS,
    )(win, info)

    whole = jnp.sum(jnp.prod(windows // 2, axis=1)) > WHOLE
    qkv, facts, whole = lax.optimization_barrier((qkv, facts, whole))
    qkv = qkv.reshape(rows, count * DIM)

    def beside(value, frame):
        up = [
            (((uly * columns + col) * 2 + frame) * 2, ((uly * columns + col + 1) * 2 + frame) * 2)
            for uly in range(8)
            for col in range(columns - 1)
        ]
        along = ("uly", "col", "f", "g")
        return lax.ppermute(value, along, up), lax.ppermute(value, along, [(b, a) for a, b in up])

    kv = qkv[:, : 2 * DIM]
    lower, upper = beside(kv, 0)
    pair = jax.ShapeDtypeStruct((rows // 2, 2 * DIM), bf16)
    half = call(cut, pair, [facts, qkv])
    low_half, up_half = beside(half, 1)

    column = lax.axis_index("col")

    def send_rest(kv):
        rest = kv[rows // 2 :]
        near = jnp.abs(jnp.arange(columns) - column) == 1
        sent = jnp.where(near[:, None, None], rest[None], jnp.zeros_like(rest)[None])
        got = lax.all_to_all(sent, "col", split_axis=0, concat_axis=0, tiled=True)
        return tuple(
            lax.dynamic_index_in_dim(got, jnp.clip(at, 0, columns - 1), 0, keepdims=False)
            for at in (column - 1, column + 1)
        )

    def no_rest(kv):
        return (jnp.zeros_like(kv[rows // 2 :]),) * 2

    low_rest, up_rest = lax.cond(whole, send_rest, no_rest, kv)

    state = (jax.ShapeDtypeStruct((rows, DIM), f32), jax.ShapeDtypeStruct((rows, 2 * DIM), f32))

    def own_kernel(facts, qkv, low_rest, up_rest, peak, total):
        del low_rest, up_rest
        own_column(facts, qkv, peak, total)

    peak, total = call(own_kernel, state, [facts, qkv], [low_rest, up_rest])
    joined = [pltpu.VMEM((rows, 2 * DIM), bf16), pltpu.SemaphoreType.DMA((3,))]
    peak, total = call(
        first_side, state, [facts, qkv, upper, peak, total], [low_half, low_rest], joined
    )
    result = call(
        second_side,
        jax.ShapeDtypeStruct((rows, DIM), bf16),
        [facts, qkv, lower, up_half, peak, total],
        [up_rest],
        joined,
    )
    back = exchange(result.reshape(MEMBERS, tokens, DIM))
    return pl.pallas_call(
        unpack,
        out_shape=jax.ShapeDtypeStruct((tokens, width), bf16),
        in_specs=[SMEM, VMEM],
        out_specs=HBM,
        scratch_shapes=[
            pltpu.VMEM((tokens, width), bf16),
            pltpu.SemaphoreType.DMA((HEADS // RUN,)),
        ],
        compiler_params=PARAMS,
    )(facts, back)


def solution(mesh):
    uly, blk, cfg = (mesh.shape[name] for name in ("uly", "blk", "cfg"))
    fine = Mesh(mesh.devices.reshape(uly, blk // 4, 2, 2, cfg), ("uly", "col", "f", "g", "cfg"))
    tokens = P(("cfg", "col", "f", "g", "uly"), None)
    return jax.shard_map(
        shards,
        mesh=fine,
        in_specs=(tokens, tokens, tokens, P()),
        out_specs=tokens,
        check_vma=False,
    )
```
